32 devices in a mesh: section: 2 (over core), seq: 8 (over z, x), fsdp: 2 (over y).
Axes of the slice: x: 2, y: 2, z: 4, core: 2. Of those that a mesh axis runs over, the one named last changes fastest.
Arguments:
- tokens: bfloat16 [2, 2, 4096, 768], P(None, 'fsdp', 'seq'), may hold values from -6 to 6
- cotangent: bfloat16 [2, 2, 4096, 768], P(None, 'fsdp', 'seq'), may hold values from -6 to 6
- lengths: int32 [2, 2, 4], P(None, 'fsdp'), may hold values from 1 to 3840, 4096 in all within a row
- doc_order: int32 [2, 2, 4], P(None, 'fsdp'), may hold values from 0 to 3, each once within a row
- norm_gain: float32 [2, 768], P('section'), may hold values from 0.1 to 1.9
- w_in: bfloat16 [2, 768, 3352], P('section', 'fsdp'), may hold values from -0.21875 to 0.21875
- conv_w: float32 [2, 4, 1792], P('section'), may hold values from -3 to 3
- conv_b: float32 [2, 1792], P('section'), may hold values from -3 to 3
- dt_bias: float32 [2, 24], P('section'), may hold values from -4 to 0
- a_log: float32 [2, 24], P('section'), may hold values from -8 to 1
- skip_scale: float32 [2, 24], P('section'), may hold values from 0 to 2
- gate_gain: float32 [2, 1536], P('section'), may hold values from 0.1 to 1.9
- w_out: bfloat16 [2, 1536, 768], P('section', 'fsdp'), may hold values from -0.15625 to 0.15625
Outputs:
- activations: bfloat16 [2, 2, 2, 4096, 768], P('section', None, 'fsdp', 'seq')
- input_grads: bfloat16 [2, 2, 2, 4096, 768], P('section', None, 'fsdp', 'seq')
- grad_norm_gain: float32 [2, 768], P('section')
- grad_w_in: float32 [2, 768, 3352], P('section', 'fsdp')
- grad_conv_w: float32 [2, 4, 1792], P('section')
- grad_conv_b: float32 [2, 1792], P('section')
- grad_dt_bias: float32 [2, 24], P('section')
- grad_a_log: float32 [2, 24], P('section')
- grad_skip_scale: float32 [2, 24], P('section')
- grad_gate_gain: float32 [2, 1536], P('section')
- grad_w_out: float32 [2, 1536, 768], P('section', 'fsdp')
The draws below stay inside these ranges and needn't reach their ends.
Inputs may be any that keep to these rules, and one draw needn't show every extreme that they name: Each row of 4 lengths sums to 4096; its largest is exactly 3840. `doc_order`: each row holds 0 to 3 once each.
All inputs are finite; a program needn't handle non-finite values.
Results may differ from the reference program's by a relative error of at most 0.022.
The reference program's roundings to bfloat16 on the way count: a program that leaves them out, or rounds other values in their place, can miss the bound.
Values may be sent and summed in bfloat16 or wider, within the bound.
No kernel may reach another device: no remote copies, remote signals or barrier semaphores. Data moves between devices by JAX's collectives and lax.ppermute only.
A program may use at most 320 MiB of HBM per device.

```python
import math
import jax
import jax.numpy as jnp
import numpy as np
from jax import lax

D = 768
DI = 1536
H = 24
P_SIZE = 64
STATE = 128
CONV = 4
GROUP = 256
DOCS = 4
MB = 2
TOK_DEV = 512
NPROJ = 3352
CONVCH = 1792
LAYERS = 2
STREAMS = 2
SEQ_TOK = 4096


def block_scale(stream_key, dims, shards, low, top_value):
    level = 1.0
    for axis_at, parts in shards:
        heights = jax.random.uniform(jax.random.fold_in(jax.random.fold_in(stream_key, 6), axis_at), (parts,), jnp.float32, low / len(shards), top_value / len(shards))
        level = level * jnp.repeat(jnp.exp(heights), dims[axis_at] // parts).reshape((-1,) + (1,) * (len(dims) - 1 - axis_at))
    return level


def length_profile(number_of, total, most, slope):
    loads = [(1 << 20) // math.isqrt(standing ** slope) + 1 for standing in range(2, number_of + 1)]
    rest, counts = total - most - (number_of - 1), [1] * (number_of - 1)
    while rest > 0:
        free = [i for i in range(number_of - 1) if counts[i] < most]
        mass, budget = sum([loads[i] for i in free]), rest
        for i in free:
            extra = min(most - counts[i], max(1, budget * loads[i] // mass), rest)
            counts[i] = counts[i] + extra
            rest = rest - extra
    return np.array([most] + counts)


def uneven_parts(own_key, number_of, total, limit, slope):
    if number_of == 2:
        one = jax.random.randint(own_key, (), max(1, total - limit), min(limit, total - 1) + 1)
        return jnp.stack([one, total - one])
    sizes = jnp.asarray(length_profile(number_of, total, limit, slope), jnp.int32)
    couples = (number_of - 1) // 2
    giver, sink = sizes[1:1 + 2 * couples:2], sizes[2:2 + 2 * couples:2]
    margin = jnp.minimum(giver - 1, limit - sink)
    passed = jax.random.randint(jax.random.fold_in(own_key, 1), (couples,), 0, 1 << 20) % (margin + 1)
    sizes = sizes.at[1:1 + 2 * couples:2].set(giver - passed).at[2:2 + 2 * couples:2].set(sink + passed)
    return sizes[jax.random.permutation(jax.random.fold_in(own_key, 2), number_of)]


def scatter_about(own_key, shape, scale, limit, cuts=(), held_as=jnp.bfloat16):
    array = jax.random.normal(own_key, shape, jnp.float32) * scale
    if len(cuts) > 0:
        array = block_scale(own_key, shape, cuts, -0.22, 0.18) * array
    return jnp.clip(array, min=-limit, max=limit).astype(held_as)


def setup_inputs(seed: int = 0) -> dict:
    splits = jax.random.split(jax.random.key(seed), 14)
    return {
        "tokens": scatter_about(splits[0], (MB, STREAMS, SEQ_TOK, D), 1.0, 6.0, ((1, 2), (2, 8))),
        "cotangent": scatter_about(splits[1], (MB, STREAMS, SEQ_TOK, D), 1.0, 6.0, ((1, 2), (2, 8))),
        "lengths": jax.vmap(lambda own: uneven_parts(own, DOCS, SEQ_TOK, SEQ_TOK - TOK_DEV // 2, 2))(jax.random.split(splits[2], MB * STREAMS)).reshape((MB, STREAMS, DOCS)).astype(jnp.int32),
        "doc_order": jax.vmap(lambda own: jax.random.permutation(own, DOCS))(jax.random.split(splits[3], MB * STREAMS)).reshape((MB, STREAMS, DOCS)).astype(jnp.int32),
        "norm_gain": jnp.clip(1.0 + 0.18 * jax.random.normal(splits[4], (LAYERS, D), jnp.float32), 0.1, 1.9),
        "w_in": scatter_about(splits[5], (LAYERS, D, NPROJ), D ** -0.5, 0.21875, ((0, 2), (1, 2))),
        "conv_w": scatter_about(splits[6], (LAYERS, CONV, CONVCH), 0.5, 3.0, ((0, 2),), jnp.float32),
        "conv_b": scatter_about(splits[7], (LAYERS, CONVCH), 0.5, 3.0, ((0, 2),), jnp.float32),
        "dt_bias": jnp.clip(-4.0 + 4.0 * jax.random.uniform(splits[8], (LAYERS, H), jnp.float32) ** block_scale(splits[8], (LAYERS, H), ((0, 2),), -0.2, 0.2), -4.0, 0.0),
        "a_log": jnp.clip(-8.0 + 9.0 * jax.random.uniform(splits[9], (LAYERS, H), jnp.float32) ** block_scale(splits[9], (LAYERS, H), ((0, 2),), -0.2, 0.2), -8.0, 1.0),
        "skip_scale": jnp.clip(2.0 * jax.random.uniform(splits[10], (LAYERS, H), jnp.float32) ** block_scale(splits[10], (LAYERS, H), ((0, 2),), -0.2, 0.2), 0.0, 2.0),
        "gate_gain": jnp.clip(1.0 + 0.18 * jax.random.normal(splits[11], (LAYERS, DI), jnp.float32), 0.1, 1.9),
        "w_out": scatter_about(splits[12], (LAYERS, DI, D), DI ** -0.5, 0.15625, ((0, 2), (1, 2))),
    }


epsilon = 1e-05
highest = lax.Precision.HIGHEST

@jax.custom_vjp
def low(v):
    return lax.optimization_barrier(v.astype(jnp.bfloat16)).astype(jnp.float32)

@jax.custom_vjp
def low_back(v):
    return v

def low_keep(v):
    return (low(v), None)

def low_pass(kept, grad):
    return (grad,)

def back_keep(v):
    return (v, None)

def back_low(kept, grad):
    return (low(grad),)
low.defvjp(low_keep, low_pass)
low_back.defvjp(back_keep, back_low)

def segment_ids(doc_lengths, doc_order, positions):
    labels = jnp.arange(doc_lengths.shape[0], dtype=jnp.int32)
    picked = (doc_order.astype(jnp.int32)[:, None] == labels[None, :]).astype(jnp.int32)
    ordered = lax.optimization_barrier(jnp.sum(picked * doc_lengths.astype(jnp.int32)[None, :], axis=1)).astype(jnp.int32)
    bounds = jnp.cumsum(ordered).astype(jnp.int32)
    return lax.optimization_barrier(jnp.sum((positions.astype(jnp.int32)[:, None] >= bounds[None, :]).astype(jnp.int32), axis=1)).astype(jnp.int32)

def rms_scale(values, gain_vector):
    return values * lax.rsqrt(lax.optimization_barrier(jnp.mean(values * values, axis=-1, keepdims=True)) + epsilon) * gain_vector

def convolve(padded, padded_labels, conv_weight, conv_bias):
    row_count = padded.shape[0] - CONV + 1
    summed = jnp.zeros((row_count, padded.shape[1]), jnp.float32) + conv_bias[None, :]
    for offset in range(CONV):
        same_doc = (padded_labels[offset:offset + row_count].astype(jnp.int32) == padded_labels[CONV - 1:].astype(jnp.int32)).astype(jnp.float32)
        summed = summed + conv_weight[offset][None, :] * padded[offset:offset + row_count] * same_doc[:, None]
    return jax.nn.silu(summed)

def group_terms(values, b_rows, c_rows, step_sizes, decay_rates, labels, before):
    labels = labels.astype(jnp.int32)
    cumulated = jnp.cumsum(step_sizes * decay_rates[None, :], axis=0).T
    previous = jnp.concatenate([jnp.reshape(before, (1,)).astype(jnp.int32), labels[:-1]])
    starts = (labels != previous).astype(jnp.int32)
    opened = (jnp.cumsum(starts).astype(jnp.int32) == 0).astype(jnp.float32)
    places = jnp.arange(labels.shape[0], dtype=jnp.int32)
    inside = ((places[:, None] >= places[None, :]) & (labels[:, None] == labels[None, :])).astype(jnp.float32)
    log_gaps = jnp.where(inside[None] > 0.0, cumulated[:, :, None] - cumulated[:, None, :], jnp.zeros((), jnp.float32))
    kernel = jnp.exp(log_gaps) * inside[None]
    scores = jnp.dot(c_rows, b_rows.T, precision=highest)
    mixing = kernel * scores[None] * step_sizes.T[:, None, :]
    intra_out = jnp.einsum('hts,shp->thp', mixing, values, precision=highest)
    same_end = (labels == labels[-1]).astype(jnp.float32)
    weights = jnp.exp(cumulated[:, -1:] - cumulated) * step_sizes.T * same_end[None, :]
    scaled = values * weights.T[:, :, None]
    group_state = jnp.einsum('shp,sn->hpn', scaled, b_rows, precision=highest)
    group_decay = jnp.exp(cumulated[:, -1]) * opened[-1]
    reach_rows = jnp.exp(cumulated).T * opened[:, None]
    return (intra_out, group_state, group_decay, reach_rows)

def state_space(values, b_rows, c_rows, step_sizes, decay_rates, labels):
    blocks = values.shape[0] // GROUP
    label_blocks = labels.astype(jnp.int32).reshape(blocks, GROUP)
    befores = jnp.concatenate([jnp.full((1,), -1, jnp.int32), label_blocks[:-1, -1]]).astype(jnp.int32)

    @jax.checkpoint
    def advance(carry_state, pieces):
        part_v, part_b, part_c, part_s, part_l, part_p = pieces
        intra_out, group_state, group_decay, reach_rows = group_terms(part_v, part_b, part_c, part_s, decay_rates, part_l, part_p)
        outside = jnp.einsum('tn,th,hpn->thp', part_c, reach_rows, carry_state, precision=highest)
        return (group_decay[:, None, None] * carry_state + group_state, intra_out + outside)
    pieces = (values.reshape(blocks, GROUP, H, P_SIZE), b_rows.reshape(blocks, GROUP, STATE), c_rows.reshape(blocks, GROUP, STATE), step_sizes.reshape(blocks, GROUP, H), label_blocks, befores)
    _, result = lax.scan(advance, jnp.zeros((H, P_SIZE, STATE), jnp.float32), pieces)
    return result.reshape(-1, H, P_SIZE)

def layer_pass(hidden, labels, params):
    norm_gain, w_in, conv_w, conv_b, dt_bias, a_log, skip_scale, gate_gain, w_out = params
    labels = labels.astype(jnp.int32)
    hidden = low_back(hidden)
    projected = low_back(jnp.dot(low(rms_scale(hidden, norm_gain)), w_in, precision=highest))
    gate_part = projected[:, :DI]
    conv_input = low(projected[:, DI:DI + CONVCH])
    step_sizes = jax.nn.softplus(projected[:, DI + CONVCH:] + dt_bias[None, :])
    padded = jnp.concatenate([jnp.zeros((CONV - 1, CONVCH), jnp.float32), conv_input])
    padded_labels = jnp.concatenate([jnp.full((CONV - 1,), -1, jnp.int32), labels])
    mixed_rows = convolve(padded, padded_labels, conv_w, conv_b)
    values = mixed_rows[:, :DI].reshape(-1, H, P_SIZE)
    b_rows = mixed_rows[:, DI:DI + STATE]
    c_rows = mixed_rows[:, DI + STATE:]
    decay_rates = -jnp.exp(a_log)
    scanned = state_space(values, b_rows, c_rows, step_sizes, decay_rates, labels) + skip_scale[None, :, None] * values
    gated_rows = scanned.reshape(-1, DI) * jax.nn.silu(gate_part)
    branch = low_back(jnp.dot(low(rms_scale(gated_rows, gate_gain)), w_out, precision=highest))
    return low(hidden + branch)

def reference(tokens, cotangent, lengths, doc_order, norm_gain, w_in, conv_w, conv_b, dt_bias, a_log, skip_scale, gate_gain, w_out):
    places = jnp.arange(SEQ_TOK, dtype=jnp.int32)

    def stream_labels(doc_lengths, stream_order):
        return segment_ids(doc_lengths, stream_order, places)
    labels = jax.vmap(stream_labels)(lengths.astype(jnp.int32).reshape(-1, DOCS), doc_order.astype(jnp.int32).reshape(-1, DOCS)).astype(jnp.int32)

    def forward(start_rows, probes, *weights):
        outputs = []
        hidden = start_rows
        for layer_index in range(LAYERS):
            params = tuple((weight[layer_index] for weight in weights))

            def one_stream(stream_pair):
                return layer_pass(stream_pair[0], stream_pair[1], params)
            flat = (hidden + probes[layer_index]).reshape(-1, SEQ_TOK, D)
            hidden = lax.map(jax.checkpoint(one_stream), (flat, labels)).reshape(start_rows.shape)
            outputs.append(hidden)
        return (hidden, jnp.stack(outputs))
    start_rows = tokens.astype(jnp.float32)
    probes = jnp.zeros((LAYERS,) + start_rows.shape, jnp.float32)
    floats = [norm_gain.astype(jnp.float32), w_in.astype(jnp.float32), conv_w.astype(jnp.float32), conv_b.astype(jnp.float32), dt_bias.astype(jnp.float32), a_log.astype(jnp.float32), skip_scale.astype(jnp.float32), gate_gain.astype(jnp.float32), w_out.astype(jnp.float32)]
    final_rows, pullback, layer_outputs = jax.vjp(forward, start_rows, probes, *floats, has_aux=True)
    gradients = pullback(cotangent.astype(jnp.float32))
    return (layer_outputs.astype(jnp.bfloat16), gradients[1].astype(jnp.bfloat16), gradients[2], gradients[3], gradients[4], gradients[5], gradients[6], gradients[7], gradients[8], gradients[9], gradients[10])
```

```python
import jax
import jax.numpy as jnp
from jax import lax
from jax.experimental import pallas as pl
from jax.experimental.pallas import tpu as pltpu
from jax.sharding import PartitionSpec as P

D = 768
DI = 1536
H = 24
P_SIZE = 64
STATE = 128
CONV = 4
CONVCH = 1792
Q = 128
HALF = DI // 2
PACK = STATE + 16
PACK_WIDE = STATE + 8
TAP_BIAS, NORM, GAIN, STEP_BIAS, BASE_RATE, SKIP = 4, 5, 6, 7, 8, 9
TABLE = (16, CONVCH)
SWAP = ((0, 1), (1, 0))

f32 = jnp.float32
bf16 = jnp.bfloat16
epsilon = 1e-05
masked = -1e30


def nn(a, b):
    return lax.dot_general(a, b, (((1,), (0,)), ((), ())), preferred_element_type=f32)


def nt(a, b):
    return lax.dot_general(a, b, (((1,), (1,)), ((), ())), preferred_element_type=f32)


def tn(a, b):
    return nn(a.astype(f32).T.astype(bf16), b)


def split(v):
    high = v.astype(bf16)
    return high, (v - high.astype(f32)).astype(bf16)


def expand(v, spread):
    high, low = split(v)
    return nn(high, spread) + nn(low, spread)


def expand_row(v, spread):
    return expand(jnp.broadcast_to(v, (8, v.shape[1])), spread)[0:1]


def head_sum(v, spread):
    high, low = split(v)
    return nt(high, spread) + nt(low, spread)


def tri_sum(tri, v):
    high, rest = split(v)
    middle, low = split(v - high.astype(f32))
    return nn(tri, high) + nn(tri, middle) + nn(tri, low)


def iota(shape, dim):
    return lax.broadcasted_iota(jnp.int32, shape, dim)


def spread_matrix():
    return (iota((128, DI), 1) // P_SIZE == iota((128, DI), 0)).astype(bf16)


def two_heads(tile):
    left = iota(tile.shape, 1) < P_SIZE
    zero = jnp.zeros_like(tile)
    return jnp.concatenate([jnp.where(left, tile, zero), jnp.where(left, zero, tile)], axis=0)


def product(a, a_low, b, b_low):
    both = jnp.concatenate([b, b_low], axis=0)
    return nn(jnp.concatenate([a, a], axis=1), both) + nn(a_low, b)


def decay_rows(decay):
    high, low = split(decay)
    row = iota((16, decay.shape[1]), 0)
    both = jnp.where(row == 0, high.astype(f32), jnp.where(row == 1, low.astype(f32), 0.0))
    return both.astype(bf16)


def label_kernel(doc_ref, table_ref, col_ref, lab_ref):
    rows = col_ref.shape[0]
    base = doc_ref[8]
    ends = []
    end = 0
    for k in range(4):
        end = end + doc_ref[doc_ref[4 + k]]
        ends.append(end)

    def label(position):
        found = jnp.zeros(position.shape, jnp.int32)
        for bound in ends:
            found = found + (position >= bound).astype(jnp.int32)
        return jnp.where(position < 0, -1, found)

    def columns(row, lane):
        here = label(base + row)
        block = (row // Q) * Q
        other = jnp.where(
            lane < 3,
            row - 1 - lane,
            jnp.where(lane == 3, block - 1, jnp.where(lane == 4, block + Q - 1, jnp.where(lane == 5, -1, rows - 1))),
        )
        same = (label(base + other) == here).astype(f32)
        return jnp.where(lane == 7, here.astype(f32), same)

    lane = iota((rows + 16, 128), 1)
    row = iota((rows + 16, 128), 0) - 8
    whole_table = columns(jnp.clip(row, 0, rows - 1), lane)
    table_ref[...] = jnp.where((row >= 0) & (row < rows), whole_table, 0.0)
    col_ref[...] = columns(iota((rows, 128), 0), iota((rows, 128), 1))
    lab_ref[...] = label(base + iota((8, rows), 1)).astype(f32)


def head_row(par_ref, k):
    return jnp.where(iota((1, 128), 1) < H, par_ref[k : k + 1, 0:128], 0.0)


def rates(par_ref):
    return jnp.where(iota((1, 128), 1) < H, -jnp.exp(par_ref[BASE_RATE : BASE_RATE + 1, 0:128]), 0.0)


def skip_row(par_ref, spread):
    return expand_row(head_row(par_ref, SKIP), spread)


def conv_kernel(
    rc_ref, halo_ref, e_ref, col_ref, par_ref, sp_ref,
    q_ref, ds_ref, dt_ref, cum_ref, all_ref, lin_ref, pack_ref,
):
    spread = sp_ref[...]
    tri = (iota((Q, Q), 0) >= iota((Q, Q), 1)).astype(bf16)
    rate = rates(par_ref)
    bias = head_row(par_ref, STEP_BIAS)
    state = jnp.zeros((STATE, DI), f32)
    offset = jnp.zeros((1, 128), f32)
    decay = jnp.ones((1, 128), f32)
    for c in range(rc_ref.shape[0] // Q):
        rows = slice(c * Q, (c + 1) * Q)
        col = col_ref[rows, :]
        dt = jax.nn.softplus(e_ref[rows, :] + bias)
        cum = tri_sum(tri, dt * rate)
        dt_ref[rows, :] = dt
        cum_ref[rows, :] = cum
        all_ref[rows, :] = cum + offset
        for j in range(CONVCH // 128):
            lanes = slice(j * 128, (j + 1) * 128)
            if c == 0:
                window = jnp.concatenate([halo_ref[:, lanes], rc_ref[0:Q, lanes]], axis=0)
            else:
                window = rc_ref[c * Q - 16 : (c + 1) * Q, lanes]
            window = window.astype(f32)
            pre = par_ref[TAP_BIAS : TAP_BIAS + 1, lanes] + par_ref[3:4, lanes] * window[16:]
            for d in range(1, CONV):
                pre = pre + par_ref[3 - d : 4 - d, lanes] * window[16 - d : 16 + Q - d] * col[:, d - 1 : d]
            gate = jax.nn.sigmoid(pre)
            out = pre * gate
            q_ref[rows, lanes] = out
            ds_ref[rows, lanes] = (gate + out * (1.0 - gate)).astype(bf16)
        end = cum[Q - 1 : Q, :]
        weight = dt * jnp.exp(end - cum) * col[:, 4:5]
        scaled, scaled_low = split(q_ref[rows, 0:DI] * expand(weight, spread))
        b_rows, b_low = split(q_ref[rows, DI : DI + STATE].T)
        lin_ref[c, 0:STATE], lin_ref[c, STATE:] = split(state)
        step = jnp.exp(end) * col[Q - 1 : Q, 3:4]
        state = state * expand_row(step, spread) + product(b_rows, b_low, scaled, scaled_low)
        decay = decay * step
        offset = offset + end
    wide = expand_row(decay, spread)
    for half in range(2):
        lanes = slice(half * HALF, (half + 1) * HALF)
        pack_ref[half, 0:STATE, :] = state[:, lanes]
        pack_ref[half, STATE:, :] = jnp.broadcast_to(wide[:, lanes], (8, HALF))


def intra_kernel(q_ref, dt_ref, cum_ref, col_ref, lab_ref, lin_ref, par_ref, sp_ref, y_ref):
    spread = sp_ref[...]
    col = col_ref[...]
    cum = cum_ref[...]
    cum_t = cum.T
    x = q_ref[:, 0:DI]
    b_rows, b_low = split(q_ref[:, DI : DI + STATE])
    c_rows, c_low = split(q_ref[:, DI + STATE :])
    x_dt, x_low = split(x * expand(dt_ref[...], spread))
    scores = nt(c_rows, b_rows) + (nt(c_rows, b_low) + nt(c_low, b_rows))
    same = (col[:, 7:8] == lab_ref[0:1, :]) & (iota((Q, Q), 0) >= iota((Q, Q), 1))
    shut = jnp.where(same, 0.0, masked)
    reach = expand(jnp.exp(cum) * col[:, 3:4], spread)
    base = product(c_rows, c_low, lin_ref[0, 0:STATE], lin_ref[0, STATE:]) * reach + skip_row(par_ref, spread) * x
    for j in range(H // 2):
        lanes = slice(j * 128, (j + 1) * 128)
        mixing, mixing_low = split(
            jnp.concatenate(
                [
                    jnp.exp(cum[:, h : h + 1] - cum_t[h : h + 1, :] + shut) * scores
                    for h in (2 * j, 2 * j + 1)
                ],
                axis=1,
            )
        )
        pair = two_heads(x_dt[:, lanes])
        y_ref[:, lanes] = (
            base[:, lanes]
            + nn(mixing, pair)
            + (nn(mixing_low, pair) + nn(mixing, two_heads(x_low[:, lanes])))
        )


def gate_kernel(
    y0_ref, z_ref, c_ref, all_ref, col_ref, inc_ref, par_ref, w_ref, x_ref, sp_ref,
    y_ref, v_ref, out_ref,
):
    reach = jnp.exp(all_ref[...]) * col_ref[:, 5:6]
    y = y0_ref[...] + expand(reach, sp_ref[...]) * product(
        *split(c_ref[...]), *split(inc_ref[...])
    )
    y_ref[...] = y
    z = z_ref[...]
    gated = y * (z * jax.nn.sigmoid(z))
    scale = lax.rsqrt(jnp.mean(gated * gated, axis=1, keepdims=True) + epsilon)
    v = (gated * scale * par_ref[GAIN : GAIN + 1, 0:DI]).astype(bf16)
    v_ref[...] = v
    out_ref[...] = (x_ref[...].astype(f32) + nn(v, w_ref[...])).astype(bf16)


def gate_back_kernel(
    g_ref, w_ref, y_ref, z_ref, par_ref, c_ref, all_ref, col_ref, decay_ref, sp_ref,
    dy_ref, dz_ref, dgain_ref, pack_ref, total_ref,
):
    step = pl.program_id(0)
    dv = nt(g_ref[...], w_ref[...])
    y = y_ref[...]
    z = z_ref[...]
    gate = jax.nn.sigmoid(z)
    silu = z * gate
    gated = y * silu
    scale = lax.rsqrt(jnp.mean(gated * gated, axis=1, keepdims=True) + epsilon)
    normed = gated * scale
    dn = dv * par_ref[GAIN : GAIN + 1, 0:DI]
    dgated = scale * (dn - normed * jnp.mean(dn * normed, axis=1, keepdims=True))
    dz_ref[...] = (dgated * y * (gate + silu * (1.0 - gate))).astype(bf16)
    dy = (dgated * silu).astype(bf16)
    dy_ref[...] = dy
    reach = jnp.exp(all_ref[...]) * col_ref[:, 5:6]
    reached = (dy.astype(f32) * expand(reach, sp_ref[...])).astype(bf16)
    part = tn(c_ref[...], reached)
    gain_part = jnp.sum(dv * normed, axis=0, keepdims=True)

    @pl.when(step == 0)
    def _():
        total_ref[...] = part
        dgain_ref[...] = gain_part

    @pl.when(step > 0)
    def _():
        total_ref[...] += part
        dgain_ref[...] += gain_part

    @pl.when(step == pl.num_programs(0) - 1)
    def _():
        for half in range(2):
            pack_ref[half, 0:STATE, :] = total_ref[:, half * HALF : (half + 1) * HALF].astype(bf16)
            pack_ref[half, STATE:, :] = decay_rows(decay_ref[half, STATE : STATE + 1, :])


def intra_back_kernel(
    q_ref, dt_ref, cum_ref, all_ref, col_ref, lab_ref, lin_ref, inc_ref, dy_ref, y_ref, par_ref, sp_ref,
    dx_ref, dbc_ref, hs_ref, carry_ref,
):
    @pl.when(pl.program_id(0) == 0)
    def _():
        carry_ref[...] = jnp.zeros_like(carry_ref)

    spread = sp_ref[...]
    col = col_ref[...]
    cum = cum_ref[...]
    cum_t = cum.T
    x = q_ref[:, 0:DI]
    b_rows, b_low = split(q_ref[:, DI : DI + STATE])
    c_rows, c_low = split(q_ref[:, DI + STATE :])
    dy = dy_ref[...]
    dy32 = dy.astype(f32)
    x_wide = x * expand(dt_ref[...], spread)
    x_dt = x_wide.astype(bf16)
    end = cum[Q - 1 : Q, :]
    leave = expand(jnp.exp(end - cum) * col[:, 4:5], spread)
    carry = carry_ref[...]
    carry_high, carry_low = split(carry)
    base = product(b_rows, b_low, carry_high, carry_low) * leave
    scores = nt(b_rows, c_rows) + (nt(b_low, c_rows) + nt(b_rows, c_low))
    same = (col[:, 7:8] == lab_ref[0:1, :]) & (iota((Q, Q), 1) >= iota((Q, Q), 0))
    shut = jnp.where(same, 0.0, masked)
    dscores = jnp.zeros((Q, Q), f32)
    for j in range(H // 2):
        lanes = slice(j * 128, (j + 1) * 128)
        dy_pair = dy[:, lanes]
        grads = nt(two_heads(x_dt[:, lanes]), dy_pair)
        mixing = []
        for k in range(2):
            h = 2 * j + k
            kernel = jnp.exp(cum_t[h : h + 1, :] - cum[:, h : h + 1] + shut)
            mixing.append(kernel * scores)
            dscores = dscores + grads[k * Q : (k + 1) * Q] * kernel
        mixing, mixing_low = split(jnp.concatenate(mixing, axis=1))
        pair = two_heads(dy_pair)
        dx_ref[:, lanes] = base[:, lanes] + nn(mixing, pair) + nn(mixing_low, pair)
    dx = dx_ref[...]
    near, near_low = split(dy32 * expand(jnp.exp(cum) * col[:, 3:4], spread))
    far = (dy32 * expand(jnp.exp(all_ref[...]) * col[:, 5:6], spread)).astype(bf16)
    low = dscores.astype(bf16)
    inc_high, inc_low = split(inc_ref[...])
    left = (x_wide * leave).astype(bf16)
    dbc_ref[:, 0:STATE] = nn(low, c_rows) + nt(left, carry_high)
    dbc_ref[:, STATE:] = (
        nn(dscores.T.astype(bf16), b_rows)
        + nt(near, lin_ref[0, 0:STATE])
        + nt(near, lin_ref[0, STATE:])
        + nt(far, inc_high)
        + nt(far, inc_low)
    )
    hs_ref[:, 0:128] = head_sum(
        dy32 * (y_ref[...] - skip_row(par_ref, spread) * x) - x_wide * dx, spread
    )
    hs_ref[:, 128:] = head_sum(x * dx, spread)
    step = jnp.exp(end) * col[Q - 1 : Q, 3:4]
    c_rows, c_low = split(q_ref[:, DI + STATE :].T)
    carry_ref[...] = carry * expand_row(step, spread) + product(c_rows, c_low, near, near_low)


def conv_back_kernel(
    outg_ref, inc_ref, q_ref, ds_ref, dt_ref, all_ref, col_ref, e_ref, rc_ref, halo_ref,
    dy_ref, dx_ref, dbc_ref, hs_ref, par_ref, sp_ref,
    dre_ref, tail_ref, back_ref, dw_ref, dh_ref, pre_ref, sum_ref,
):
    count = q_ref.shape[0] // Q
    spread = sp_ref[...]
    outg = outg_ref[...]
    last = all_ref[count * Q - 1 : count * Q, :]
    skip = skip_row(par_ref, spread)
    rate = rates(par_ref)
    bias = head_row(par_ref, STEP_BIAS)
    total = jnp.zeros((1, 128), f32)
    skip_total = jnp.zeros((1, 128), f32)
    pre_ref[0:8, :] = jnp.zeros((8, CONVCH), f32)
    pre_ref[8 + count * Q :, :] = jnp.zeros((8, CONVCH), f32)
    for c in range(count):
        rows = slice(c * Q, (c + 1) * Q)
        moved = slice(8 + c * Q, 8 + (c + 1) * Q)
        col = col_ref[moved, :]
        x = q_ref[rows, 0:DI]
        dy = dy_ref[rows, :].astype(f32)
        wide_dt = expand(dt_ref[rows, :], spread)
        x_dt = (x * wide_dt).astype(bf16).astype(f32)
        leave = expand(jnp.exp(last - all_ref[rows, :]) * col[:, 6:7], spread)
        dx_far = leave * nn(q_ref[rows, DI : DI + STATE].astype(bf16), outg)
        dx = dx_ref[rows, :] + dx_far
        db = dbc_ref[rows, 0:STATE] + nt((x_dt * leave).astype(bf16), outg)
        far = head_sum(x_dt * dx_far, spread)
        total = total + jnp.sum(far, axis=0, keepdims=True)
        sum_ref[rows, 0:128] = hs_ref[rows, 0:128] - far
        sum_ref[rows, 128:] = hs_ref[rows, 128:] + head_sum(x * dx_far, spread)
        skip_total = skip_total + jnp.sum(head_sum(x * dy, spread), axis=0, keepdims=True)
        pre_ref[moved, 0:DI] = (wide_dt * dx + skip * dy) * ds_ref[rows, 0:DI].astype(f32)
        pre_ref[moved, DI : DI + STATE] = db * ds_ref[rows, DI : DI + STATE].astype(f32)
        pre_ref[moved, DI + STATE :] = dbc_ref[rows, STATE:] * ds_ref[rows, DI + STATE :].astype(f32)
    kept = jnp.exp(last) * col_ref[7 + count * Q : 8 + count * Q, 5:6]
    both = jnp.sum(outg.astype(f32) * inc_ref[...], axis=0, keepdims=True)
    through = kept * head_sum(jnp.broadcast_to(both, (8, DI)), spread)[0:1]
    tri = (iota((Q, Q), 0) <= iota((Q, Q), 1)).astype(bf16)
    later = total + through
    rate_total = jnp.zeros((1, 128), f32)
    bias_total = jnp.zeros((1, 128), f32)
    for c in reversed(range(count)):
        rows = slice(c * Q, (c + 1) * Q)
        sums = tri_sum(tri, sum_ref[rows, 0:128])
        dlog = sums + later
        later = later + sums[0:1]
        ddt = rate * dlog + sum_ref[rows, 128:]
        de = ddt * jax.nn.sigmoid(e_ref[rows, :] + bias)
        dre_ref[rows, CONVCH:] = jnp.where(iota((Q, 128), 1) < H, de, 0.0).astype(bf16)
        rate_total = rate_total + jnp.sum(dlog * dt_ref[rows, :], axis=0, keepdims=True)
        bias_total = bias_total + jnp.sum(de, axis=0, keepdims=True)
    row = iota((8, 128), 0)
    dh_ref[...] = jnp.where(
        row == 0,
        bias_total,
        jnp.where(row == 1, rate_total * rate, jnp.where(row == 2, skip_total, 0.0)),
    )
    for j in range(CONVCH // 128):
        lanes = slice(j * 128, (j + 1) * 128)
        taps = [par_ref[3 - d : 4 - d, lanes] for d in range(CONV)]
        sums = [jnp.zeros((1, 128), f32) for _ in range(CONV + 1)]
        front = pre_ref[0:16, lanes]
        early = jnp.zeros((8, 128), f32)
        for d in range(1, CONV):
            early = early + taps[d] * (front * col_ref[0:16, d - 1 : d])[d : d + 8]
        back_ref[:, lanes] = early
        for c in range(count):
            rows = slice(c * Q, (c + 1) * Q)
            ahead = pre_ref[8 + c * Q : 16 + (c + 1) * Q, lanes]
            col = col_ref[8 + c * Q : 16 + (c + 1) * Q, :]
            if c == 0:
                window = jnp.concatenate([halo_ref[:, lanes], rc_ref[0:Q, lanes]], axis=0)
            else:
                window = rc_ref[c * Q - 16 : (c + 1) * Q, lanes]
            window = window.astype(f32)
            here = ahead[0:Q]
            sums[CONV] = sums[CONV] + jnp.sum(here, axis=0, keepdims=True)
            sums[3] = sums[3] + jnp.sum(here * window[16:], axis=0, keepdims=True)
            grad = taps[0] * here
            for d in range(1, CONV):
                same = ahead * col[:, d - 1 : d]
                sums[3 - d] = sums[3 - d] + jnp.sum(
                    same[0:Q] * window[16 - d : 16 + Q - d], axis=0, keepdims=True
                )
                grad = grad + taps[d] * same[d : d + Q]
            dre_ref[rows, lanes] = grad.astype(bf16)
            if c == count - 1:
                tail_ref[:, lanes] = grad[Q - 8 :]
        row = iota((8, 128), 0)
        stacked = jnp.zeros((8, 128), f32)
        for k in range(CONV + 1):
            stacked = jnp.where(row == k, sums[k], stacked)
        dw_ref[:, lanes] = stacked


def params(steps):
    return pltpu.CompilerParams(
        dimension_semantics=("arbitrary",) * steps, vmem_limit_bytes=48 * 1024 * 1024
    )


def shape(*dims, dtype=f32):
    return jax.ShapeDtypeStruct(dims, dtype)


def whole(array):
    rank = len(array.shape)
    return pl.BlockSpec(array.shape, lambda *_: (0,) * rank)


def conv_forward(rc, halo, e, col, par, spread):
    rows = rc.shape[0]
    outs = (
        shape(rows, CONVCH),
        shape(rows, CONVCH, dtype=bf16),
        shape(rows, 128),
        shape(rows, 128),
        shape(rows, 128),
        shape(rows // Q, 2 * STATE, DI, dtype=bf16),
        shape(2, PACK_WIDE, HALF),
    )
    return pl.pallas_call(conv_kernel, out_shape=outs, compiler_params=params(0))(
        rc, halo, e, col, par, spread
    )


def intra_forward(q, dt, cum, col, lab, lin, par, spread):
    rows = q.shape[0]

    def by_row(width):
        return pl.BlockSpec((Q, width), lambda i: (i, 0))

    return pl.pallas_call(
        intra_kernel,
        grid=(rows // Q,),
        in_specs=[
            by_row(CONVCH),
            by_row(128),
            by_row(128),
            by_row(128),
            pl.BlockSpec((8, Q), lambda i: (0, i)),
            pl.BlockSpec((1, 2 * STATE, DI), lambda i: (i, 0, 0)),
            whole(par),
            whole(spread),
        ],
        out_specs=by_row(DI),
        out_shape=shape(rows, DI),
        compiler_params=params(1),
        cost_estimate=pl.CostEstimate(
            flops=8 * rows * Q * DI, bytes_accessed=rows * 20000, transcendentals=rows * Q * H
        ),
    )(q, dt, cum, col, lab, lin, par, spread)


def gate_forward(y0, z, q, total, col, inc, par, w_out, hidden, spread):
    rows = y0.shape[0]
    size = 256

    def by_row(width):
        return pl.BlockSpec((size, width), lambda i: (i, 0))

    return pl.pallas_call(
        gate_kernel,
        grid=(rows // size,),
        in_specs=[
            by_row(DI),
            by_row(DI),
            pl.BlockSpec((size, STATE), lambda i: (i, (DI + STATE) // STATE)),
            by_row(128),
            by_row(128),
            whole(inc),
            whole(par),
            whole(w_out),
            by_row(D),
            whole(spread),
        ],
        out_specs=(by_row(DI), by_row(DI), by_row(D)),
        out_shape=(shape(rows, DI), shape(rows, DI, dtype=bf16), shape(rows, D, dtype=bf16)),
        compiler_params=params(1),
    )(y0, z, q, total, col, inc, par, w_out, hidden, spread)


def gate_backward(grad, w_out, y, z, par, q, total, col, pack, spread):
    rows = y.shape[0]
    size = 256

    def by_row(width):
        return pl.BlockSpec((size, width), lambda i: (i, 0))

    outs = (
        shape(rows, DI, dtype=bf16),
        shape(rows, DI, dtype=bf16),
        shape(1, DI),
        shape(2, PACK, HALF, dtype=bf16),
    )
    return pl.pallas_call(
        gate_back_kernel,
        grid=(rows // size,),
        in_specs=[
            by_row(D),
            whole(w_out),
            by_row(DI),
            by_row(DI),
            whole(par),
            pl.BlockSpec((size, STATE), lambda i: (i, (DI + STATE) // STATE)),
            by_row(128),
            by_row(128),
            whole(pack),
            whole(spread),
        ],
        out_specs=(by_row(DI), by_row(DI), whole(outs[2]), whole(outs[3])),
        out_shape=outs,
        scratch_shapes=[pltpu.VMEM((STATE, DI), f32)],
        compiler_params=params(1),
    )(grad, w_out, y, z, par, q, total, col, pack, spread)


def intra_backward(q, dt, cum, total, col, lab, lin, inc, dy, y, par, spread):
    rows = q.shape[0]
    top = rows // Q - 1

    def by_row(width):
        return pl.BlockSpec((Q, width), lambda i: (top - i, 0))

    return pl.pallas_call(
        intra_back_kernel,
        grid=(rows // Q,),
        in_specs=[
            by_row(CONVCH),
            by_row(128),
            by_row(128),
            by_row(128),
            by_row(128),
            pl.BlockSpec((8, Q), lambda i: (0, top - i)),
            pl.BlockSpec((1, 2 * STATE, DI), lambda i: (top - i, 0, 0)),
            whole(inc),
            by_row(DI),
            by_row(DI),
            whole(par),
            whole(spread),
        ],
        out_specs=(by_row(DI), by_row(256), by_row(256)),
        out_shape=(shape(rows, DI), shape(rows, 256), shape(rows, 256)),
        scratch_shapes=[pltpu.VMEM((STATE, DI), f32)],
        compiler_params=params(1),
        cost_estimate=pl.CostEstimate(
            flops=30 * rows * Q * DI, bytes_accessed=rows * 30000, transcendentals=rows * Q * H
        ),
    )(q, dt, cum, total, col, lab, lin, inc, dy, y, par, spread)


def conv_backward(outg, inc, q, ds, dt, total, col, e, rc, halo, dy, dx, dbc, hs, par, spread):
    rows = q.shape[0]
    outs = (
        shape(rows, CONVCH + 128, dtype=bf16),
        shape(8, CONVCH),
        shape(8, CONVCH),
        shape(8, CONVCH),
        shape(8, 128),
    )
    return pl.pallas_call(
        conv_back_kernel,
        out_shape=outs,
        scratch_shapes=[pltpu.VMEM((rows + 16, CONVCH), f32), pltpu.VMEM((rows, 256), f32)],
        compiler_params=params(0),
    )(outg, inc, q, ds, dt, total, col, e, rc, halo, dy, dx, dbc, hs, par, spread)


def pick(first, a, b):
    return jnp.where(first, a, b)


def unpack(block):
    wide = block.astype(f32)
    if block.dtype == f32:
        return wide[STATE : STATE + 1], wide[:STATE]
    return wide[STATE : STATE + 1] + wide[STATE + 1 : STATE + 2], wide[:STATE]


def pack_up(pair, kind):
    if kind == f32:
        decay = jnp.broadcast_to(pair[0], (8, HALF))
        return jnp.concatenate([pair[1], decay], axis=0)
    return jnp.concatenate([pair[1].astype(bf16), decay_rows(pair[0])], axis=0)


def combine(earlier, later):
    return (earlier[0] * later[0], later[0] * earlier[1] + later[1])


def after(arrays, event):
    return lax.optimization_barrier((tuple(arrays), event))[0]


def chain_scan(pack, reverse, beside):
    section = lax.axis_index("section")
    size = lax.axis_size("seq")
    kept = lax.dynamic_index_in_dim(pack, section, 0, keepdims=False)
    given = lax.dynamic_index_in_dim(pack, 1 - section, 0, keepdims=False)
    got = lax.ppermute(given, "section", SWAP)
    leads = (section == 1) if reverse else (section == 0)
    lead = unpack(pick(leads, kept, got))
    follow = unpack(pick(leads, got, kept))
    reached = combine(lead, follow)
    before = None
    distance = 2
    results = []
    while distance < size:
        route = [(i, i + distance) for i in range(size - distance)]
        if reverse:
            route = [(b, a) for a, b in route]
        sent = pack_up(reached, pack.dtype)
        arrived = lax.ppermute(sent, "seq", route)
        if beside:
            needed, other = beside.pop(0)(sent)
            arrived, needed = tie(arrived, needed)
            results.append((needed, other))
        arrived = unpack(arrived)
        before = arrived if before is None else combine(arrived, before)
        reached = combine(arrived, reached)
        distance *= 2
    first = before[1]
    second = lead[1] + lead[0] * first
    own = pick(leads, first, second).astype(pack.dtype)
    other = lax.ppermute(pick(leads, second, first).astype(pack.dtype), "section", SWAP)
    low = section == 0
    incoming = jnp.concatenate([pick(low, own, other), pick(low, other, own)], axis=1)
    return incoming, results


def spread_layer(shard, layer):
    section, row = lax.axis_index("section"), lax.axis_index("fsdp")
    parts = lax.axis_size("fsdp")
    here = section == layer
    across = [(layer, 1 - layer)]
    own = pick(here, shard, lax.ppermute(shard, "section", across))
    blocks = []
    for shift in range(1, parts):
        route = [(layer * parts + i, layer * parts + (i + shift) % parts) for i in range(parts)]
        moved = lax.ppermute(shard, ("section", "fsdp"), route)
        blocks.append(pick(here, moved, lax.ppermute(moved, "section", across)))
    blocks = [own] + blocks
    if parts == 2:
        low = row == 0
        return jnp.concatenate([pick(low, blocks[0], blocks[1]), pick(low, blocks[1], blocks[0])], axis=0)
    ordered = []
    for k in range(parts):
        block = blocks[0]
        for shift in range(1, parts):
            block = pick((row - shift) % parts == k, blocks[shift], block)
        ordered.append(block)
    return jnp.concatenate(ordered, axis=0)


def fold(make):
    section, row = lax.axis_index("section"), lax.axis_index("fsdp")
    parts = lax.axis_size("fsdp")
    got = lax.ppermute(make(1 - section).astype(bf16), "section", SWAP)
    summed = (make(section) + got.astype(f32)).astype(bf16)
    if parts == 2:
        kept = lax.dynamic_index_in_dim(summed, row, 0, keepdims=False)
        given = lax.dynamic_index_in_dim(summed, 1 - row, 0, keepdims=False)
        got = lax.ppermute(given, "fsdp", SWAP)
        return (kept.astype(f32) + got.astype(f32)).astype(bf16)
    return lax.psum_scatter(summed, "fsdp", scatter_dimension=0, tiled=False)


def pair_sum(array):
    size, bit = lax.axis_size("seq"), lax.axis_index("seq") % 2
    halves = array.reshape(2, -1, array.shape[1])
    kept = lax.dynamic_index_in_dim(halves, bit, 0, keepdims=False)
    given = lax.dynamic_index_in_dim(halves, 1 - bit, 0, keepdims=False)
    got = lax.ppermute(given, "seq", [(i, i ^ 1) for i in range(size)])
    return (kept.astype(f32) + got.astype(f32)).astype(bf16)


def pair_collect(array):
    size, low = lax.axis_size("seq"), lax.axis_index("seq") % 2 == 0
    got = lax.ppermute(array, "seq", [(i, i ^ 1) for i in range(size)])
    return jnp.concatenate([pick(low, array, got), pick(low, got, array)], axis=0)


def strides():
    size = lax.axis_size("seq")
    return [[i for i in range(size) if i % 2 == b] for b in range(2)]


def scatter_sum(array):
    count = lax.axis_size("seq") // 2
    blocks = array.reshape(count, -1, array.shape[1])
    got = lax.all_to_all(blocks, "seq", 0, 0, axis_index_groups=strides())
    return jnp.sum(got.astype(f32), axis=0).astype(bf16)


def collect(part):
    count = lax.axis_size("seq") // 2
    everyone = jnp.broadcast_to(part[None], (count,) + part.shape)
    got = lax.all_to_all(everyone, "seq", 0, 0, axis_index_groups=strides())
    return got.reshape(-1, part.shape[1])


def sum_everywhere(array):
    for axis in ("fsdp", "seq"):
        size = lax.axis_size(axis)
        distance = 1
        while distance < size:
            array = array + lax.ppermute(array, axis, [(i, i ^ distance) for i in range(size)])
            distance *= 2
    return array


def tie(*arrays):
    return lax.optimization_barrier(arrays)


def place_kernel(section_ref, early_ref, early_got_ref, late_ref, late_got_ref, e_ref, in_ref, out_ref):
    low = section_ref[0] == 0
    early, early_got = early_ref[...].astype(f32), early_got_ref[...].astype(f32)
    late, late_got = late_ref[...].astype(f32), late_got_ref[...].astype(f32)
    for half in range(2):
        own = low if half == 0 else jnp.logical_not(low)
        both = jnp.where(own, early, early_got)
        in_ref[:, half * HALF : (half + 1) * HALF] = both[:, :HALF]
        for k in range(2):
            at = HALF + k * (D // 2)
            out_ref[k, :, half * (D // 2) : (half + 1) * (D // 2)] = both[:, at : at + D // 2]
        at = DI + half * (CONVCH // 2)
        in_ref[:, at : at + CONVCH // 2] = jnp.where(own, late, late_got)
    in_ref[:, DI + CONVCH :] = e_ref[:, :H]


def place(early, early_got, late, late_got, e):
    rows = early.shape[0]
    size = rows // 4

    def by_row(width):
        return pl.BlockSpec((size, width), lambda i: (i, 0))

    section = lax.axis_index("section").astype(jnp.int32)[None]
    width = DI + CONVCH + H
    w_in, w_out = pl.pallas_call(
        place_kernel,
        grid=(4,),
        in_specs=[
            pl.BlockSpec(memory_space=pltpu.SMEM),
            by_row(DI),
            by_row(DI),
            by_row(CONVCH // 2),
            by_row(CONVCH // 2),
            by_row(128),
        ],
        out_specs=(by_row(width), pl.BlockSpec((2, size, D), lambda i: (0, i, 0))),
        out_shape=(shape(rows, width), shape(2, rows, D)),
        compiler_params=params(1),
    )(section, early, early_got, late, late_got, e)
    return w_in[None], w_out.reshape(1, 2 * rows, D)


def labels(lengths, order, base, rows):
    documents = jnp.concatenate([lengths, order, base[None]]).astype(jnp.int32)
    return pl.pallas_call(
        label_kernel,
        in_specs=[pl.BlockSpec(memory_space=pltpu.SMEM)],
        out_shape=(shape(rows + 16, 128), shape(rows, 128), shape(8, rows)),
        compiler_params=params(0),
    )(documents)


def parameter_table(norm_gain, conv_w, conv_b, dt_bias, a_log, skip_scale, gate_gain):
    def row(array):
        return jnp.pad(array, ((0, 0), (0, CONVCH - array.shape[1])))

    pieces = [conv_w, conv_b, row(norm_gain), row(gate_gain), row(dt_bias), row(a_log), row(skip_scale)]
    return jnp.pad(jnp.concatenate(pieces, axis=0), ((0, 6), (0, 0)))


def local(
    tokens, cotangent, lengths, doc_order, norm_gain, w_in, conv_w, conv_b, dt_bias, a_log,
    skip_scale, gate_gain, w_out,
):
    rows = tokens.shape[2]
    section, seq = lax.axis_index("section"), lax.axis_index("seq")
    size = lax.axis_size("seq")
    micro = seq % 2
    aligned = section == micro
    spot = (seq // 2) * 2 + section

    def flat(s, i):
        return s * size + i

    everywhere = ("section", "seq")
    exchange = [
        (flat(s, 2 * k + s), flat(s, 2 * k + 1 - s)) for k in range(size // 2) for s in range(2)
    ]

    def to_chain(array):
        given = lax.dynamic_index_in_dim(array[:, 0], 1 - section, 0, keepdims=False)
        own = lax.dynamic_index_in_dim(array[:, 0], section, 0, keepdims=False)
        return pick(aligned, own, lax.ppermute(given, everywhere, exchange))

    first_in, first_z, first_out = w_in[0, :, DI:], w_in[0, :, :DI], w_out[0]

    def projection(shard, layer):
        return jnp.pad(spread_layer(shard, layer), ((0, 0), (0, CONVCH + 128 - shard.shape[1])))

    w_conv = [projection(first_in, 0), None]
    hidden = to_chain(tokens)
    second_in, second_z, second_out, w_first = lax.optimization_barrier(
        (first_in, first_z, first_out, w_conv[0])
    )
    w_conv[0] = w_first
    w_gate = [spread_layer(second_z, 0), None]
    w_back = [spread_layer(second_out, 0), None]
    third_in, third_z, third_out, w_back[0] = lax.optimization_barrier(
        (second_in, second_z, second_out, w_back[0])
    )
    w_conv[1] = projection(third_in, 1)
    w_gate[1] = spread_layer(third_z, 1)
    w_back[1] = spread_layer(third_out, 1)
    top_grad = to_chain(cotangent)

    table = parameter_table(
        norm_gain, conv_w[0], conv_b, dt_bias, a_log, skip_scale, gate_gain
    )
    other = lax.ppermute(table, "section", SWAP)
    low = section == 0
    tables = [pick(low, table, other), pick(low, other, table)]
    spread = spread_matrix()

    stream_lengths = lax.dynamic_index_in_dim(lengths[:, 0], micro, 0, keepdims=False)
    stream_order = lax.dynamic_index_in_dim(doc_order[:, 0], micro, 0, keepdims=False)
    col_padded, col, lab = labels(stream_lengths, stream_order, spot * rows, rows)
    follow = [(flat(0, i), flat(1, i)) for i in range(size)] + [
        (flat(1, i), flat(0, i + 2)) for i in range(size - 2)
    ]
    precede = [(b, a) for a, b in follow]

    kept = []
    results = []
    for layer in range(2):
        par = tables[layer]
        wide = hidden.astype(f32)
        scale = lax.rsqrt(jnp.mean(wide * wide, axis=1, keepdims=True) + epsilon)
        u = (wide * scale * par[NORM : NORM + 1, :D]).astype(bf16)
        rc = nn(u, w_conv[layer][:, :CONVCH]).astype(bf16)
        e = nn(u, w_conv[layer][:, CONVCH:])
        halo = lax.ppermute(rc[rows - 16 :], everywhere, follow)
        q, ds, dt, cum, total, lin, pack = conv_forward(
            rc, halo, e, col, par, spread
        )
        inc, ((y0, _), (z, _)) = chain_scan(
            pack,
            False,
            [
                lambda sent: (
                    intra_forward(*after((q, dt, cum, col, lab, lin, par), sent), spread),
                    None,
                ),
                lambda sent: (nn(*after((u, w_gate[layer]), sent)), None),
            ],
        )
        y, v, out = gate_forward(
            y0, z, q, total, col, inc, par, w_back[layer], hidden, spread
        )
        kept.append((hidden, scale, u, rc, e, halo, q, ds, dt, cum, total, lin, pack, inc, z, y, v))
        results.append(out)
        hidden = out

    def columns(a, b):
        return lax.dot_general(a, b, (((0,), (0,)), ((), ())), preferred_element_type=f32)

    parts = lax.axis_size("fsdp")

    def half_of(array, half):
        width = array.shape[1] // 2
        return lax.dynamic_slice_in_dim(array, half * width, width, axis=1)

    def early_grads(u, dz, v, grad):
        def make(half):
            for_in = columns(u, half_of(dz, half)).reshape(parts, -1, HALF)
            for_out = columns(v, half_of(grad, half)).reshape(parts, 2, -1, D // 2)
            return jnp.concatenate([for_in, for_out[:, 0], for_out[:, 1]], axis=2)

        return make

    def late_grads(u, dr):
        return lambda half: columns(u, half_of(dr, half)).reshape(parts, -1, CONVCH // 2)

    grad = top_grad
    input_grads = [None, None]
    early = [None, None]
    late = [None, None]
    small = [None, None]
    for layer in (1, 0):
        par = tables[layer]
        hidden, scale, u, rc, e, halo, q, ds, dt, cum, total, lin, pack, inc, z, y, v = kept[layer]
        dy, dz, dgain, back = gate_backward(
            grad, w_back[layer], y, z, par, q, total, col, pack, spread
        )
        if layer == 0:
            early[1], back = tie(early[1], back)
            early[1] = pair_sum(early[1])

        def beside_first(sent):
            needed = intra_backward(
                *after((q, dt, cum, total, col, lab, lin, inc, dy, y, par), sent), spread
            )
            return needed, None

        def beside_second(sent):
            a, b, c, d = after((v, u, grad, dz), sent)
            ahead = None
            if layer == 0:
                ahead = pair_sum(tie(late[1], early[1], sent)[0])
            return nt(d, w_gate[layer]), (fold(early_grads(b, d, a, c)), ahead)

        outg, (((dx, dbc, hs), _), (du, (early[layer], ahead))) = chain_scan(
            back, True, [beside_first, beside_second]
        )
        if layer == 0:
            outg, first, second = tie(outg, early[1], ahead)
            upper = scatter_sum(jnp.concatenate([first, second], axis=1))
        dre, tail, front, dw, dh = conv_backward(
            outg, inc, q, ds, dt, total, col_padded, e, rc, halo, dy, dx, dbc, hs, par, spread
        )
        returned = lax.ppermute(front, everywhere, precede)
        dre = lax.dynamic_update_slice(dre, (tail + returned).astype(bf16), (rows - 8, 0))
        du = du + nt(dre, w_conv[layer])
        wide = hidden.astype(f32)
        normed = wide * scale
        dn = du * par[NORM : NORM + 1, :D]
        dnorm = jnp.sum(du * normed, axis=0)
        dhidden = scale * (dn - normed * jnp.mean(dn * normed, axis=1, keepdims=True))
        grad_e = columns(dre[:, CONVCH:], u)[:H].reshape(H // 2, 2 * D)
        if layer == 0:
            dre, upper, early[0] = tie(dre, upper, early[0])
            upper = collect(upper)
            early[0] = pair_sum(early[0])
        late[layer] = fold(late_grads(u, dre[:, :CONVCH]))
        grad = (grad.astype(f32) + dhidden).astype(bf16)
        input_grads[layer] = grad
        small[layer] = jnp.concatenate(
            [
                dw[: CONV + 1],
                jnp.pad(dnorm, (0, CONVCH - D))[None],
                jnp.pad(dgain, ((0, 0), (0, CONVCH - DI))),
                jnp.pad(dh[0:3], ((0, 0), (0, CONVCH - 128))),
                jnp.pad(grad_e, ((0, 0), (0, CONVCH - 2 * D))),
            ],
            axis=0,
        )
    late[0], upper, early[0] = tie(late[0], upper, early[0])
    early[0] = scatter_sum(early[0])
    late[0] = pair_sum(late[0])
    upper = pair_collect(upper)
    early[1], late[1] = upper[:, :DI], upper[:, DI:]
    late[0], early[0] = tie(late[0], early[0])
    late[0] = pair_collect(collect(scatter_sum(late[0])))
    early[0] = pair_collect(collect(early[0]))
    early_got = lax.ppermute(pick(low, early[1], early[0]), "section", SWAP)
    late_got = lax.ppermute(pick(low, late[1], late[0]), "section", SWAP)
    mine = pick(low, small[0], small[1]) + lax.ppermute(pick(low, small[1], small[0]), "section", SWAP)
    mine = sum_everywhere(mine)
    grad_e = mine[SKIP + 1 :, : 2 * D].reshape(H, parts, D // parts)
    grad_e = lax.dynamic_index_in_dim(grad_e, lax.axis_index("fsdp"), 1, keepdims=False).T
    shard_in, shard_out = place(
        pick(low, early[0], early[1]),
        early_got,
        pick(low, late[0], late[1]),
        late_got,
        jnp.pad(grad_e, ((0, 0), (0, 128 - H))),
    )

    def to_holders(first, second):
        even = micro == 0
        one, two = [], []
        for k in range(size // 2):
            for s in range(2):
                one += [(flat(s, 2 * k), flat(0, 2 * k + s)), (flat(s, 2 * k + 1), flat(1, 2 * k + s))]
                two += [(flat(s, 2 * k), flat(1, 2 * k + s)), (flat(s, 2 * k + 1), flat(0, 2 * k + s))]
        got_one = lax.ppermute(pick(even, first, second), everywhere, one)
        got_two = lax.ppermute(pick(even, second, first), everywhere, two)
        stacked = jnp.stack([pick(low, got_one, got_two), pick(low, got_two, got_one)])
        return stacked[None, :, None]

    activations = to_holders(results[0], results[1])
    grads = to_holders(input_grads[0], input_grads[1])
    return (
        activations,
        grads,
        mine[NORM : NORM + 1, :D],
        shard_in,
        mine[None, :CONV],
        mine[TAP_BIAS : TAP_BIAS + 1],
        mine[STEP_BIAS : STEP_BIAS + 1, :H],
        mine[BASE_RATE : BASE_RATE + 1, :H],
        mine[SKIP : SKIP + 1, :H],
        mine[GAIN : GAIN + 1, :DI],
        shard_out,
    )


def solution(mesh):
    in_specs = (
        P(None, "fsdp", "seq", None),
        P(None, "fsdp", "seq", None),
        P(None, "fsdp", None),
        P(None, "fsdp", None),
        P("section", None),
        P("section", "fsdp", None),
        P("section", None, None),
        P("section", None),
        P("section", None),
        P("section", None),
        P("section", None),
        P("section", None),
        P("section", "fsdp", None),
    )
    out_specs = (
        P("section", None, "fsdp", "seq", None),
        P("section", None, "fsdp", "seq", None),
        P("section", None),
        P("section", "fsdp", None),
        P("section", None, None),
        P("section", None),
        P("section", None),
        P("section", None),
        P("section", None),
        P("section", None),
        P("section", "fsdp", None),
    )
    return jax.shard_map(local, mesh=mesh, in_specs=in_specs, out_specs=out_specs, check_vma=False)
```

```python
import jax
import jax.numpy as jnp
from jax import lax
from jax.experimental import pallas as pl
from jax.experimental.pallas import tpu as pltpu
from jax.sharding import PartitionSpec as P

D = 768
DI = 1536
H = 24
P_SIZE = 64
STATE = 128
CONV = 4
CONVCH = 1792
Q = 128
HALF = DI // 2
PACK = STATE + 16
PACK_WIDE = STATE + 8
TAP_BIAS, NORM, GAIN, STEP_BIAS, BASE_RATE, SKIP = 4, 5, 6, 7, 8, 9
TABLE = (16, CONVCH)
SWAP = ((0, 1), (1, 0))

f32 = jnp.float32
bf16 = jnp.bfloat16
epsilon = 1e-05
masked = -1e30


def nn(a, b):
    return lax.dot_general(a, b, (((1,), (0,)), ((), ())), preferred_element_type=f32)


def nt(a, b):
    return lax.dot_general(a, b, (((1,), (1,)), ((), ())), preferred_element_type=f32)


def tn(a, b):
    return nn(a.astype(f32).T.astype(bf16), b)


def split(v):
    high = v.astype(bf16)
    return high, (v - high.astype(f32)).astype(bf16)


def expand(v, spread):
    high, low = split(v)
    return nn(high, spread) + nn(low, spread)


def expand_row(v, spread):
    return expand(jnp.broadcast_to(v, (8, v.shape[1])), spread)[0:1]


def head_sum(v, spread):
    high, low = split(v)
    return nt(high, spread) + nt(low, spread)


def tri_sum(tri, v):
    high, rest = split(v)
    middle, low = split(v - high.astype(f32))
    return nn(tri, high) + nn(tri, middle) + nn(tri, low)


def iota(shape, dim):
    return lax.broadcasted_iota(jnp.int32, shape, dim)


def spread_matrix():
    return (iota((128, DI), 1) // P_SIZE == iota((128, DI), 0)).astype(bf16)


def two_heads(tile):
    left = iota(tile.shape, 1) < P_SIZE
    zero = jnp.zeros_like(tile)
    return jnp.concatenate([jnp.where(left, tile, zero), jnp.where(left, zero, tile)], axis=0)


def product(a, a_low, b, b_low):
    both = jnp.concatenate([b, b_low], axis=0)
    return nn(jnp.concatenate([a, a], axis=1), both) + nn(a_low, b)


def decay_rows(decay):
    high, low = split(decay)
    row = iota((16, decay.shape[1]), 0)
    both = jnp.where(row == 0, high.astype(f32), jnp.where(row == 1, low.astype(f32), 0.0))
    return both.astype(bf16)


def label_kernel(doc_ref, table_ref, col_ref, lab_ref):
    rows = col_ref.shape[0]
    base = doc_ref[8]
    ends = []
    end = 0
    for k in range(4):
        end = end + doc_ref[doc_ref[4 + k]]
        ends.append(end)

    def label(position):
        found = jnp.zeros(position.shape, jnp.int32)
        for bound in ends:
            found = found + (position >= bound).astype(jnp.int32)
        return jnp.where(position < 0, -1, found)

    def columns(row, lane):
        here = label(base + row)
        block = (row // Q) * Q
        other = jnp.where(
            lane < 3,
            row - 1 - lane,
            jnp.where(lane == 3, block - 1, jnp.where(lane == 4, block + Q - 1, jnp.where(lane == 5, -1, rows - 1))),
        )
        same = (label(base + other) == here).astype(f32)
        return jnp.where(lane == 7, here.astype(f32), same)

    lane = iota((rows + 16, 128), 1)
    row = iota((rows + 16, 128), 0) - 8
    whole_table = columns(jnp.clip(row, 0, rows - 1), lane)
    table_ref[...] = jnp.where((row >= 0) & (row < rows), whole_table, 0.0)
    col_ref[...] = columns(iota((rows, 128), 0), iota((rows, 128), 1))
    lab_ref[...] = label(base + iota((8, rows), 1)).astype(f32)


def head_row(par_ref, k):
    return jnp.where(iota((1, 128), 1) < H, par_ref[k : k + 1, 0:128], 0.0)


def rates(par_ref):
    return jnp.where(iota((1, 128), 1) < H, -jnp.exp(par_ref[BASE_RATE : BASE_RATE + 1, 0:128]), 0.0)


def skip_row(par_ref, spread):
    return expand_row(head_row(par_ref, SKIP), spread)


def conv_kernel(
    rc_ref, halo_ref, e_ref, col_ref, par_ref, sp_ref,
    q_ref, ds_ref, dt_ref, cum_ref, all_ref, lin_ref, pack_ref,
):
    spread = sp_ref[...]
    tri = (iota((Q, Q), 0) >= iota((Q, Q), 1)).astype(bf16)
    rate = rates(par_ref)
    bias = head_row(par_ref, STEP_BIAS)
    state = jnp.zeros((STATE, DI), f32)
    offset = jnp.zeros((1, 128), f32)
    decay = jnp.ones((1, 128), f32)
    for c in range(rc_ref.shape[0] // Q):
        rows = slice(c * Q, (c + 1) * Q)
        col = col_ref[rows, :]
        dt = jax.nn.softplus(e_ref[rows, :] + bias)
        cum = tri_sum(tri, dt * rate)
        dt_ref[rows, :] = dt
        cum_ref[rows, :] = cum
        all_ref[rows, :] = cum + offset
        for j in range(CONVCH // 128):
            lanes = slice(j * 128, (j + 1) * 128)
            if c == 0:
                window = jnp.concatenate([halo_ref[:, lanes], rc_ref[0:Q, lanes]], axis=0)
            else:
                window = rc_ref[c * Q - 16 : (c + 1) * Q, lanes]
            window = window.astype(f32)
            pre = par_ref[TAP_BIAS : TAP_BIAS + 1, lanes] + par_ref[3:4, lanes] * window[16:]
            for d in range(1, CONV):
                pre = pre + par_ref[3 - d : 4 - d, lanes] * window[16 - d : 16 + Q - d] * col[:, d - 1 : d]
            gate = jax.nn.sigmoid(pre)
            out = pre * gate
            q_ref[rows, lanes] = out
            ds_ref[rows, lanes] = (gate + out * (1.0 - gate)).astype(bf16)
        end = cum[Q - 1 : Q, :]
        weight = dt * jnp.exp(end - cum) * col[:, 4:5]
        scaled, scaled_low = split(q_ref[rows, 0:DI] * expand(weight, spread))
        b_rows, b_low = split(q_ref[rows, DI : DI + STATE].T)
        lin_ref[c, 0:STATE], lin_ref[c, STATE:] = split(state)
        step = jnp.exp(end) * col[Q - 1 : Q, 3:4]
        state = state * expand_row(step, spread) + product(b_rows, b_low, scaled, scaled_low)
        decay = decay * step
        offset = offset + end
    wide = expand_row(decay, spread)
    for half in range(2):
        lanes = slice(half * HALF, (half + 1) * HALF)
        pack_ref[half, 0:STATE, :] = state[:, lanes]
        pack_ref[half, STATE:, :] = jnp.broadcast_to(wide[:, lanes], (8, HALF))


def intra_kernel(q_ref, dt_ref, cum_ref, col_ref, lab_ref, lin_ref, par_ref, sp_ref, y_ref):
    spread = sp_ref[...]
    col = col_ref[...]
    cum = cum_ref[...]
    cum_t = cum.T
    x = q_ref[:, 0:DI]
    b_rows, b_low = split(q_ref[:, DI : DI + STATE])
    c_rows, c_low = split(q_ref[:, DI + STATE :])
    x_dt, x_low = split(x * expand(dt_ref[...], spread))
    scores = nt(c_rows, b_rows) + (nt(c_rows, b_low) + nt(c_low, b_rows))
    same = (col[:, 7:8] == lab_ref[0:1, :]) & (iota((Q, Q), 0) >= iota((Q, Q), 1))
    shut = jnp.where(same, 0.0, masked)
    reach = expand(jnp.exp(cum) * col[:, 3:4], spread)
    base = product(c_rows, c_low, lin_ref[0, 0:STATE], lin_ref[0, STATE:]) * reach + skip_row(par_ref, spread) * x
    for j in range(H // 2):
        lanes = slice(j * 128, (j + 1) * 128)
        mixing, mixing_low = split(
            jnp.concatenate(
                [
                    jnp.exp(cum[:, h : h + 1] - cum_t[h : h + 1, :] + shut) * scores
                    for h in (2 * j, 2 * j + 1)
                ],
                axis=1,
            )
        )
        pair = two_heads(x_dt[:, lanes])
        y_ref[:, lanes] = (
            base[:, lanes]
            + nn(mixing, pair)
            + (nn(mixing_low, pair) + nn(mixing, two_heads(x_low[:, lanes])))
        )


def gate_kernel(
    y0_ref, z_ref, c_ref, all_ref, col_ref, inc_ref, par_ref, w_ref, x_ref, sp_ref,
    y_ref, v_ref, out_ref,
):
    reach = jnp.exp(all_ref[...]) * col_ref[:, 5:6]
    y = y0_ref[...] + expand(reach, sp_ref[...]) * product(
        *split(c_ref[...]), *split(inc_ref[...])
    )
    y_ref[...] = y
    z = z_ref[...]
    gated = y * (z * jax.nn.sigmoid(z))
    scale = lax.rsqrt(jnp.mean(gated * gated, axis=1, keepdims=True) + epsilon)
    v = (gated * scale * par_ref[GAIN : GAIN + 1, 0:DI]).astype(bf16)
    v_ref[...] = v
    out_ref[...] = (x_ref[...].astype(f32) + nn(v, w_ref[...])).astype(bf16)


def gate_back_kernel(
    g_ref, w_ref, y_ref, z_ref, par_ref, c_ref, all_ref, col_ref, decay_ref, sp_ref,
    dy_ref, dz_ref, dgain_ref, pack_ref, total_ref,
):
    step = pl.program_id(0)
    dv = nt(g_ref[...], w_ref[...])
    y = y_ref[...]
    z = z_ref[...]
    gate = jax.nn.sigmoid(z)
    silu = z * gate
    gated = y * silu
    scale = lax.rsqrt(jnp.mean(gated * gated, axis=1, keepdims=True) + epsilon)
    normed = gated * scale
    dn = dv * par_ref[GAIN : GAIN + 1, 0:DI]
    dgated = scale * (dn - normed * jnp.mean(dn * normed, axis=1, keepdims=True))
    dz_ref[...] = (dgated * y * (gate + silu * (1.0 - gate))).astype(bf16)
    dy = (dgated * silu).astype(bf16)
    dy_ref[...] = dy
    reach = jnp.exp(all_ref[...]) * col_ref[:, 5:6]
    reached = (dy.astype(f32) * expand(reach, sp_ref[...])).astype(bf16)
    part = tn(c_ref[...], reached)
    gain_part = jnp.sum(dv * normed, axis=0, keepdims=True)

    @pl.when(step == 0)
    def _():
        total_ref[...] = part
        dgain_ref[...] = gain_part

    @pl.when(step > 0)
    def _():
        total_ref[...] += part
        dgain_ref[...] += gain_part

    @pl.when(step == pl.num_programs(0) - 1)
    def _():
        for half in range(2):
            pack_ref[half, 0:STATE, :] = total_ref[:, half * HALF : (half + 1) * HALF].astype(bf16)
            pack_ref[half, STATE:, :] = decay_rows(decay_ref[half, STATE : STATE + 1, :])


def intra_back_kernel(
    q_ref, dt_ref, cum_ref, all_ref, col_ref, lab_ref, lin_ref, inc_ref, dy_ref, y_ref, par_ref, sp_ref,
    dx_ref, dbc_ref, hs_ref, carry_ref,
):
    @pl.when(pl.program_id(0) == 0)
    def _():
        carry_ref[...] = jnp.zeros_like(carry_ref)

    spread = sp_ref[...]
    col = col_ref[...]
    cum = cum_ref[...]
    cum_t = cum.T
    x = q_ref[:, 0:DI]
    b_rows, b_low = split(q_ref[:, DI : DI + STATE])
    c_rows, c_low = split(q_ref[:, DI + STATE :])
    dy = dy_ref[...]
    dy32 = dy.astype(f32)
    x_wide = x * expand(dt_ref[...], spread)
    x_dt = x_wide.astype(bf16)
    end = cum[Q - 1 : Q, :]
    leave = expand(jnp.exp(end - cum) * col[:, 4:5], spread)
    carry = carry_ref[...]
    carry_high, carry_low = split(carry)
    base = product(b_rows, b_low, carry_high, carry_low) * leave
    scores = nt(b_rows, c_rows) + (nt(b_low, c_rows) + nt(b_rows, c_low))
    same = (col[:, 7:8] == lab_ref[0:1, :]) & (iota((Q, Q), 1) >= iota((Q, Q), 0))
    shut = jnp.where(same, 0.0, masked)
    dscores = jnp.zeros((Q, Q), f32)
    for j in range(H // 2):
        lanes = slice(j * 128, (j + 1) * 128)
        dy_pair = dy[:, lanes]
        grads = nt(two_heads(x_dt[:, lanes]), dy_pair)
        mixing = []
        for k in range(2):
            h = 2 * j + k
            kernel = jnp.exp(cum_t[h : h + 1, :] - cum[:, h : h + 1] + shut)
            mixing.append(kernel * scores)
            dscores = dscores + grads[k * Q : (k + 1) * Q] * kernel
        mixing, mixing_low = split(jnp.concatenate(mixing, axis=1))
        pair = two_heads(dy_pair)
        dx_ref[:, lanes] = base[:, lanes] + nn(mixing, pair) + nn(mixing_low, pair)
    dx = dx_ref[...]
    near, near_low = split(dy32 * expand(jnp.exp(cum) * col[:, 3:4], spread))
    far = (dy32 * expand(jnp.exp(all_ref[...]) * col[:, 5:6], spread)).astype(bf16)
    low = dscores.astype(bf16)
    inc_high, inc_low = split(inc_ref[...])
    left = (x_wide * leave).astype(bf16)
    dbc_ref[:, 0:STATE] = nn(low, c_rows) + nt(left, carry_high)
    dbc_ref[:, STATE:] = (
        nn(dscores.T.astype(bf16), b_rows)
        + nt(near, lin_ref[0, 0:STATE])
        + nt(near, lin_ref[0, STATE:])
        + nt(far, inc_high)
        + nt(far, inc_low)
    )
    hs_ref[:, 0:128] = head_sum(
        dy32 * (y_ref[...] - skip_row(par_ref, spread) * x) - x_wide * dx, spread
    )
    hs_ref[:, 128:] = head_sum(x * dx, spread)
    step = jnp.exp(end) * col[Q - 1 : Q, 3:4]
    c_rows, c_low = split(q_ref[:, DI + STATE :].T)
    carry_ref[...] = carry * expand_row(step, spread) + product(c_rows, c_low, near, near_low)


def conv_back_kernel(
    outg_ref, inc_ref, q_ref, ds_ref, dt_ref, all_ref, col_ref, e_ref, rc_ref, halo_ref,
    dy_ref, dx_ref, dbc_ref, hs_ref, par_ref, sp_ref,
    dr_ref, de_ref, tail_ref, back_ref, dw_ref, dh_ref, pre_ref, sum_ref,
):
    count = q_ref.shape[0] // Q
    spread = sp_ref[...]
    outg = outg_ref[...]
    last = all_ref[count * Q - 1 : count * Q, :]
    skip = skip_row(par_ref, spread)
    rate = rates(par_ref)
    bias = head_row(par_ref, STEP_BIAS)
    total = jnp.zeros((1, 128), f32)
    skip_total = jnp.zeros((1, 128), f32)
    pre_ref[0:8, :] = jnp.zeros((8, CONVCH), f32)
    pre_ref[8 + count * Q :, :] = jnp.zeros((8, CONVCH), f32)
    for c in range(count):
        rows = slice(c * Q, (c + 1) * Q)
        moved = slice(8 + c * Q, 8 + (c + 1) * Q)
        col = col_ref[moved, :]
        x = q_ref[rows, 0:DI]
        dy = dy_ref[rows, :].astype(f32)
        wide_dt = expand(dt_ref[rows, :], spread)
        x_dt = (x * wide_dt).astype(bf16).astype(f32)
        leave = expand(jnp.exp(last - all_ref[rows, :]) * col[:, 6:7], spread)
        dx_far = leave * nn(q_ref[rows, DI : DI + STATE].astype(bf16), outg)
        dx = dx_ref[rows, :] + dx_far
        db = dbc_ref[rows, 0:STATE] + nt((x_dt * leave).astype(bf16), outg)
        far = head_sum(x_dt * dx_far, spread)
        total = total + jnp.sum(far, axis=0, keepdims=True)
        sum_ref[rows, 0:128] = hs_ref[rows, 0:128] - far
        sum_ref[rows, 128:] = hs_ref[rows, 128:] + head_sum(x * dx_far, spread)
        skip_total = skip_total + jnp.sum(head_sum(x * dy, spread), axis=0, keepdims=True)
        pre_ref[moved, 0:DI] = (wide_dt * dx + skip * dy) * ds_ref[rows, 0:DI].astype(f32)
        pre_ref[moved, DI : DI + STATE] = db * ds_ref[rows, DI : DI + STATE].astype(f32)
        pre_ref[moved, DI + STATE :] = dbc_ref[rows, STATE:] * ds_ref[rows, DI + STATE :].astype(f32)
    kept = jnp.exp(last) * col_ref[7 + count * Q : 8 + count * Q, 5:6]
    both = jnp.sum(outg.astype(f32) * inc_ref[...], axis=0, keepdims=True)
    through = kept * head_sum(jnp.broadcast_to(both, (8, DI)), spread)[0:1]
    tri = (iota((Q, Q), 0) <= iota((Q, Q), 1)).astype(bf16)
    later = total + through
    rate_total = jnp.zeros((1, 128), f32)
    bias_total = jnp.zeros((1, 128), f32)
    for c in reversed(range(count)):
        rows = slice(c * Q, (c + 1) * Q)
        sums = tri_sum(tri, sum_ref[rows, 0:128])
        dlog = sums + later
        later = later + sums[0:1]
        ddt = rate * dlog + sum_ref[rows, 128:]
        de = ddt * jax.nn.sigmoid(e_ref[rows, :] + bias)
        de_ref[rows, :] = jnp.where(iota((Q, 128), 1) < H, de, 0.0).astype(bf16)
        rate_total = rate_total + jnp.sum(dlog * dt_ref[rows, :], axis=0, keepdims=True)
        bias_total = bias_total + jnp.sum(de, axis=0, keepdims=True)
    row = iota((8, 128), 0)
    dh_ref[...] = jnp.where(
        row == 0,
        bias_total,
        jnp.where(row == 1, rate_total * rate, jnp.where(row == 2, skip_total, 0.0)),
    )
    for j in range(CONVCH // 128):
        lanes = slice(j * 128, (j + 1) * 128)
        taps = [par_ref[3 - d : 4 - d, lanes] for d in range(CONV)]
        sums = [jnp.zeros((1, 128), f32) for _ in range(CONV + 1)]
        front = pre_ref[0:16, lanes]
        early = jnp.zeros((8, 128), f32)
        for d in range(1, CONV):
            early = early + taps[d] * (front * col_ref[0:16, d - 1 : d])[d : d + 8]
        back_ref[:, lanes] = early
        for c in range(count):
            rows = slice(c * Q, (c + 1) * Q)
            ahead = pre_ref[8 + c * Q : 16 + (c + 1) * Q, lanes]
            col = col_ref[8 + c * Q : 16 + (c + 1) * Q, :]
            if c == 0:
                window = jnp.concatenate([halo_ref[:, lanes], rc_ref[0:Q, lanes]], axis=0)
            else:
                window = rc_ref[c * Q - 16 : (c + 1) * Q, lanes]
            window = window.astype(f32)
            here = ahead[0:Q]
            sums[CONV] = sums[CONV] + jnp.sum(here, axis=0, keepdims=True)
            sums[3] = sums[3] + jnp.sum(here * window[16:], axis=0, keepdims=True)
            grad = taps[0] * here
            for d in range(1, CONV):
                same = ahead * col[:, d - 1 : d]
                sums[3 - d] = sums[3 - d] + jnp.sum(
                    same[0:Q] * window[16 - d : 16 + Q - d], axis=0, keepdims=True
                )
                grad = grad + taps[d] * same[d : d + Q]
            dr_ref[rows, lanes] = grad.astype(bf16)
            if c == count - 1:
                tail_ref[:, lanes] = grad[Q - 8 :]
        row = iota((8, 128), 0)
        stacked = jnp.zeros((8, 128), f32)
        for k in range(CONV + 1):
            stacked = jnp.where(row == k, sums[k], stacked)
        dw_ref[:, lanes] = stacked


def params(steps):
    return pltpu.CompilerParams(
        dimension_semantics=("arbitrary",) * steps, vmem_limit_bytes=48 * 1024 * 1024
    )


def shape(*dims, dtype=f32):
    return jax.ShapeDtypeStruct(dims, dtype)


def whole(array):
    rank = len(array.shape)
    return pl.BlockSpec(array.shape, lambda *_: (0,) * rank)


def conv_forward(rc, halo, e, col, par, spread):
    rows = rc.shape[0]
    outs = (
        shape(rows, CONVCH),
        shape(rows, CONVCH, dtype=bf16),
        shape(rows, 128),
        shape(rows, 128),
        shape(rows, 128),
        shape(rows // Q, 2 * STATE, DI, dtype=bf16),
        shape(2, PACK_WIDE, HALF),
    )
    return pl.pallas_call(conv_kernel, out_shape=outs, compiler_params=params(0))(
        rc, halo, e, col, par, spread
    )


def intra_forward(q, dt, cum, col, lab, lin, par, spread):
    rows = q.shape[0]

    def by_row(width):
        return pl.BlockSpec((Q, width), lambda i: (i, 0))

    return pl.pallas_call(
        intra_kernel,
        grid=(rows // Q,),
        in_specs=[
            by_row(CONVCH),
            by_row(128),
            by_row(128),
            by_row(128),
            pl.BlockSpec((8, Q), lambda i: (0, i)),
            pl.BlockSpec((1, 2 * STATE, DI), lambda i: (i, 0, 0)),
            whole(par),
            whole(spread),
        ],
        out_specs=by_row(DI),
        out_shape=shape(rows, DI),
        compiler_params=params(1),
        cost_estimate=pl.CostEstimate(
            flops=8 * rows * Q * DI, bytes_accessed=rows * 20000, transcendentals=rows * Q * H
        ),
    )(q, dt, cum, col, lab, lin, par, spread)


def gate_forward(y0, z, q, total, col, inc, par, w_out, hidden, spread):
    rows = y0.shape[0]
    size = 256

    def by_row(width):
        return pl.BlockSpec((size, width), lambda i: (i, 0))

    return pl.pallas_call(
        gate_kernel,
        grid=(rows // size,),
        in_specs=[
            by_row(DI),
            by_row(DI),
            pl.BlockSpec((size, STATE), lambda i: (i, (DI + STATE) // STATE)),
            by_row(128),
            by_row(128),
            whole(inc),
            whole(par),
            whole(w_out),
            by_row(D),
            whole(spread),
        ],
        out_specs=(by_row(DI), by_row(DI), by_row(D)),
        out_shape=(shape(rows, DI), shape(rows, DI, dtype=bf16), shape(rows, D, dtype=bf16)),
        compiler_params=params(1),
    )(y0, z, q, total, col, inc, par, w_out, hidden, spread)


def gate_backward(grad, w_out, y, z, par, q, total, col, pack, spread):
    rows = y.shape[0]
    size = 256

    def by_row(width):
        return pl.BlockSpec((size, width), lambda i: (i, 0))

    outs = (
        shape(rows, DI, dtype=bf16),
        shape(rows, DI, dtype=bf16),
        shape(1, DI),
        shape(2, PACK, HALF, dtype=bf16),
    )
    return pl.pallas_call(
        gate_back_kernel,
        grid=(rows // size,),
        in_specs=[
            by_row(D),
            whole(w_out),
            by_row(DI),
            by_row(DI),
            whole(par),
            pl.BlockSpec((size, STATE), lambda i: (i, (DI + STATE) // STATE)),
            by_row(128),
            by_row(128),
            whole(pack),
            whole(spread),
        ],
        out_specs=(by_row(DI), by_row(DI), whole(outs[2]), whole(outs[3])),
        out_shape=outs,
        scratch_shapes=[pltpu.VMEM((STATE, DI), f32)],
        compiler_params=params(1),
    )(grad, w_out, y, z, par, q, total, col, pack, spread)


def intra_backward(q, dt, cum, total, col, lab, lin, inc, dy, y, par, spread):
    rows = q.shape[0]
    top = rows // Q - 1

    def by_row(width):
        return pl.BlockSpec((Q, width), lambda i: (top - i, 0))

    return pl.pallas_call(
        intra_back_kernel,
        grid=(rows // Q,),
        in_specs=[
            by_row(CONVCH),
            by_row(128),
            by_row(128),
            by_row(128),
            by_row(128),
            pl.BlockSpec((8, Q), lambda i: (0, top - i)),
            pl.BlockSpec((1, 2 * STATE, DI), lambda i: (top - i, 0, 0)),
            whole(inc),
            by_row(DI),
            by_row(DI),
            whole(par),
            whole(spread),
        ],
        out_specs=(by_row(DI), by_row(256), by_row(256)),
        out_shape=(shape(rows, DI), shape(rows, 256), shape(rows, 256)),
        scratch_shapes=[pltpu.VMEM((STATE, DI), f32)],
        compiler_params=params(1),
        cost_estimate=pl.CostEstimate(
            flops=30 * rows * Q * DI, bytes_accessed=rows * 30000, transcendentals=rows * Q * H
        ),
    )(q, dt, cum, total, col, lab, lin, inc, dy, y, par, spread)


def conv_backward(outg, inc, q, ds, dt, total, col, e, rc, halo, dy, dx, dbc, hs, par, spread):
    rows = q.shape[0]
    outs = (
        shape(rows, CONVCH, dtype=bf16),
        shape(rows, 128, dtype=bf16),
        shape(8, CONVCH),
        shape(8, CONVCH),
        shape(8, CONVCH),
        shape(8, 128),
    )
    return pl.pallas_call(
        conv_back_kernel,
        out_shape=outs,
        scratch_shapes=[pltpu.VMEM((rows + 16, CONVCH), f32), pltpu.VMEM((rows, 256), f32)],
        compiler_params=params(0),
    )(outg, inc, q, ds, dt, total, col, e, rc, halo, dy, dx, dbc, hs, par, spread)


def pick(first, a, b):
    return jnp.where(first, a, b)


def unpack(block):
    wide = block.astype(f32)
    if block.dtype == f32:
        return wide[STATE : STATE + 1], wide[:STATE]
    return wide[STATE : STATE + 1] + wide[STATE + 1 : STATE + 2], wide[:STATE]


def pack_up(pair, kind):
    if kind == f32:
        decay = jnp.broadcast_to(pair[0], (8, HALF))
        return jnp.concatenate([pair[1], decay], axis=0)
    return jnp.concatenate([pair[1].astype(bf16), decay_rows(pair[0])], axis=0)


def combine(earlier, later):
    return (earlier[0] * later[0], later[0] * earlier[1] + later[1])


def chain_scan(pack, reverse, beside):
    section = lax.axis_index("section")
    size = lax.axis_size("seq")
    kept = lax.dynamic_index_in_dim(pack, section, 0, keepdims=False)
    given = lax.dynamic_index_in_dim(pack, 1 - section, 0, keepdims=False)
    got = lax.ppermute(given, "section", SWAP)
    leads = (section == 1) if reverse else (section == 0)
    lead = unpack(pick(leads, kept, got))
    follow = unpack(pick(leads, got, kept))
    reached = combine(lead, follow)
    before = None
    distance = 2
    results = []
    other = None
    while distance < size:
        route = [(i, i + distance) for i in range(size - distance)]
        if reverse:
            route = [(b, a) for a, b in route]
        sent = pack_up(reached, pack.dtype)
        if beside:
            arrays, work = beside.pop(0)
            sent, arrays = tie(sent, arrays)
            arrived = lax.ppermute(sent, "seq", route)
            needed, other = work(other, *arrays)
            arrived, needed = tie(arrived, needed)
            results.append((needed, other))
        else:
            arrived = lax.ppermute(sent, "seq", route)
        arrived = unpack(arrived)
        before = arrived if before is None else combine(arrived, before)
        reached = combine(arrived, reached)
        distance *= 2
    first = before[1]
    second = lead[1] + lead[0] * first
    own = pick(leads, first, second).astype(pack.dtype)
    other = lax.ppermute(pick(leads, second, first).astype(pack.dtype), "section", SWAP)
    low = section == 0
    incoming = jnp.concatenate([pick(low, own, other), pick(low, other, own)], axis=1)
    return incoming, results


def move_rows(shard, layer):
    parts = lax.axis_size("fsdp")
    blocks = [shard]
    for shift in range(1, parts):
        route = [(layer * parts + i, layer * parts + (i + shift) % parts) for i in range(parts)]
        blocks.append(lax.ppermute(shard, ("section", "fsdp"), route))
    return blocks


def share(blocks, layer):
    section, row = lax.axis_index("section"), lax.axis_index("fsdp")
    parts = lax.axis_size("fsdp")
    across = [(layer, 1 - layer)]
    blocks = [pick(section == layer, block, lax.ppermute(block, "section", across)) for block in blocks]
    if parts == 2:
        low = row == 0
        return [pick(low, blocks[0], blocks[1]), pick(low, blocks[1], blocks[0])]
    ordered = []
    for k in range(parts):
        block = blocks[0]
        for shift in range(1, parts):
            block = pick((row - shift) % parts == k, blocks[shift], block)
        ordered.append(block)
    return ordered


def row_sum(summed):
    row, parts = lax.axis_index("fsdp"), lax.axis_size("fsdp")
    if parts == 2:
        kept = lax.dynamic_index_in_dim(summed, row, 0, keepdims=False)
        given = lax.dynamic_index_in_dim(summed, 1 - row, 0, keepdims=False)
        got = lax.ppermute(given, "fsdp", SWAP)
        return (kept.astype(f32) + got.astype(f32)).astype(bf16)
    return lax.psum_scatter(summed, "fsdp", scatter_dimension=0, tiled=False)


def halve(array, distance):
    size, bit = lax.axis_size("seq"), (lax.axis_index("seq") // distance) % 2
    halves = array.reshape(2, -1, array.shape[1])
    kept = lax.dynamic_index_in_dim(halves, bit, 0, keepdims=False)
    given = lax.dynamic_index_in_dim(halves, 1 - bit, 0, keepdims=False)
    got = lax.ppermute(given, "seq", [(i, i ^ distance) for i in range(size)])
    return (kept.astype(f32) + got.astype(f32)).astype(bf16)


def rejoin(array, distance):
    size, low = lax.axis_size("seq"), (lax.axis_index("seq") // distance) % 2 == 0
    got = lax.ppermute(array, "seq", [(i, i ^ distance) for i in range(size)])
    return jnp.concatenate([pick(low, array, got), pick(low, got, array)], axis=0)


def distances():
    found = [1]
    while 2 * found[-1] < lax.axis_size("seq"):
        found.append(2 * found[-1])
    return found


def exchanges():
    found = []
    for axis in ("fsdp", "seq"):
        distance = 1
        while distance < lax.axis_size(axis):
            found.append((axis, distance))
            distance *= 2
    return found


def exchange_sum(array, step):
    axis, distance = step
    partners = [(i, i ^ distance) for i in range(lax.axis_size(axis))]
    return array + lax.ppermute(array, axis, partners)


def tie(*arrays):
    return lax.optimization_barrier(arrays)


def place_kernel(
    section_ref, early_ref, early_got_ref, late_ref, late_got_ref, e_ref, in_ref, out_ref
):
    low = section_ref[0] == 0
    conv_rows = CONVCH // 2
    for half in range(2):
        own = low if half == 0 else jnp.logical_not(low)

        def block(ref, got_ref, start, count):
            rows = slice(start, start + count)
            return jnp.where(own, ref[rows, :], got_ref[rows, :]).astype(f32)

        in_ref[half * HALF : (half + 1) * HALF, :] = block(early_ref, early_got_ref, 0, HALF)
        lanes = slice(half * (D // 2), (half + 1) * (D // 2))
        out_ref[:, lanes] = block(early_ref, early_got_ref, HALF, HALF)
        at = DI + half * conv_rows
        in_ref[at : at + conv_rows, :] = block(late_ref, late_got_ref, 0, conv_rows)
    in_ref[DI + CONVCH :, :] = e_ref[...]


def place(early, early_got, late, late_got, e, rows_out):
    section = lax.axis_index("section")
    width = early.shape[1]
    if rows_out == HALF:
        vmem = pl.BlockSpec(memory_space=pltpu.VMEM)
        w_in, w_out = pl.pallas_call(
            place_kernel,
            in_specs=[pl.BlockSpec(memory_space=pltpu.SMEM)] + [vmem] * 5,
            out_shape=(shape(DI + CONVCH + H, width), shape(rows_out, D)),
            compiler_params=params(0),
        )(section.astype(jnp.int32)[None], early, early_got, late, late_got, e)
        return w_in.T[None], w_out[None]
    gates, convs, backs = [], [], []
    for half in range(2):
        array = pick(section == half, early, early_got).astype(f32)
        gates.append(array[:HALF])
        backs += [array[at : at + rows_out] for at in range(HALF, 2 * HALF, rows_out)]
        convs.append(pick(section == half, late, late_got).astype(f32))
    w_in = jnp.concatenate(gates + convs + [e], axis=0)
    return w_in.T[None], jnp.concatenate(backs, axis=1)[None]


def labels(lengths, order, base, rows):
    documents = jnp.concatenate([lengths, order, base[None]]).astype(jnp.int32)
    return pl.pallas_call(
        label_kernel,
        in_specs=[pl.BlockSpec(memory_space=pltpu.SMEM)],
        out_shape=(shape(rows + 16, 128), shape(rows, 128), shape(8, rows)),
        compiler_params=params(0),
    )(documents)


def parameter_table(norm_gain, conv_w, conv_b, dt_bias, a_log, skip_scale, gate_gain):
    def row(array):
        return jnp.pad(array, ((0, 0), (0, CONVCH - array.shape[1])))

    pieces = [conv_w, conv_b, row(norm_gain), row(gate_gain), row(dt_bias), row(a_log), row(skip_scale)]
    return jnp.pad(jnp.concatenate(pieces, axis=0), ((0, 6), (0, 0)))


def local(
    tokens, cotangent, lengths, doc_order, norm_gain, w_in, conv_w, conv_b, dt_bias, a_log,
    skip_scale, gate_gain, w_out,
):
    rows = tokens.shape[2]
    section, seq = lax.axis_index("section"), lax.axis_index("seq")
    size = lax.axis_size("seq")
    micro = seq % 2
    aligned = section == micro
    spot = (seq // 2) * 2 + section

    def flat(s, i):
        return s * size + i

    everywhere = ("section", "seq")
    exchange = [
        (flat(s, 2 * k + s), flat(s, 2 * k + 1 - s)) for k in range(size // 2) for s in range(2)
    ]

    def to_chain(array):
        given = lax.dynamic_index_in_dim(array[:, 0], 1 - section, 0, keepdims=False)
        own = lax.dynamic_index_in_dim(array[:, 0], section, 0, keepdims=False)
        return pick(aligned, own, lax.ppermute(given, everywhere, exchange))

    turned = w_in[0].T
    shard_conv = jnp.pad(turned[DI:], ((0, 8), (0, 0)))
    width = turned.shape[1]
    rows_out = w_out.shape[1]
    pieces = [w_out[0, :, k * width : (k + 1) * width] for k in range(D // width)]
    shard_rest = jnp.concatenate([turned[:DI]] + pieces, axis=0)

    def join_conv(blocks):
        whole_rows = jnp.concatenate([block[: CONVCH + 32] for block in blocks], axis=1)
        return whole_rows[:CONVCH], jnp.pad(whole_rows[CONVCH:], ((0, 96), (0, 0)))

    def join_rest(blocks):
        gate = jnp.concatenate([block[:DI] for block in blocks], axis=1)
        back = [
            jnp.concatenate(
                [block[at : at + rows_out] for at in range(DI, block.shape[0], rows_out)], axis=1
            )
            for block in blocks
        ]
        return gate, jnp.concatenate(back, axis=0)

    w_conv, w_step, w_gate, w_back = [[None, None] for _ in range(4)]
    blocks = move_rows(shard_conv, 0)
    hidden = to_chain(tokens)
    blocks = share(blocks, 0)
    shard_conv, shard_rest, blocks, cotangent = tie(shard_conv, shard_rest, blocks, cotangent)
    w_conv[0], w_step[0] = join_conv(blocks)
    moved_rest = move_rows(shard_rest, 0)

    top_grad = to_chain(cotangent)

    table = parameter_table(
        norm_gain, conv_w[0], conv_b, dt_bias, a_log, skip_scale, gate_gain
    )
    other = lax.ppermute(table, "section", SWAP)
    low = section == 0
    tables = [pick(low, table, other), pick(low, other, table)]
    spread = spread_matrix()

    stream_lengths = lax.dynamic_index_in_dim(lengths[:, 0], micro, 0, keepdims=False)
    stream_order = lax.dynamic_index_in_dim(doc_order[:, 0], micro, 0, keepdims=False)
    col_padded, col, lab = labels(stream_lengths, stream_order, spot * rows, rows)
    follow = [(flat(0, i), flat(1, i)) for i in range(size)] + [
        (flat(1, i), flat(0, i + 2)) for i in range(size - 2)
    ]
    precede = [(b, a) for a, b in follow]

    def to_holders(array, layer):
        return tuple(
            lax.ppermute(
                array,
                everywhere,
                [
                    (flat(s, 2 * k + m), flat(layer, 2 * k + s))
                    for k in range(size // 2)
                    for s in range(2)
                ],
            )
            for m in range(2)
        )

    def held(first, second):
        stacked = jnp.stack([pick(low, first[m], second[m]) for m in range(2)])
        return stacked[None, :, None]

    kept = []
    results = []
    for layer in range(2):
        par = tables[layer]
        if layer == 1:
            w_conv[1], w_step[1] = join_conv(second_conv)
        wide = hidden.astype(f32)
        scale = lax.rsqrt(jnp.mean(wide * wide, axis=1, keepdims=True) + epsilon)
        u = (wide * scale * par[NORM : NORM + 1, :D]).astype(bf16)
        rc = nt(u, w_conv[layer]).astype(bf16)
        e = nt(u, w_step[layer])
        halo = lax.ppermute(rc[rows - 16 :], everywhere, follow)
        q, ds, dt, cum, total, lin, pack = conv_forward(
            rc, halo, e, col, par, spread
        )
        def beside_first(_, shards, *arrays):
            following = move_rows(shards, 1) if layer == 0 else ()
            return intra_forward(*arrays, spread), following

        def beside_second(following, moved, u):
            gate, back = join_rest(share(moved, layer))
            return nt(u, gate), (gate, back, following)

        inc, ((y0, _), (z, (w_gate[layer], w_back[layer], following))) = chain_scan(
            pack,
            False,
            [
                ((shard_conv, q, dt, cum, col, lab, lin, par), beside_first),
                ((moved_rest, u), beside_second),
            ],
        )
        if layer == 0:
            inc, following, shard_rest, top_grad = tie(inc, following, shard_rest, top_grad)
            second_conv = share(following, 1)
            moved_rest = move_rows(shard_rest, 1)
        y, v, out = gate_forward(
            y0, z, q, total, col, inc, par, w_back[layer], hidden, spread
        )
        kept.append((hidden, scale, u, rc, e, halo, q, ds, dt, cum, total, lin, pack, inc, z, y, v))
        results.append(out)
        hidden = out

    def columns(a, b):
        return lax.dot_general(a, b, (((0,), (0,)), ((), ())), preferred_element_type=f32)

    parts = lax.axis_size("fsdp")

    def half_of(array, half):
        width = array.shape[1] // 2
        return lax.dynamic_slice_in_dim(array, half * width, width, axis=1)

    def by_part(array):
        width = D // parts
        return jnp.stack([array[:, k * width : (k + 1) * width] for k in range(parts)])

    def early_grads(u, dz, v, grad):
        def make(half):
            for_in = by_part(columns(half_of(dz, half), u))
            for_out = columns(v, half_of(grad, half)).reshape(parts, -1, D // 2)
            step = D // parts
            pieces = [for_out[:, :, at : at + step] for at in range(0, D // 2, step)]
            return jnp.concatenate([for_in] + pieces, axis=1)

        return make

    def late_grads(u, dr):
        return lambda half: by_part(columns(half_of(dr, half), u))

    grad = top_grad
    early = [None, None]
    late = [None, None]
    pieces = [None, None]
    acts = [None, None]
    grads = [None, None]
    for layer in (1, 0):
        par = tables[layer]
        hidden, scale, u, rc, e, halo, q, ds, dt, cum, total, lin, pack, inc, z, y, v = kept[layer]
        dy, dz, dgain, back = gate_backward(
            grad, w_back[layer], y, z, par, q, total, col, pack, spread
        )
        extra = ()
        if layer == 0:
            back, early[1], late[1] = tie(back, early[1], late[1])
            extra = late[1]
        given = early_grads(u, dz, v, grad)(1 - section).astype(bf16)

        def first(_, extra, given, *arrays):
            if layer == 0:
                extra = halve(extra, 1)
            got = lax.ppermute(given, "section", SWAP)
            return (intra_backward(*arrays, spread), extra, got), None

        def second(_, u, dz, v, grad):
            return (nn(dz, w_gate[layer]), early_grads(u, dz, v, grad)(section)), None

        outg, ((((dx, dbc, hs), extra, got), _), ((du, kept_half), _)) = chain_scan(
            back,
            True,
            [
                ((extra, given, q, dt, cum, total, col, lab, lin, inc, dy, y, par), first),
                ((u, dz, v, grad), second),
            ],
        )
        summed = (kept_half + got.astype(f32)).astype(bf16)
        early[layer] = row_sum(summed)
        if layer == 0:
            outg, extra, holding = tie(outg, extra, holding)
            upper = halve(jnp.concatenate([early[1], extra], axis=0), 2)
            grads[1] = to_holders(holding, 1)
        else:
            outg, results = tie(outg, results)
            acts = [to_holders(results[k], k) for k in range(2)]
        dr, de, tail, front, dw, dh = conv_backward(
            outg, inc, q, ds, dt, total, col_padded, e, rc, halo, dy, dx, dbc, hs, par, spread
        )
        if layer == 1:
            front, early[1] = tie(front, early[1])
            early[1] = halve(early[1], 1)
        returned = lax.ppermute(front, everywhere, precede)
        if layer == 0:
            returned, pieces[1], upper = tie(returned, pieces[1], upper)
            upper = halve(upper, 4) if size > 4 else upper
        dr = lax.dynamic_update_slice(dr, (tail + returned).astype(bf16), (rows - 8, 0))
        given = late_grads(u, dr)(1 - section).astype(bf16)
        given, dr, de = tie(given, dr, de)
        got = lax.ppermute(given, "section", SWAP)
        summed = (late_grads(u, dr)(section) + got.astype(f32)).astype(bf16)
        if layer == 0:
            summed, early[0], grads[1] = tie(summed, early[0], grads[1])
            early[0] = halve(early[0], 1)
        late[layer] = row_sum(summed)
        du = du + nn(dr, w_conv[layer]) + nn(de, w_step[layer])
        wide = hidden.astype(f32)
        normed = wide * scale
        dn = du * par[NORM : NORM + 1, :D]
        dnorm = jnp.sum(du * normed, axis=0)
        dhidden = scale * (dn - normed * jnp.mean(dn * normed, axis=1, keepdims=True))
        grad_e = columns(de, u)[:H].reshape(H // 2, 2 * D)
        grad = (grad.astype(f32) + dhidden).astype(bf16)
        if layer == 1:
            grad, acts = tie(grad, acts)
            holding = grad
        else:
            grads[0] = to_holders(grad, 0)
        pieces[layer] = (dw, dnorm, dgain, dh, grad_e)

    def table_of(dw, dnorm, dgain, dh, grad_e):
        return jnp.concatenate(
            [
                dw[: CONV + 1],
                jnp.pad(dnorm, (0, CONVCH - D))[None],
                jnp.pad(dgain, ((0, 0), (0, CONVCH - DI))),
                jnp.pad(dh[0:3], ((0, 0), (0, CONVCH - 128))),
                jnp.pad(grad_e, ((0, 0), (0, CONVCH - 2 * D))),
            ],
            axis=0,
        )

    steps = exchanges()
    small = [table_of(*pieces[layer]) for layer in range(2)]
    mine = pick(low, small[0], small[1]) + lax.ppermute(pick(low, small[1], small[0]), "section", SWAP)
    mine = exchange_sum(mine, steps[0])
    late[0], early[0], mine, grads[0], upper = tie(late[0], early[0], mine, grads[0], upper)
    far = distances()
    late[0] = halve(late[0], 1)
    mine = exchange_sum(mine, steps[1])
    late[0], mine = tie(late[0], mine)
    for distance in far[3:]:
        upper = halve(upper, distance)
    for distance in far[1:]:
        late[0] = halve(late[0], distance)
        early[0] = halve(early[0], distance)
    for step in steps[2:]:
        mine = exchange_sum(mine, step)
    for distance in reversed(far[1:]):
        late[0] = rejoin(late[0], distance)
        early[0] = rejoin(early[0], distance)
        upper = rejoin(upper, distance)
    late[0] = rejoin(late[0], 1)
    early[0] = rejoin(early[0], 1)
    split_at = early[0].shape[0] // 2
    early[1], late[1] = rejoin(upper[:split_at], 1), rejoin(upper[split_at:], 1)
    early_got = lax.ppermute(pick(low, early[1], early[0]), "section", SWAP)
    late_got = lax.ppermute(pick(low, late[1], late[0]), "section", SWAP)
    early_own, late_own = pick(low, early[0], early[1]), pick(low, late[0], late[1])
    grad_e = mine[SKIP + 1 :, : 2 * D].reshape(H, D)
    grad_e = lax.dynamic_slice_in_dim(grad_e, lax.axis_index("fsdp") * width, width, axis=1)
    shard_in, shard_out = place(early_own, early_got, late_own, late_got, grad_e, rows_out)
    return (
        held(*acts),
        held(*grads),
        mine[NORM : NORM + 1, :D],
        shard_in,
        mine[None, :CONV],
        mine[TAP_BIAS : TAP_BIAS + 1],
        mine[STEP_BIAS : STEP_BIAS + 1, :H],
        mine[BASE_RATE : BASE_RATE + 1, :H],
        mine[SKIP : SKIP + 1, :H],
        mine[GAIN : GAIN + 1, :DI],
        shard_out,
    )


def solution(mesh):
    in_specs = (
        P(None, "fsdp", "seq", None),
        P(None, "fsdp", "seq", None),
        P(None, "fsdp", None),
        P(None, "fsdp", None),
        P("section", None),
        P("section", "fsdp", None),
        P("section", None, None),
        P("section", None),
        P("section", None),
        P("section", None),
        P("section", None),
        P("section", None),
        P("section", "fsdp", None),
    )
    out_specs = (
        P("section", None, "fsdp", "seq", None),
        P("section", None, "fsdp", "seq", None),
        P("section", None),
        P("section", "fsdp", None),
        P("section", None, None),
        P("section", None),
        P("section", None),
        P("section", None),
        P("section", None),
        P("section", None),
        P("section", "fsdp", None),
    )
    return jax.shard_map(local, mesh=mesh, in_specs=in_specs, out_specs=out_specs, check_vma=False)
```

```python
import jax
import jax.numpy as jnp
from jax import lax
from jax.experimental import pallas as pl
from jax.experimental.pallas import tpu as pltpu
from jax.sharding import PartitionSpec as P

D = 768
DI = 1536
H = 24
P_SIZE = 64
STATE = 128
CONV = 4
CONVCH = 1792
Q = 128
HALF = DI // 2
PACK = STATE + 16
PACK_WIDE = STATE + 8
TAP_BIAS, NORM, GAIN, STEP_BIAS, BASE_RATE, SKIP = 4, 5, 6, 7, 8, 9
TABLE = (16, CONVCH)
SWAP = ((0, 1), (1, 0))

f32 = jnp.float32
bf16 = jnp.bfloat16
epsilon = 1e-05
masked = -1e30


def nn(a, b):
    return lax.dot_general(a, b, (((1,), (0,)), ((), ())), preferred_element_type=f32)


def nt(a, b):
    return lax.dot_general(a, b, (((1,), (1,)), ((), ())), preferred_element_type=f32)


def tn(a, b):
    return nn(a.astype(f32).T.astype(bf16), b)


def split(v):
    high = v.astype(bf16)
    return high, (v - high.astype(f32)).astype(bf16)


def expand(v, spread):
    return nn(jnp.concatenate(split(v), axis=1), spread)


def expand_row(v, spread):
    return expand(jnp.broadcast_to(v, (8, v.shape[1])), spread)[0:1]


def head_sum(v, spread):
    high, low = split(v)
    return nt(high, spread[0:128]) + nt(low, spread[0:128])


def tri_sum(tri, v):
    high, rest = split(v)
    middle, low = split(v - high.astype(f32))
    return nn(tri, high) + nn(tri, middle) + nn(tri, low)


def iota(shape, dim):
    return lax.broadcasted_iota(jnp.int32, shape, dim)


def spread_matrix():
    return (iota((256, DI), 1) // P_SIZE == iota((256, DI), 0) % 128).astype(bf16)


def two_heads(tile):
    left = iota(tile.shape, 1) < P_SIZE
    zero = jnp.zeros_like(tile)
    return jnp.concatenate([jnp.where(left, tile, zero), jnp.where(left, zero, tile)], axis=0)


def product(a, a_low, b, b_low):
    both = jnp.concatenate([b, b_low], axis=0)
    return nn(jnp.concatenate([a, a], axis=1), both) + nn(a_low, b)


def decay_rows(decay):
    high, low = split(decay)
    row = iota((16, decay.shape[1]), 0)
    both = jnp.where(row == 0, high.astype(f32), jnp.where(row == 1, low.astype(f32), 0.0))
    return both.astype(bf16)


def label_kernel(doc_ref, table_ref, col_ref, lab_ref):
    rows = col_ref.shape[0]
    base = doc_ref[8]
    ends = []
    end = 0
    for k in range(4):
        end = end + doc_ref[doc_ref[4 + k]]
        ends.append(end)

    def label(position):
        found = jnp.zeros(position.shape, jnp.int32)
        for bound in ends:
            found = found + (position >= bound).astype(jnp.int32)
        return jnp.where(position < 0, -1, found)

    def columns(row, lane):
        here = label(base + row)
        block = (row // Q) * Q
        other = jnp.where(
            lane < 3,
            row - 1 - lane,
            jnp.where(lane == 3, block - 1, jnp.where(lane == 4, block + Q - 1, jnp.where(lane == 5, -1, rows - 1))),
        )
        same = (label(base + other) == here).astype(f32)
        return jnp.where(lane == 7, here.astype(f32), same)

    lane = iota((rows + 16, 128), 1)
    row = iota((rows + 16, 128), 0) - 8
    whole_table = columns(jnp.clip(row, 0, rows - 1), lane)
    table_ref[...] = jnp.where((row >= 0) & (row < rows), whole_table, 0.0)
    col_ref[...] = columns(iota((rows, 128), 0), iota((rows, 128), 1))
    lab_ref[...] = label(base + iota((8, rows), 1)).astype(f32)


def head_row(par_ref, k):
    return jnp.where(iota((1, 128), 1) < H, par_ref[k : k + 1, 0:128], 0.0)


def rates(par_ref):
    return jnp.where(iota((1, 128), 1) < H, -jnp.exp(par_ref[BASE_RATE : BASE_RATE + 1, 0:128]), 0.0)


def skip_row(par_ref, spread):
    return expand_row(head_row(par_ref, SKIP), spread)


def conv_kernel(
    section_ref, rc_ref, before_ref, halo_ref, e_ref, col_ref, par_ref, sp_ref,
    q_ref, ds_ref, dt_ref, cum_ref, all_ref, lin_ref, kept_ref, given_ref, state_ref, row_ref,
):
    step = pl.program_id(0)

    @pl.when(step == 0)
    def _():
        state_ref[...] = jnp.zeros_like(state_ref)
        row_ref[0:1, :] = jnp.zeros((1, 128), f32)
        row_ref[1:2, :] = jnp.ones((1, 128), f32)

    spread = sp_ref[...]
    tri = (iota((Q, Q), 0) >= iota((Q, Q), 1)).astype(bf16)
    col = col_ref[...]
    dt = jax.nn.softplus(e_ref[...] + head_row(par_ref, STEP_BIAS))
    cum = tri_sum(tri, dt * rates(par_ref))
    dt_ref[...] = dt
    cum_ref[...] = cum
    all_ref[...] = cum + row_ref[0:1, :]
    for j in range(CONVCH // 128):
        lanes = slice(j * 128, (j + 1) * 128)
        before = jnp.where(step == 0, halo_ref[:, lanes], before_ref[:, lanes])
        window = jnp.concatenate([before, rc_ref[:, lanes]], axis=0).astype(f32)
        pre = par_ref[TAP_BIAS : TAP_BIAS + 1, lanes] + par_ref[3:4, lanes] * window[16:]
        for d in range(1, CONV):
            pre = pre + par_ref[3 - d : 4 - d, lanes] * window[16 - d : 16 + Q - d] * col[:, d - 1 : d]
        gate = jax.nn.sigmoid(pre)
        out = pre * gate
        q_ref[:, lanes] = out
        ds_ref[:, lanes] = (gate + out * (1.0 - gate)).astype(bf16)
    end = cum[Q - 1 : Q, :]
    weight = dt * jnp.exp(end - cum) * col[:, 4:5]
    scaled, scaled_low = split(q_ref[:, 0:DI] * expand(weight, spread))
    b_rows, b_low = split(q_ref[:, DI : DI + STATE].T)
    state = state_ref[...]
    lin_ref[0, 0:STATE], lin_ref[0, STATE:] = split(state)
    fade = jnp.exp(end) * col[Q - 1 : Q, 3:4]
    state = state * expand_row(fade, spread) + product(b_rows, b_low, scaled, scaled_low)
    state_ref[...] = state
    decay = row_ref[1:2, :] * fade
    row_ref[0:1, :] = row_ref[0:1, :] + end
    row_ref[1:2, :] = decay

    @pl.when(step == pl.num_programs(0) - 1)
    def _():
        wide = expand_row(decay, spread)
        low = section_ref[0] == 0

        def place_half(half, rows, decays):
            ours = low if half == 0 else jnp.logical_not(low)

            @pl.when(ours)
            def _():
                kept_ref[0:STATE, :] = rows
                kept_ref[STATE:, :] = decays

            @pl.when(jnp.logical_not(ours))
            def _():
                given_ref[0:STATE, :] = rows
                given_ref[STATE:, :] = decays

        for half in range(2):
            lanes = slice(half * HALF, (half + 1) * HALF)
            place_half(half, state[:, lanes], jnp.broadcast_to(wide[:, lanes], (8, HALF)))


def intra_kernel(q_ref, dt_ref, cum_ref, col_ref, lab_ref, lin_ref, par_ref, sp_ref, y_ref):
    spread = sp_ref[...]
    col = col_ref[...]
    cum = cum_ref[...]
    cum_t = cum.T
    x = q_ref[:, 0:DI]
    b_rows, b_low = split(q_ref[:, DI : DI + STATE])
    c_rows, c_low = split(q_ref[:, DI + STATE :])
    x_dt, x_low = split(x * expand(dt_ref[...], spread))
    scores = nt(c_rows, b_rows) + (nt(c_rows, b_low) + nt(c_low, b_rows))
    same = (col[:, 7:8] == lab_ref[0:1, :]) & (iota((Q, Q), 0) >= iota((Q, Q), 1))
    shut = jnp.where(same, 0.0, masked)
    reach = expand(jnp.exp(cum) * col[:, 3:4], spread)
    base = product(c_rows, c_low, lin_ref[0, 0:STATE], lin_ref[0, STATE:]) * reach + skip_row(par_ref, spread) * x
    for j in range(H // 2):
        lanes = slice(j * 128, (j + 1) * 128)
        mixing, mixing_low = split(
            jnp.concatenate(
                [
                    jnp.exp(cum[:, h : h + 1] - cum_t[h : h + 1, :] + shut) * scores
                    for h in (2 * j, 2 * j + 1)
                ],
                axis=1,
            )
        )
        pair = two_heads(x_dt[:, lanes])
        y_ref[:, lanes] = (
            base[:, lanes]
            + nn(mixing, pair)
            + (nn(mixing_low, pair) + nn(mixing, two_heads(x_low[:, lanes])))
        )


def gate_kernel(
    y0_ref, z_ref, c_ref, all_ref, col_ref, inc_ref, par_ref, w_ref, x_ref, sp_ref,
    y_ref, v_ref, out_ref,
):
    reach = jnp.exp(all_ref[...]) * col_ref[:, 5:6]
    y = y0_ref[...] + expand(reach, sp_ref[...]) * product(
        *split(c_ref[...]), *split(inc_ref[...])
    )
    y_ref[...] = y
    z = z_ref[...]
    gated = y * (z * jax.nn.sigmoid(z))
    scale = lax.rsqrt(jnp.mean(gated * gated, axis=1, keepdims=True) + epsilon)
    v = (gated * scale * par_ref[GAIN : GAIN + 1, 0:DI]).astype(bf16)
    v_ref[...] = v
    out_ref[...] = (x_ref[...].astype(f32) + nn(v, w_ref[...])).astype(bf16)


def gate_back_kernel(
    section_ref, g_ref, w_ref, y_ref, z_ref, par_ref, c_ref, all_ref, col_ref, kept_ref, given_ref, sp_ref,
    dy_ref, dz_ref, dgain_ref, to_keep_ref, to_give_ref, total_ref,
):
    step = pl.program_id(0)
    dv = nt(g_ref[...], w_ref[...])
    y = y_ref[...]
    z = z_ref[...]
    gate = jax.nn.sigmoid(z)
    silu = z * gate
    gated = y * silu
    scale = lax.rsqrt(jnp.mean(gated * gated, axis=1, keepdims=True) + epsilon)
    normed = gated * scale
    dn = dv * par_ref[GAIN : GAIN + 1, 0:DI]
    dgated = scale * (dn - normed * jnp.mean(dn * normed, axis=1, keepdims=True))
    dz_ref[...] = (dgated * y * (gate + silu * (1.0 - gate))).astype(bf16)
    dy = (dgated * silu).astype(bf16)
    dy_ref[...] = dy
    reach = jnp.exp(all_ref[...]) * col_ref[:, 5:6]
    reached = (dy.astype(f32) * expand(reach, sp_ref[...])).astype(bf16)
    part = tn(c_ref[...], reached)
    gain_part = jnp.sum(dv * normed, axis=0, keepdims=True)

    @pl.when(step == 0)
    def _():
        total_ref[...] = part
        dgain_ref[...] = gain_part

    @pl.when(step > 0)
    def _():
        total_ref[...] += part
        dgain_ref[...] += gain_part

    @pl.when(step == pl.num_programs(0) - 1)
    def _():
        low = section_ref[0] == 0
        left, right = total_ref[:, 0:HALF], total_ref[:, HALF:]
        to_keep_ref[0:STATE, :] = jnp.where(low, left, right).astype(bf16)
        to_give_ref[0:STATE, :] = jnp.where(low, right, left).astype(bf16)
        to_keep_ref[STATE:, :] = decay_rows(kept_ref[STATE : STATE + 1, :])
        to_give_ref[STATE:, :] = decay_rows(given_ref[STATE : STATE + 1, :])


def four_heads(tile, pair):
    lane = iota(tile.shape, 1)
    first = (lane < 128) if pair else ((lane // P_SIZE) % 2 == 0)
    zero = jnp.zeros_like(tile)
    return jnp.concatenate([jnp.where(first, tile, zero), jnp.where(first, zero, tile)], axis=0)


def intra_back_kernel(
    q_ref, dt_ref, cum_ref, all_ref, col_ref, lab_ref, lin_ref, inc_ref, dy_ref, y_ref, par_ref, sp_ref,
    dx_ref, dbc_ref, hs_ref, carry_ref,
):
    @pl.when(pl.program_id(0) == 0)
    def _():
        carry_ref[...] = jnp.zeros_like(carry_ref)

    spread = sp_ref[...]
    col = col_ref[...]
    cum = cum_ref[...]
    cum_t = cum.T
    x = q_ref[:, 0:DI]
    b_rows, b_low = split(q_ref[:, DI : DI + STATE])
    c_rows, c_low = split(q_ref[:, DI + STATE :])
    dy = dy_ref[...]
    dy32 = dy.astype(f32)
    x_wide = x * expand(dt_ref[...], spread)
    x_dt = x_wide.astype(bf16)
    end = cum[Q - 1 : Q, :]
    leave = expand(jnp.exp(end - cum) * col[:, 4:5], spread)
    carry = carry_ref[...]
    carry_high, carry_low = split(carry)
    base = product(b_rows, b_low, carry_high, carry_low) * leave
    scores = nt(b_rows, c_rows) + (nt(b_low, c_rows) + nt(b_rows, c_low))
    same = (col[:, 7:8] == lab_ref[0:1, :]) & (iota((Q, Q), 1) >= iota((Q, Q), 0))
    shut = jnp.where(same, 0.0, masked)
    dscores = jnp.zeros((Q, Q), f32)
    for g in range(H // 4):
        wide = slice(g * 256, (g + 1) * 256)
        grads = nt(four_heads(x_dt[:, wide], False), four_heads(dy[:, wide], True))
        for k in range(2):
            lanes = slice(g * 256 + k * 128, g * 256 + (k + 1) * 128)
            mixing = []
            for m in range(2):
                h = 4 * g + 2 * k + m
                kernel = jnp.exp(cum_t[h : h + 1, :] - cum[:, h : h + 1] + shut)
                mixing.append(kernel * scores)
                dscores = dscores + grads[m * Q : (m + 1) * Q, k * Q : (k + 1) * Q] * kernel
            mixed = nn(
                jnp.concatenate(split(jnp.concatenate(mixing, axis=1)), axis=0),
                two_heads(dy[:, lanes]),
            )
            dx_ref[:, lanes] = base[:, lanes] + (mixed[:Q] + mixed[Q:])
    dx = dx_ref[...]
    near, near_low = split(dy32 * expand(jnp.exp(cum) * col[:, 3:4], spread))
    offset = jnp.exp(all_ref[0:1, :] - cum[0:1, :]) * jnp.max(
        col[:, 5:6], axis=0, keepdims=True
    )
    entered = (
        lin_ref[0, 0:STATE].astype(f32)
        + lin_ref[0, STATE:].astype(f32)
        + expand_row(offset, spread) * inc_ref[...]
    )
    entered, entered_low = split(entered)
    low = dscores.astype(bf16)
    left = (x_wide * leave).astype(bf16)
    dbc_ref[:, 0:STATE] = nn(low, c_rows) + nt(left, carry_high)
    dbc_ref[:, STATE:] = (
        nn(dscores.T.astype(bf16), b_rows) + nt(near, entered) + nt(near, entered_low)
    )
    hs_ref[:, 0:128] = head_sum(
        dy32 * (y_ref[...] - skip_row(par_ref, spread) * x) - x_wide * dx, spread
    )
    hs_ref[:, 128:] = nt((x * dx).astype(bf16), spread[0:128])
    step = jnp.exp(end) * col[Q - 1 : Q, 3:4]
    c_rows, c_low = split(q_ref[:, DI + STATE :].T)
    carry_ref[...] = carry * expand_row(step, spread) + product(c_rows, c_low, near, near_low)


def conv_back_kernel(
    outg_ref, inc_ref, q_ref, ds_ref, dt_ref, all_ref, col_ref, e_ref, rc_ref, before_ref, halo_ref,
    dy_ref, dx_ref, dbc_ref, hs_ref, par_ref, sp_ref,
    dr_ref, de_ref, tail_ref, back_ref, dw_ref, dh_ref, pre_ref, sum_ref, row_ref, skip_ref,
):
    count = dt_ref.shape[0] // Q
    step = pl.program_id(0)
    spread = sp_ref[...]
    last = all_ref[count * Q - 1 : count * Q, :]

    @pl.when(step == 0)
    def _():
        pre_ref[0:8, :] = jnp.zeros((8, CONVCH), f32)
        pre_ref[8 + count * Q :, :] = jnp.zeros((8, CONVCH), f32)
        row_ref[...] = jnp.zeros_like(row_ref)
        skip_ref[...] = jnp.zeros_like(skip_ref)

    @pl.when(step < count)
    def _():
        start = pl.multiple_of(step * Q, Q)
        rows = pl.ds(start, Q)
        moved = pl.ds(pl.multiple_of(start + 8, 8), Q)
        outg = outg_ref[...]
        dt = dt_ref[rows, :]
        x = q_ref[:, 0:DI]
        dy = dy_ref[...].astype(f32)
        wide_dt = expand(dt, spread)
        leave = expand(jnp.exp(last - all_ref[rows, :]) * col_ref[moved, 6:7], spread)
        dx_far = leave * nn(q_ref[:, DI : DI + STATE].astype(bf16), outg)
        dx = dx_ref[...] + dx_far
        db = dbc_ref[rows, 0:STATE] + nt((x * wide_dt * leave).astype(bf16), outg)
        far = head_sum(x * dx_far, spread)
        row_ref[0:1, :] = row_ref[0:1, :] + jnp.sum(dt * far, axis=0, keepdims=True)
        sum_ref[rows, 0:128] = hs_ref[rows, 0:128] - dt * far
        sum_ref[rows, 128:] = hs_ref[rows, 128:] + far
        skip_ref[0:1, :] = skip_ref[0:1, :] + jnp.sum(x * dy, axis=0, keepdims=True)
        skip = skip_row(par_ref, spread)
        pre_ref[moved, 0:DI] = (wide_dt * dx + skip * dy) * ds_ref[:, 0:DI].astype(f32)
        pre_ref[moved, DI : DI + STATE] = db * ds_ref[:, DI : DI + STATE].astype(f32)
        pre_ref[moved, DI + STATE :] = dbc_ref[rows, STATE:] * ds_ref[:, DI + STATE :].astype(f32)

    @pl.when(step == count)
    def _():
        kept = jnp.exp(last) * col_ref[7 + count * Q : 8 + count * Q, 5:6]
        both = jnp.sum(outg_ref[...].astype(f32) * inc_ref[...], axis=0, keepdims=True)
        row_ref[0:1, :] = (
            row_ref[0:1, :] + kept * head_sum(jnp.broadcast_to(both, (8, DI)), spread)[0:1]
        )
        row_ref[3:4, :] = head_sum(skip_ref[...], spread)[0:1]
        dw_ref[...] = jnp.zeros_like(dw_ref)

    @pl.when(step >= count)
    def _():
        c = 2 * count - 1 - step
        start = pl.multiple_of(c * Q, Q)
        rows = pl.ds(start, Q)
        rate = rates(par_ref)
        tri = (iota((Q, Q), 0) <= iota((Q, Q), 1)).astype(bf16)
        sums = tri_sum(tri, sum_ref[rows, 0:128])
        dlog = sums + row_ref[0:1, :]
        row_ref[0:1, :] = row_ref[0:1, :] + sums[0:1]
        ddt = rate * dlog + sum_ref[rows, 128:]
        de = ddt * jax.nn.sigmoid(e_ref[rows, :] + head_row(par_ref, STEP_BIAS))
        de_ref[...] = jnp.where(iota((Q, 128), 1) < H, de, 0.0).astype(bf16)
        row_ref[1:2, :] = row_ref[1:2, :] + jnp.sum(de, axis=0, keepdims=True)
        row_ref[2:3, :] = row_ref[2:3, :] + rate * jnp.sum(
            dlog * dt_ref[rows, :], axis=0, keepdims=True
        )
        around = pl.ds(pl.multiple_of(start + 8, 8), Q + 8)
        col = col_ref[around, :]
        row = iota((8, 128), 0)
        for j in range(CONVCH // 128):
            lanes = slice(j * 128, (j + 1) * 128)
            taps = [par_ref[3 - d : 4 - d, lanes] for d in range(CONV)]
            ahead = pre_ref[around, lanes]
            before = jnp.where(c == 0, halo_ref[:, lanes], before_ref[:, lanes])
            window = jnp.concatenate([before, rc_ref[:, lanes]], axis=0).astype(f32)
            here = ahead[0:Q]
            found = [None] * (CONV + 1)
            found[CONV] = jnp.sum(here, axis=0, keepdims=True)
            found[3] = jnp.sum(here * window[16:], axis=0, keepdims=True)
            grad = taps[0] * here
            for d in range(1, CONV):
                same = ahead * col[:, d - 1 : d]
                found[3 - d] = jnp.sum(
                    same[0:Q] * window[16 - d : 16 + Q - d], axis=0, keepdims=True
                )
                grad = grad + taps[d] * same[d : d + Q]
            dr_ref[:, lanes] = grad.astype(bf16)
            tail_ref[:, lanes] = jnp.where(step == count, grad[Q - 8 :], tail_ref[:, lanes])
            stacked = jnp.zeros((8, 128), f32)
            for k in range(CONV + 1):
                stacked = jnp.where(row == k, found[k], stacked)
            dw_ref[:, lanes] = dw_ref[:, lanes] + stacked

    @pl.when(step == 2 * count - 1)
    def _():
        dh_ref[0:3, :] = row_ref[1:4, :]
        for j in range(CONVCH // 128):
            lanes = slice(j * 128, (j + 1) * 128)
            front = pre_ref[0:16, lanes]
            early = jnp.zeros((8, 128), f32)
            for d in range(1, CONV):
                tap = par_ref[3 - d : 4 - d, lanes]
                early = early + tap * (front * col_ref[0:16, d - 1 : d])[d : d + 8]
            back_ref[:, lanes] = early


def params(steps):
    return pltpu.CompilerParams(
        dimension_semantics=("arbitrary",) * steps, vmem_limit_bytes=48 * 1024 * 1024
    )


def shape(*dims, dtype=f32):
    return jax.ShapeDtypeStruct(dims, dtype)


def whole(array):
    rank = len(array.shape)
    return pl.BlockSpec(array.shape, lambda *_: (0,) * rank)


def conv_forward(rc, halo, e, col, par, spread):
    rows = rc.shape[0]

    def by_row(width):
        return pl.BlockSpec((Q, width), lambda i: (i, 0))

    outs = (
        shape(rows, CONVCH),
        shape(rows, CONVCH, dtype=bf16),
        shape(rows, 128),
        shape(rows, 128),
        shape(rows, 128),
        shape(rows // Q, 2 * STATE, DI, dtype=bf16),
        shape(PACK_WIDE, HALF),
        shape(PACK_WIDE, HALF),
    )
    section = lax.axis_index("section").astype(jnp.int32)[None]
    return pl.pallas_call(
        conv_kernel,
        grid=(rows // Q,),
        in_specs=[
            pl.BlockSpec(memory_space=pltpu.SMEM),
            by_row(CONVCH),
            pl.BlockSpec((16, CONVCH), lambda i: (jnp.maximum(i * (Q // 16) - 1, 0), 0)),
            whole(halo),
            by_row(128),
            by_row(128),
            whole(par),
            whole(spread),
        ],
        out_specs=(
            by_row(CONVCH),
            by_row(CONVCH),
            by_row(128),
            by_row(128),
            by_row(128),
            pl.BlockSpec((1, 2 * STATE, DI), lambda i: (i, 0, 0)),
            whole(outs[-2]),
            whole(outs[-1]),
        ),
        out_shape=outs,
        scratch_shapes=[pltpu.VMEM((STATE, DI), f32), pltpu.VMEM((8, 128), f32)],
        compiler_params=params(1),
    )(section, rc, rc, halo, e, col, par, spread)


def intra_forward(q, dt, cum, col, lab, lin, par, spread):
    rows = q.shape[0]

    def by_row(width):
        return pl.BlockSpec((Q, width), lambda i: (i, 0))

    return pl.pallas_call(
        intra_kernel,
        grid=(rows // Q,),
        in_specs=[
            by_row(CONVCH),
            by_row(128),
            by_row(128),
            by_row(128),
            pl.BlockSpec((8, Q), lambda i: (0, i)),
            pl.BlockSpec((1, 2 * STATE, DI), lambda i: (i, 0, 0)),
            whole(par),
            whole(spread),
        ],
        out_specs=by_row(DI),
        out_shape=shape(rows, DI),
        compiler_params=params(1),
        cost_estimate=pl.CostEstimate(
            flops=8 * rows * Q * DI, bytes_accessed=rows * 20000, transcendentals=rows * Q * H
        ),
    )(q, dt, cum, col, lab, lin, par, spread)


def gate_forward(y0, z, q, total, col, inc, par, w_out, hidden, spread):
    rows = y0.shape[0]
    size = 256

    def by_row(width):
        return pl.BlockSpec((size, width), lambda i: (i, 0))

    return pl.pallas_call(
        gate_kernel,
        grid=(rows // size,),
        in_specs=[
            by_row(DI),
            by_row(DI),
            pl.BlockSpec((size, STATE), lambda i: (i, (DI + STATE) // STATE)),
            by_row(128),
            by_row(128),
            whole(inc),
            whole(par),
            whole(w_out),
            by_row(D),
            whole(spread),
        ],
        out_specs=(by_row(DI), by_row(DI), by_row(D)),
        out_shape=(shape(rows, DI), shape(rows, DI, dtype=bf16), shape(rows, D, dtype=bf16)),
        compiler_params=params(1),
    )(y0, z, q, total, col, inc, par, w_out, hidden, spread)


def gate_backward(grad, w_out, y, z, par, q, total, col, kept, given, spread):
    rows = y.shape[0]
    size = 256

    def by_row(width):
        return pl.BlockSpec((size, width), lambda i: (i, 0))

    outs = (
        shape(rows, DI, dtype=bf16),
        shape(rows, DI, dtype=bf16),
        shape(1, DI),
        shape(PACK, HALF, dtype=bf16),
        shape(PACK, HALF, dtype=bf16),
    )
    section = lax.axis_index("section").astype(jnp.int32)[None]
    return pl.pallas_call(
        gate_back_kernel,
        grid=(rows // size,),
        in_specs=[
            pl.BlockSpec(memory_space=pltpu.SMEM),
            by_row(D),
            whole(w_out),
            by_row(DI),
            by_row(DI),
            whole(par),
            pl.BlockSpec((size, STATE), lambda i: (i, (DI + STATE) // STATE)),
            by_row(128),
            by_row(128),
            whole(kept),
            whole(given),
            whole(spread),
        ],
        out_specs=(by_row(DI), by_row(DI), whole(outs[2]), whole(outs[3]), whole(outs[4])),
        out_shape=outs,
        scratch_shapes=[pltpu.VMEM((STATE, DI), f32)],
        compiler_params=params(1),
    )(section, grad, w_out, y, z, par, q, total, col, kept, given, spread)


def intra_backward(q, dt, cum, total, col, lab, lin, inc, dy, y, par, spread):
    rows = q.shape[0]
    top = rows // Q - 1

    def by_row(width):
        return pl.BlockSpec((Q, width), lambda i: (top - i, 0))

    return pl.pallas_call(
        intra_back_kernel,
        grid=(rows // Q,),
        in_specs=[
            by_row(CONVCH),
            by_row(128),
            by_row(128),
            by_row(128),
            by_row(128),
            pl.BlockSpec((8, Q), lambda i: (0, top - i)),
            pl.BlockSpec((1, 2 * STATE, DI), lambda i: (top - i, 0, 0)),
            whole(inc),
            by_row(DI),
            by_row(DI),
            whole(par),
            whole(spread),
        ],
        out_specs=(by_row(DI), by_row(256), by_row(256)),
        out_shape=(shape(rows, DI), shape(rows, 256), shape(rows, 256)),
        scratch_shapes=[pltpu.VMEM((STATE, DI), f32)],
        compiler_params=params(1),
        cost_estimate=pl.CostEstimate(
            flops=30 * rows * Q * DI, bytes_accessed=rows * 30000, transcendentals=rows * Q * H
        ),
    )(q, dt, cum, total, col, lab, lin, inc, dy, y, par, spread)


def conv_backward(outg, inc, q, ds, dt, total, col, e, rc, halo, dy, dx, dbc, hs, par, spread):
    rows = q.shape[0]
    count = rows // Q

    def first(width):
        return pl.BlockSpec((Q, width), lambda i: (jnp.minimum(i, count - 1), 0))

    def back(i):
        return jnp.minimum(2 * count - 1 - i, count - 1)

    def second(width):
        return pl.BlockSpec((Q, width), lambda i: (back(i), 0))

    outs = (
        shape(rows, CONVCH, dtype=bf16),
        shape(rows, 128, dtype=bf16),
        shape(8, CONVCH),
        shape(8, CONVCH),
        shape(8, CONVCH),
        shape(8, 128),
    )
    return pl.pallas_call(
        conv_back_kernel,
        grid=(2 * count,),
        in_specs=[
            whole(outg),
            whole(inc),
            first(CONVCH),
            first(CONVCH),
            whole(dt),
            whole(total),
            whole(col),
            whole(e),
            second(CONVCH),
            pl.BlockSpec((16, CONVCH), lambda i: (jnp.maximum(back(i) * (Q // 16) - 1, 0), 0)),
            whole(halo),
            first(DI),
            first(DI),
            whole(dbc),
            whole(hs),
            whole(par),
            whole(spread),
        ],
        out_specs=(second(CONVCH), second(128)) + tuple(whole(out) for out in outs[2:]),
        out_shape=outs,
        scratch_shapes=[
            pltpu.VMEM((rows + 16, CONVCH), f32),
            pltpu.VMEM((rows, 256), f32),
            pltpu.VMEM((8, 128), f32),
            pltpu.VMEM((8, DI), f32),
        ],
        compiler_params=params(1),
    )(outg, inc, q, ds, dt, total, col, e, rc, rc, halo, dy, dx, dbc, hs, par, spread)


def pick(first, a, b):
    return jnp.where(first, a, b)


def unpack(block):
    wide = block.astype(f32)
    if block.dtype == f32:
        return wide[STATE : STATE + 1], wide[:STATE]
    return wide[STATE : STATE + 1] + wide[STATE + 1 : STATE + 2], wide[:STATE]


def pack_up(pair, kind):
    if kind == f32:
        decay = jnp.broadcast_to(pair[0], (8, HALF))
        return jnp.concatenate([pair[1], decay], axis=0)
    return jnp.concatenate([pair[1].astype(bf16), decay_rows(pair[0])], axis=0)


def combine(earlier, later):
    return (earlier[0] * later[0], later[0] * earlier[1] + later[1])


def chain_scan(kept, given, reverse, beside):
    section = lax.axis_index("section")
    size = lax.axis_size("seq")
    got = lax.ppermute(given, "section", SWAP)
    leads = (section == 1) if reverse else (section == 0)
    lead = unpack(pick(leads, kept, got))
    follow = unpack(pick(leads, got, kept))
    reached = combine(lead, follow)
    before = None
    distance = 2
    results = []
    other = None
    while distance < size:
        route = [(i, i + distance) for i in range(size - distance)]
        if reverse:
            route = [(b, a) for a, b in route]
        sent = pack_up(reached, kept.dtype)
        if beside:
            arrays, work = beside.pop(0)
            sent, arrays = tie(sent, arrays)
            arrived = lax.ppermute(sent, "seq", route)
            needed, other = work(other, *arrays)
            arrived, needed = tie(arrived, needed)
            results.append((needed, other))
        else:
            arrived = lax.ppermute(sent, "seq", route)
        arrived = unpack(arrived)
        before = arrived if before is None else combine(arrived, before)
        reached = combine(arrived, reached)
        distance *= 2
    first = before[1]
    second = lead[1] + lead[0] * first
    own = pick(leads, first, second).astype(kept.dtype)
    other = lax.ppermute(pick(leads, second, first).astype(kept.dtype), "section", SWAP)
    low = section == 0
    incoming = jnp.concatenate([pick(low, own, other), pick(low, other, own)], axis=1)
    return incoming, results


def move_rows(shard):
    parts = lax.axis_size("fsdp")
    blocks = [shard]
    for shift in range(1, parts):
        blocks.append(lax.ppermute(shard, "fsdp", [(i, (i + shift) % parts) for i in range(parts)]))
    return blocks


def share(blocks):
    section, row = lax.axis_index("section"), lax.axis_index("fsdp")
    parts = lax.axis_size("fsdp")
    others = [lax.ppermute(block, "section", SWAP) for block in blocks]
    layers = []
    for layer in range(2):
        held = [pick(section == layer, a, b) for a, b in zip(blocks, others)]
        if parts == 2:
            low = row == 0
            layers.append([pick(low, held[0], held[1]), pick(low, held[1], held[0])])
            continue
        ordered = []
        for k in range(parts):
            block = held[0]
            for shift in range(1, parts):
                block = pick((row - shift) % parts == k, held[shift], block)
            ordered.append(block)
        layers.append(ordered)
    return layers


def row_sum(summed):
    row, parts = lax.axis_index("fsdp"), lax.axis_size("fsdp")
    if parts == 2:
        kept = lax.dynamic_index_in_dim(summed, row, 0, keepdims=False)
        given = lax.dynamic_index_in_dim(summed, 1 - row, 0, keepdims=False)
        got = lax.ppermute(given, "fsdp", SWAP)
        return (kept.astype(f32) + got.astype(f32)).astype(bf16)
    return lax.psum_scatter(summed, "fsdp", scatter_dimension=0, tiled=False)


def halve(array, distance):
    size, bit = lax.axis_size("seq"), (lax.axis_index("seq") // distance) % 2
    halves = array.reshape(2, -1, array.shape[1])
    kept = lax.dynamic_index_in_dim(halves, bit, 0, keepdims=False)
    given = lax.dynamic_index_in_dim(halves, 1 - bit, 0, keepdims=False)
    got = lax.ppermute(given, "seq", [(i, i ^ distance) for i in range(size)])
    return (kept.astype(f32) + got.astype(f32)).astype(bf16)


def rejoin(array, distance):
    size, low = lax.axis_size("seq"), (lax.axis_index("seq") // distance) % 2 == 0
    got = lax.ppermute(array, "seq", [(i, i ^ distance) for i in range(size)])
    return jnp.concatenate([pick(low, array, got), pick(low, got, array)], axis=0)


def distances():
    found = [1]
    while 2 * found[-1] < lax.axis_size("seq"):
        found.append(2 * found[-1])
    return found


def exchanges():
    found = []
    for axis in ("fsdp", "seq"):
        distance = 1
        while distance < lax.axis_size(axis):
            found.append((axis, distance))
            distance *= 2
    return found


def exchange_sum(array, step):
    axis, distance = step
    partners = [(i, i ^ distance) for i in range(lax.axis_size(axis))]
    return array + lax.ppermute(array, axis, partners)


def tie(*arrays):
    return lax.optimization_barrier(arrays)


def place_kernel(
    section_ref, early_ref, early_got_ref, late_ref, late_got_ref, e_ref, in_ref, out_ref
):
    low = section_ref[0] == 0
    conv_rows = CONVCH // 2
    for half in range(2):
        own = low if half == 0 else jnp.logical_not(low)

        def block(ref, got_ref, start, count):
            rows = slice(start, start + count)
            return jnp.where(own, ref[rows, :], got_ref[rows, :]).astype(f32)

        in_ref[half * HALF : (half + 1) * HALF, :] = block(early_ref, early_got_ref, 0, HALF)
        lanes = slice(half * (D // 2), (half + 1) * (D // 2))
        out_ref[:, lanes] = block(early_ref, early_got_ref, HALF, HALF)
        at = DI + half * conv_rows
        in_ref[at : at + conv_rows, :] = block(late_ref, late_got_ref, 0, conv_rows)
    in_ref[DI + CONVCH :, :] = e_ref[...]


def place(early, early_got, late, late_got, e, rows_out):
    section = lax.axis_index("section")
    width = early.shape[1]
    if rows_out == HALF:
        vmem = pl.BlockSpec(memory_space=pltpu.VMEM)
        w_in, w_out = pl.pallas_call(
            place_kernel,
            in_specs=[pl.BlockSpec(memory_space=pltpu.SMEM)] + [vmem] * 5,
            out_shape=(shape(DI + CONVCH + H, width), shape(rows_out, D)),
            compiler_params=params(0),
        )(section.astype(jnp.int32)[None], early, early_got, late, late_got, e)
        return w_in.T[None], w_out[None]
    gates, convs, backs = [], [], []
    for half in range(2):
        array = pick(section == half, early, early_got).astype(f32)
        gates.append(array[:HALF])
        backs += [array[at : at + rows_out] for at in range(HALF, 2 * HALF, rows_out)]
        convs.append(pick(section == half, late, late_got).astype(f32))
    w_in = jnp.concatenate(gates + convs + [e], axis=0)
    return w_in.T[None], jnp.concatenate(backs, axis=1)[None]


def labels(lengths, order, base, rows):
    documents = jnp.concatenate([lengths, order, base[None]]).astype(jnp.int32)
    return pl.pallas_call(
        label_kernel,
        in_specs=[pl.BlockSpec(memory_space=pltpu.SMEM)],
        out_shape=(shape(rows + 16, 128), shape(rows, 128), shape(8, rows)),
        compiler_params=params(0),
    )(documents)


def parameter_table(norm_gain, conv_w, conv_b, dt_bias, a_log, skip_scale, gate_gain):
    def row(array):
        return jnp.pad(array, ((0, 0), (0, CONVCH - array.shape[1])))

    pieces = [conv_w, conv_b, row(norm_gain), row(gate_gain), row(dt_bias), row(a_log), row(skip_scale)]
    return jnp.pad(jnp.concatenate(pieces, axis=0), ((0, 6), (0, 0)))


def local(
    tokens, cotangent, lengths, doc_order, norm_gain, w_in, conv_w, conv_b, dt_bias, a_log,
    skip_scale, gate_gain, w_out,
):
    rows = tokens.shape[2]
    section, seq = lax.axis_index("section"), lax.axis_index("seq")
    size = lax.axis_size("seq")
    micro = seq % 2
    aligned = section == micro
    spot = (seq // 2) * 2 + section

    def flat(s, i):
        return s * size + i

    everywhere = ("section", "seq")
    exchange = [
        (flat(s, 2 * k + s), flat(s, 2 * k + 1 - s)) for k in range(size // 2) for s in range(2)
    ]

    def to_chain(array):
        given = lax.dynamic_index_in_dim(array[:, 0], 1 - section, 0, keepdims=False)
        own = lax.dynamic_index_in_dim(array[:, 0], section, 0, keepdims=False)
        return pick(aligned, own, lax.ppermute(given, everywhere, exchange))

    turned = w_in[0].T
    shard_conv = jnp.pad(turned[DI:], ((0, 8), (0, 0)))
    width = turned.shape[1]
    rows_out = w_out.shape[1]
    pieces = [w_out[0, :, k * width : (k + 1) * width] for k in range(D // width)]
    shard_rest = jnp.concatenate([turned[:DI]] + pieces, axis=0)

    def join_conv(blocks):
        whole_rows = jnp.concatenate([block[: CONVCH + 32] for block in blocks], axis=1)
        return whole_rows[:CONVCH], jnp.pad(whole_rows[CONVCH:], ((0, 96), (0, 0)))

    def join_rest(blocks):
        gate = jnp.concatenate([block[:DI] for block in blocks], axis=1)
        back = [
            jnp.concatenate(
                [block[at : at + rows_out] for at in range(DI, block.shape[0], rows_out)], axis=1
            )
            for block in blocks
        ]
        return gate, jnp.concatenate(back, axis=0)

    blocks = move_rows(shard_conv)
    hidden = to_chain(tokens)
    top_grad = to_chain(cotangent)
    blocks, hidden, shard_rest, top_grad = tie(blocks, hidden, shard_rest, top_grad)
    joined = [join_conv(layer) for layer in share(blocks)]
    w_conv, w_step = [[pair[k] for pair in joined] for k in range(2)]
    moved_rest = move_rows(shard_rest)
    w_gate, w_back = [None, None], [None, None]

    table = parameter_table(
        norm_gain, conv_w[0], conv_b, dt_bias, a_log, skip_scale, gate_gain
    )
    other = lax.ppermute(table, "section", SWAP)
    low = section == 0
    tables = [pick(low, table, other), pick(low, other, table)]
    spread = spread_matrix()

    stream_lengths = lax.dynamic_index_in_dim(lengths[:, 0], micro, 0, keepdims=False)
    stream_order = lax.dynamic_index_in_dim(doc_order[:, 0], micro, 0, keepdims=False)
    col_padded, col, lab = labels(stream_lengths, stream_order, spot * rows, rows)
    follow = [(flat(0, i), flat(1, i)) for i in range(size)] + [
        (flat(1, i), flat(0, i + 2)) for i in range(size - 2)
    ]
    precede = [(b, a) for a, b in follow]

    routes = [[], []]
    for k in range(size // 2):
        for s in range(2):
            for m in range(2):
                for way in range(2):
                    routes[way].append((flat(s, 2 * k + m), flat((m + way) % 2, 2 * k + s)))

    def to_holders(first, second):
        even = micro == 0
        return (
            lax.ppermute(pick(even, first, second), everywhere, routes[0]),
            lax.ppermute(pick(even, second, first), everywhere, routes[1]),
        )

    def held(one, two):
        return jnp.stack([pick(low, one, two), pick(low, two, one)])[None, :, None]

    kept = []
    results = []
    for layer in range(2):
        par = tables[layer]
        wide = hidden.astype(f32)
        scale = lax.rsqrt(jnp.mean(wide * wide, axis=1, keepdims=True) + epsilon)
        u = (wide * scale * par[NORM : NORM + 1, :D]).astype(bf16)
        rc = nt(u, w_conv[layer]).astype(bf16)
        e = nt(u, w_step[layer])
        halo = lax.ppermute(rc[rows - 16 :], everywhere, follow)
        q, ds, dt, cum, total, lin, to_keep, to_give = conv_forward(
            rc, halo, e, col, par, spread
        )
        def beside_first(_, *arrays):
            return intra_forward(*arrays, spread), None

        def beside_second(_, u, moved):
            if layer == 0:
                for k, blocks in enumerate(share(moved)):
                    w_gate[k], w_back[k] = join_rest(blocks)
            return nt(u, w_gate[layer]), None

        inc, ((y0, _), (z, _)) = chain_scan(
            to_keep,
            to_give,
            False,
            [
                ((q, dt, cum, col, lab, lin, par), beside_first),
                ((u, moved_rest if layer == 0 else ()), beside_second),
            ],
        )
        y, v, out = gate_forward(
            y0, z, q, total, col, inc, par, w_back[layer], hidden, spread
        )
        kept.append((hidden, scale, u, rc, e, halo, q, ds, dt, cum, total, lin, to_keep, to_give, inc, z, y, v))
        results.append(out)
        hidden = out

    def columns(a, b):
        return lax.dot_general(a, b, (((0,), (0,)), ((), ())), preferred_element_type=f32)

    parts = lax.axis_size("fsdp")

    def half_of(array, half):
        width = array.shape[1] // 2
        return lax.dynamic_slice_in_dim(array, half * width, width, axis=1)

    def by_part(array):
        width = D // parts
        return jnp.stack([array[:, k * width : (k + 1) * width] for k in range(parts)])

    def early_grads(u, dz, v, grad):
        def make(half):
            for_in = by_part(columns(half_of(dz, half), u))
            for_out = columns(v, half_of(grad, half)).reshape(parts, -1, D // 2)
            step = D // parts
            pieces = [for_out[:, :, at : at + step] for at in range(0, D // 2, step)]
            return jnp.concatenate([for_in] + pieces, axis=1)

        return make

    def late_grads(u, dr):
        return lambda half: by_part(columns(half_of(dr, half), u))

    grad = top_grad
    early = [None, None]
    late = [None, None]
    pieces = [None, None]
    acts = [None, None]
    grads = [None, None]
    for layer in (1, 0):
        par = tables[layer]
        hidden, scale, u, rc, e, halo, q, ds, dt, cum, total, lin, to_keep, to_give, inc, z, y, v = kept[layer]
        dy, dz, dgain, back, back_given = gate_backward(
            grad, w_back[layer], y, z, par, q, total, col, to_keep, to_give, spread
        )
        extra = ()
        if layer == 0:
            back, back_given, early[1], late[1], acts = tie(back, back_given, early[1], late[1], acts)
            extra = (early[1], late[1])
        given = early_grads(u, dz, v, grad)(1 - section).astype(bf16)

        def first(_, extra, given, *arrays):
            if layer == 0:
                extra = (halve(extra[0], 1), halve(extra[1], 1))
            got = lax.ppermute(given, "section", SWAP)
            return (intra_backward(*arrays, spread), extra, got), None

        def second(_, u, dz, v, grad):
            return (nn(dz, w_gate[layer]), early_grads(u, dz, v, grad)(section)), None

        outg, ((((dx, dbc, hs), extra, got), _), ((du, kept_half), _)) = chain_scan(
            back,
            back_given,
            True,
            [
                ((extra, given, q, dt, cum, total, col, lab, lin, inc, dy, y, par), first),
                ((u, dz, v, grad), second),
            ],
        )
        summed = (kept_half + got.astype(f32)).astype(bf16)
        early[layer] = row_sum(summed)
        if layer == 0:
            outg, extra = tie(outg, extra)
        else:
            outg, results = tie(outg, results)
            acts = to_holders(*results)
        dr, de, tail, front, dw, dh = conv_backward(
            outg, inc, q, ds, dt, total, col_padded, e, rc, halo, dy, dx, dbc, hs, par, spread
        )
        if layer == 1:
            front, early[1] = tie(front, early[1])
        else:
            front, extra = tie(front, extra)
            upper = halve(jnp.concatenate(extra, axis=0), 2)
        returned = lax.ppermute(front, everywhere, precede)
        dr = lax.dynamic_update_slice(dr, (tail + returned).astype(bf16), (rows - 8, 0))
        given = late_grads(u, dr)(1 - section).astype(bf16)
        given, dr, de = tie(given, dr, de)
        got = lax.ppermute(given, "section", SWAP)
        summed = (late_grads(u, dr)(section) + got.astype(f32)).astype(bf16)
        if layer == 0:
            summed, early[0], upper, pieces[1] = tie(summed, early[0], upper, pieces[1])
            early[0] = halve(early[0], 1)
            upper = halve(upper, 4) if size > 4 else upper
        summed, dr, de = tie(summed, dr, de)
        late[layer] = row_sum(summed)
        du = du + nn(dr, w_conv[layer]) + nn(de, w_step[layer])
        wide = hidden.astype(f32)
        normed = wide * scale
        dn = du * par[NORM : NORM + 1, :D]
        dnorm = jnp.sum(du * normed, axis=0)
        dhidden = scale * (dn - normed * jnp.mean(dn * normed, axis=1, keepdims=True))
        grad_e = columns(de, u)[:H].reshape(H // 2, 2 * D)
        grad = (grad.astype(f32) + dhidden).astype(bf16)
        if layer == 1:
            holding = grad
        else:
            grads = to_holders(grad, holding)
        pieces[layer] = (dw, dnorm, dgain, dh, grad_e)

    def table_of(dw, dnorm, dgain, dh, grad_e):
        return jnp.concatenate(
            [
                dw[: CONV + 1],
                jnp.pad(dnorm, (0, CONVCH - D))[None],
                jnp.pad(dgain, ((0, 0), (0, CONVCH - DI))),
                jnp.pad(dh[0:3], ((0, 0), (0, CONVCH - 128))),
                jnp.pad(grad_e, ((0, 0), (0, CONVCH - 2 * D))),
            ],
            axis=0,
        )

    steps = exchanges()
    small = [table_of(*pieces[layer]) for layer in range(2)]
    mine = pick(low, small[0], small[1]) + lax.ppermute(pick(low, small[1], small[0]), "section", SWAP)
    mine = exchange_sum(mine, steps[0])
    late[0], early[0], mine, upper = tie(late[0], early[0], mine, upper)
    far = distances()
    for distance in far[3:]:
        upper = halve(upper, distance)
    late[0] = halve(late[0], 1)
    mine = exchange_sum(mine, steps[1])
    for distance in far[1:]:
        early[0] = halve(early[0], distance)
    for distance in reversed(far[1:]):
        upper = rejoin(upper, distance)
    for distance in far[1:2]:
        late[0] = halve(late[0], distance)
    late[0], early[0], mine, grads, upper = tie(late[0], early[0], mine, grads, upper)
    early[1], late[1] = rejoin(upper[:HALF], 1), rejoin(upper[HALF:], 1)
    for distance in far[2:]:
        late[0] = halve(late[0], distance)
    for step in steps[2:]:
        mine = exchange_sum(mine, step)
    for distance in reversed(far[1:]):
        early[0] = rejoin(early[0], distance)
    for distance in reversed(far[2:]):
        late[0] = rejoin(late[0], distance)
    late[0], early[0], mine, upper = tie(late[0], early[0], mine, (early[1], late[1]))
    early[1], late[1] = upper
    early[0] = rejoin(early[0], 1)
    for distance in far[1:2]:
        late[0] = rejoin(late[0], distance)
    late[0] = rejoin(late[0], 1)
    early_got = lax.ppermute(pick(low, early[1], early[0]), "section", SWAP)
    late_got = lax.ppermute(pick(low, late[1], late[0]), "section", SWAP)
    early_own, late_own = pick(low, early[0], early[1]), pick(low, late[0], late[1])
    grad_e = mine[SKIP + 1 :, : 2 * D].reshape(H, D)
    grad_e = lax.dynamic_slice_in_dim(grad_e, lax.axis_index("fsdp") * width, width, axis=1)
    shard_in, shard_out = place(early_own, early_got, late_own, late_got, grad_e, rows_out)
    return (
        held(*acts),
        held(*grads),
        mine[NORM : NORM + 1, :D],
        shard_in,
        mine[None, :CONV],
        mine[TAP_BIAS : TAP_BIAS + 1],
        mine[STEP_BIAS : STEP_BIAS + 1, :H],
        mine[BASE_RATE : BASE_RATE + 1, :H],
        mine[SKIP : SKIP + 1, :H],
        mine[GAIN : GAIN + 1, :DI],
        shard_out,
    )


def solution(mesh):
    in_specs = (
        P(None, "fsdp", "seq", None),
        P(None, "fsdp", "seq", None),
        P(None, "fsdp", None),
        P(None, "fsdp", None),
        P("section", None),
        P("section", "fsdp", None),
        P("section", None, None),
        P("section", None),
        P("section", None),
        P("section", None),
        P("section", None),
        P("section", None),
        P("section", "fsdp", None),
    )
    out_specs = (
        P("section", None, "fsdp", "seq", None),
        P("section", None, "fsdp", "seq", None),
        P("section", None),
        P("section", "fsdp", None),
        P("section", None, None),
        P("section", None),
        P("section", None),
        P("section", None),
        P("section", None),
        P("section", None),
        P("section", "fsdp", None),
    )
    return jax.shard_map(local, mesh=mesh, in_specs=in_specs, out_specs=out_specs, check_vma=False)
```

```python
import jax
import jax.numpy as jnp
from jax import lax
from jax.experimental import pallas as pl
from jax.experimental.pallas import tpu as pltpu
from jax.sharding import PartitionSpec as P

D = 768
DI = 1536
H = 24
P_SIZE = 64
STATE = 128
CONV = 4
CONVCH = 1792
Q = 128
HALF = DI // 2
PACK = STATE + 16
PACK_WIDE = STATE + 8
TAP_BIAS, NORM, GAIN, STEP_BIAS, BASE_RATE, SKIP = 4, 5, 6, 7, 8, 9
TABLE = (16, CONVCH)
SWAP = ((0, 1), (1, 0))

f32 = jnp.float32
bf16 = jnp.bfloat16
epsilon = 1e-05
masked = -1e30


def nn(a, b):
    return lax.dot_general(a, b, (((1,), (0,)), ((), ())), preferred_element_type=f32)


def nt(a, b):
    return lax.dot_general(a, b, (((1,), (1,)), ((), ())), preferred_element_type=f32)


def tn(a, b):
    return nn(a.astype(f32).T.astype(bf16), b)


def split(v):
    high = v.astype(bf16)
    return high, (v - high.astype(f32)).astype(bf16)


def expand(v, spread):
    return nn(jnp.concatenate(split(v), axis=1), spread)


def expand_row(v, spread):
    return expand(jnp.broadcast_to(v, (8, v.shape[1])), spread)[0:1]


def head_sum(v, spread):
    high, low = split(v)
    return nt(high, spread[0:128]) + nt(low, spread[0:128])


def tri_sum(tri, v):
    high, rest = split(v)
    middle, low = split(v - high.astype(f32))
    return nn(tri, high) + nn(tri, middle) + nn(tri, low)


def iota(shape, dim):
    return lax.broadcasted_iota(jnp.int32, shape, dim)


def spread_matrix():
    return (iota((256, DI), 1) // P_SIZE == iota((256, DI), 0) % 128).astype(bf16)


def two_heads(tile):
    left = iota(tile.shape, 1) < P_SIZE
    zero = jnp.zeros_like(tile)
    return jnp.concatenate([jnp.where(left, tile, zero), jnp.where(left, zero, tile)], axis=0)


def product(a, a_low, b, b_low):
    both = jnp.concatenate([b, b_low], axis=0)
    return nn(jnp.concatenate([a, a], axis=1), both) + nn(a_low, b)


def decay_rows(decay):
    high, low = split(decay)
    row = iota((16, decay.shape[1]), 0)
    both = jnp.where(row == 0, high.astype(f32), jnp.where(row == 1, low.astype(f32), 0.0))
    return both.astype(bf16)


def label_kernel(doc_ref, table_ref, col_ref, lab_ref):
    rows = col_ref.shape[0]
    base = doc_ref[8]
    ends = []
    end = 0
    for k in range(4):
        end = end + doc_ref[doc_ref[4 + k]]
        ends.append(end)

    def label(position):
        found = jnp.zeros(position.shape, jnp.int32)
        for bound in ends:
            found = found + (position >= bound).astype(jnp.int32)
        return jnp.where(position < 0, -1, found)

    def columns(row, lane):
        here = label(base + row)
        block = (row // Q) * Q
        other = jnp.where(
            lane < 3,
            row - 1 - lane,
            jnp.where(lane == 3, block - 1, jnp.where(lane == 4, block + Q - 1, jnp.where(lane == 5, -1, rows - 1))),
        )
        same = (label(base + other) == here).astype(f32)
        return jnp.where(lane == 7, here.astype(f32), same)

    lane = iota((rows + 16, 128), 1)
    row = iota((rows + 16, 128), 0) - 8
    whole_table = columns(jnp.clip(row, 0, rows - 1), lane)
    table_ref[...] = jnp.where((row >= 0) & (row < rows), whole_table, 0.0)
    col_ref[...] = columns(iota((rows, 128), 0), iota((rows, 128), 1))
    lab_ref[...] = label(base + iota((8, rows), 1)).astype(f32)


def head_row(par_ref, k):
    return jnp.where(iota((1, 128), 1) < H, par_ref[k : k + 1, 0:128], 0.0)


def rates(par_ref):
    return jnp.where(iota((1, 128), 1) < H, -jnp.exp(par_ref[BASE_RATE : BASE_RATE + 1, 0:128]), 0.0)


def skip_row(par_ref, spread):
    return expand_row(head_row(par_ref, SKIP), spread)


def conv_kernel(
    section_ref, rc_ref, before_ref, halo_ref, e_ref, col_ref, par_ref, sp_ref,
    q_ref, ds_ref, dt_ref, cum_ref, all_ref, lin_ref, kept_ref, given_ref, state_ref, row_ref,
):
    step = pl.program_id(0)

    @pl.when(step == 0)
    def _():
        state_ref[...] = jnp.zeros_like(state_ref)
        row_ref[0:1, :] = jnp.zeros((1, 128), f32)
        row_ref[1:2, :] = jnp.ones((1, 128), f32)

    spread = sp_ref[...]
    tri = (iota((Q, Q), 0) >= iota((Q, Q), 1)).astype(bf16)
    col = col_ref[...]
    dt = jax.nn.softplus(e_ref[...] + head_row(par_ref, STEP_BIAS))
    cum = tri_sum(tri, dt * rates(par_ref))
    dt_ref[...] = dt
    cum_ref[...] = cum
    all_ref[...] = cum + row_ref[0:1, :]
    for j in range(CONVCH // 128):
        lanes = slice(j * 128, (j + 1) * 128)
        before = jnp.where(step == 0, halo_ref[:, lanes], before_ref[:, lanes])
        window = jnp.concatenate([before, rc_ref[:, lanes]], axis=0).astype(f32)
        pre = par_ref[TAP_BIAS : TAP_BIAS + 1, lanes] + par_ref[3:4, lanes] * window[16:]
        for d in range(1, CONV):
            pre = pre + par_ref[3 - d : 4 - d, lanes] * window[16 - d : 16 + Q - d] * col[:, d - 1 : d]
        gate = jax.nn.sigmoid(pre)
        out = pre * gate
        q_ref[:, lanes] = out
        ds_ref[:, lanes] = (gate + out * (1.0 - gate)).astype(bf16)
    end = cum[Q - 1 : Q, :]
    weight = dt * jnp.exp(end - cum) * col[:, 4:5]
    scaled, scaled_low = split(q_ref[:, 0:DI] * expand(weight, spread))
    b_rows, b_low = split(q_ref[:, DI : DI + STATE].T)
    state = state_ref[...]
    lin_ref[0, 0:STATE], lin_ref[0, STATE:] = split(state)
    fade = jnp.exp(end) * col[Q - 1 : Q, 3:4]
    state = state * expand_row(fade, spread) + product(b_rows, b_low, scaled, scaled_low)
    state_ref[...] = state
    decay = row_ref[1:2, :] * fade
    row_ref[0:1, :] = row_ref[0:1, :] + end
    row_ref[1:2, :] = decay

    @pl.when(step == pl.num_programs(0) - 1)
    def _():
        wide = expand_row(decay, spread)
        low = section_ref[0] == 0

        def place_half(half, rows, decays):
            ours = low if half == 0 else jnp.logical_not(low)

            @pl.when(ours)
            def _():
                kept_ref[0:STATE, :] = rows
                kept_ref[STATE:, :] = decays

            @pl.when(jnp.logical_not(ours))
            def _():
                given_ref[0:STATE, :] = rows
                given_ref[STATE:, :] = decays

        for half in range(2):
            lanes = slice(half * HALF, (half + 1) * HALF)
            place_half(half, state[:, lanes], jnp.broadcast_to(wide[:, lanes], (8, HALF)))


def intra_kernel(q_ref, dt_ref, cum_ref, col_ref, lab_ref, lin_ref, par_ref, sp_ref, y_ref):
    spread = sp_ref[...]
    col = col_ref[...]
    cum = cum_ref[...]
    cum_t = cum.T
    x = q_ref[:, 0:DI]
    b_rows, b_low = split(q_ref[:, DI : DI + STATE])
    c_rows, c_low = split(q_ref[:, DI + STATE :])
    x_dt, x_low = split(x * expand(dt_ref[...], spread))
    scores = nt(c_rows, b_rows) + (nt(c_rows, b_low) + nt(c_low, b_rows))
    same = (col[:, 7:8] == lab_ref[0:1, :]) & (iota((Q, Q), 0) >= iota((Q, Q), 1))
    shut = jnp.where(same, 0.0, masked)
    reach = expand(jnp.exp(cum) * col[:, 3:4], spread)
    base = product(c_rows, c_low, lin_ref[0, 0:STATE], lin_ref[0, STATE:]) * reach + skip_row(par_ref, spread) * x
    for j in range(H // 2):
        lanes = slice(j * 128, (j + 1) * 128)
        mixing, mixing_low = split(
            jnp.concatenate(
                [
                    jnp.exp(cum[:, h : h + 1] - cum_t[h : h + 1, :] + shut) * scores
                    for h in (2 * j, 2 * j + 1)
                ],
                axis=1,
            )
        )
        pair = two_heads(x_dt[:, lanes])
        y_ref[:, lanes] = (
            base[:, lanes]
            + nn(mixing, pair)
            + (nn(mixing_low, pair) + nn(mixing, two_heads(x_low[:, lanes])))
        )


def gate_kernel(
    y0_ref, z_ref, c_ref, all_ref, col_ref, inc_ref, par_ref, w_ref, x_ref, sp_ref,
    y_ref, v_ref, out_ref,
):
    reach = jnp.exp(all_ref[...]) * col_ref[:, 5:6]
    y = y0_ref[...] + expand(reach, sp_ref[...]) * product(
        *split(c_ref[...]), *split(inc_ref[...])
    )
    y_ref[...] = y
    z = z_ref[...]
    gated = y * (z * jax.nn.sigmoid(z))
    scale = lax.rsqrt(jnp.mean(gated * gated, axis=1, keepdims=True) + epsilon)
    v = (gated * scale * par_ref[GAIN : GAIN + 1, 0:DI]).astype(bf16)
    v_ref[...] = v
    out_ref[...] = (x_ref[...].astype(f32) + nn(v, w_ref[...])).astype(bf16)


def gate_back_kernel(
    section_ref, g_ref, w_ref, y_ref, z_ref, par_ref, c_ref, all_ref, col_ref, kept_ref, given_ref, sp_ref,
    dy_ref, dz_ref, dgain_ref, to_keep_ref, to_give_ref, total_ref,
):
    step = pl.program_id(0)
    dv = nt(g_ref[...], w_ref[...])
    y = y_ref[...]
    z = z_ref[...]
    gate = jax.nn.sigmoid(z)
    silu = z * gate
    gated = y * silu
    scale = lax.rsqrt(jnp.mean(gated * gated, axis=1, keepdims=True) + epsilon)
    normed = gated * scale
    dn = dv * par_ref[GAIN : GAIN + 1, 0:DI]
    dgated = scale * (dn - normed * jnp.mean(dn * normed, axis=1, keepdims=True))
    dz_ref[...] = (dgated * y * (gate + silu * (1.0 - gate))).astype(bf16)
    dy = (dgated * silu).astype(bf16)
    dy_ref[...] = dy
    reach = jnp.exp(all_ref[...]) * col_ref[:, 5:6]
    reached = (dy.astype(f32) * expand(reach, sp_ref[...])).astype(bf16)
    part = tn(c_ref[...], reached)
    gain_part = jnp.sum(dv * normed, axis=0, keepdims=True)

    @pl.when(step == 0)
    def _():
        total_ref[...] = part
        dgain_ref[...] = gain_part

    @pl.when(step > 0)
    def _():
        total_ref[...] += part
        dgain_ref[...] += gain_part

    @pl.when(step == pl.num_programs(0) - 1)
    def _():
        low = section_ref[0] == 0
        left, right = total_ref[:, 0:HALF], total_ref[:, HALF:]
        to_keep_ref[0:STATE, :] = jnp.where(low, left, right).astype(bf16)
        to_give_ref[0:STATE, :] = jnp.where(low, right, left).astype(bf16)
        to_keep_ref[STATE:, :] = decay_rows(kept_ref[STATE : STATE + 1, :])
        to_give_ref[STATE:, :] = decay_rows(given_ref[STATE : STATE + 1, :])


def four_heads(tile, pair):
    lane = iota(tile.shape, 1)
    first = (lane < 128) if pair else ((lane // P_SIZE) % 2 == 0)
    zero = jnp.zeros_like(tile)
    return jnp.concatenate([jnp.where(first, tile, zero), jnp.where(first, zero, tile)], axis=0)


def intra_back_kernel(
    q_ref, dt_ref, cum_ref, all_ref, col_ref, lab_ref, lin_ref, inc_ref, dy_ref, y_ref, par_ref, sp_ref,
    dx_ref, dbc_ref, hs_ref, carry_ref,
):
    @pl.when(pl.program_id(0) == 0)
    def _():
        carry_ref[...] = jnp.zeros_like(carry_ref)

    spread = sp_ref[...]
    col = col_ref[...]
    cum = cum_ref[...]
    cum_t = cum.T
    x = q_ref[:, 0:DI]
    b_rows, b_low = split(q_ref[:, DI : DI + STATE])
    c_rows, c_low = split(q_ref[:, DI + STATE :])
    dy = dy_ref[...]
    dy32 = dy.astype(f32)
    x_wide = x * expand(dt_ref[...], spread)
    x_dt = x_wide.astype(bf16)
    end = cum[Q - 1 : Q, :]
    leave = expand(jnp.exp(end - cum) * col[:, 4:5], spread)
    carry = carry_ref[...]
    carry_high, carry_low = split(carry)
    base = product(b_rows, b_low, carry_high, carry_low) * leave
    scores = nt(b_rows, c_rows) + (nt(b_low, c_rows) + nt(b_rows, c_low))
    same = (col[:, 7:8] == lab_ref[0:1, :]) & (iota((Q, Q), 1) >= iota((Q, Q), 0))
    shut = jnp.where(same, 0.0, masked)
    dscores = jnp.zeros((Q, Q), f32)
    for g in range(H // 4):
        wide = slice(g * 256, (g + 1) * 256)
        grads = nt(four_heads(x_dt[:, wide], False), four_heads(dy[:, wide], True))
        for k in range(2):
            lanes = slice(g * 256 + k * 128, g * 256 + (k + 1) * 128)
            mixing = []
            for m in range(2):
                h = 4 * g + 2 * k + m
                kernel = jnp.exp(cum_t[h : h + 1, :] - cum[:, h : h + 1] + shut)
                mixing.append(kernel * scores)
                dscores = dscores + grads[m * Q : (m + 1) * Q, k * Q : (k + 1) * Q] * kernel
            mixed = nn(
                jnp.concatenate(split(jnp.concatenate(mixing, axis=1)), axis=0),
                two_heads(dy[:, lanes]),
            )
            dx_ref[:, lanes] = base[:, lanes] + (mixed[:Q] + mixed[Q:])
    dx = dx_ref[...]
    near, near_low = split(dy32 * expand(jnp.exp(cum) * col[:, 3:4], spread))
    offset = jnp.exp(all_ref[0:1, :] - cum[0:1, :]) * jnp.max(
        col[:, 5:6], axis=0, keepdims=True
    )
    entered = (
        lin_ref[0, 0:STATE].astype(f32)
        + lin_ref[0, STATE:].astype(f32)
        + expand_row(offset, spread) * inc_ref[...]
    )
    entered, entered_low = split(entered)
    low = dscores.astype(bf16)
    left = (x_wide * leave).astype(bf16)
    dbc_ref[:, 0:STATE] = nn(low, c_rows) + nt(left, carry_high)
    dbc_ref[:, STATE:] = (
        nn(dscores.T.astype(bf16), b_rows) + nt(near, entered) + nt(near, entered_low)
    )
    hs_ref[:, 0:128] = head_sum(
        dy32 * (y_ref[...] - skip_row(par_ref, spread) * x) - x_wide * dx, spread
    )
    hs_ref[:, 128:] = nt((x * dx).astype(bf16), spread[0:128])
    step = jnp.exp(end) * col[Q - 1 : Q, 3:4]
    c_rows, c_low = split(q_ref[:, DI + STATE :].T)
    carry_ref[...] = carry * expand_row(step, spread) + product(c_rows, c_low, near, near_low)


def conv_back_kernel(
    outg_ref, inc_ref, q_ref, ds_ref, dt_ref, all_ref, col_ref, e_ref, rc_ref, before_ref, halo_ref,
    dy_ref, dx_ref, dbc_ref, hs_ref, par_ref, sp_ref,
    dr_ref, de_ref, tail_ref, back_ref, dw_ref, dh_ref, pre_ref, sum_ref, row_ref, skip_ref,
):
    count = dt_ref.shape[0] // Q
    step = pl.program_id(0)
    spread = sp_ref[...]
    last = all_ref[count * Q - 1 : count * Q, :]

    @pl.when(step == 0)
    def _():
        pre_ref[0:8, :] = jnp.zeros((8, CONVCH), f32)
        pre_ref[8 + count * Q :, :] = jnp.zeros((8, CONVCH), f32)
        row_ref[...] = jnp.zeros_like(row_ref)
        skip_ref[...] = jnp.zeros_like(skip_ref)

    @pl.when(step < count)
    def _():
        start = pl.multiple_of(step * Q, Q)
        rows = pl.ds(start, Q)
        moved = pl.ds(pl.multiple_of(start + 8, 8), Q)
        outg = outg_ref[...]
        dt = dt_ref[rows, :]
        x = q_ref[:, 0:DI]
        dy = dy_ref[...].astype(f32)
        wide_dt = expand(dt, spread)
        leave = expand(jnp.exp(last - all_ref[rows, :]) * col_ref[moved, 6:7], spread)
        dx_far = leave * nn(q_ref[:, DI : DI + STATE].astype(bf16), outg)
        dx = dx_ref[...] + dx_far
        db = dbc_ref[rows, 0:STATE] + nt((x * wide_dt * leave).astype(bf16), outg)
        far = head_sum(x * dx_far, spread)
        row_ref[0:1, :] = row_ref[0:1, :] + jnp.sum(dt * far, axis=0, keepdims=True)
        sum_ref[rows, 0:128] = hs_ref[rows, 0:128] - dt * far
        sum_ref[rows, 128:] = hs_ref[rows, 128:] + far
        skip_ref[0:1, :] = skip_ref[0:1, :] + jnp.sum(x * dy, axis=0, keepdims=True)
        skip = skip_row(par_ref, spread)
        pre_ref[moved, 0:DI] = (wide_dt * dx + skip * dy) * ds_ref[:, 0:DI].astype(f32)
        pre_ref[moved, DI : DI + STATE] = db * ds_ref[:, DI : DI + STATE].astype(f32)
        pre_ref[moved, DI + STATE :] = dbc_ref[rows, STATE:] * ds_ref[:, DI + STATE :].astype(f32)

    @pl.when(step == count)
    def _():
        kept = jnp.exp(last) * col_ref[7 + count * Q : 8 + count * Q, 5:6]
        both = jnp.sum(outg_ref[...].astype(f32) * inc_ref[...], axis=0, keepdims=True)
        row_ref[0:1, :] = (
            row_ref[0:1, :] + kept * head_sum(jnp.broadcast_to(both, (8, DI)), spread)[0:1]
        )
        row_ref[3:4, :] = head_sum(skip_ref[...], spread)[0:1]
        dw_ref[...] = jnp.zeros_like(dw_ref)

    @pl.when(step >= count)
    def _():
        c = 2 * count - 1 - step
        start = pl.multiple_of(c * Q, Q)
        rows = pl.ds(start, Q)
        rate = rates(par_ref)
        tri = (iota((Q, Q), 0) <= iota((Q, Q), 1)).astype(bf16)
        sums = tri_sum(tri, sum_ref[rows, 0:128])
        dlog = sums + row_ref[0:1, :]
        row_ref[0:1, :] = row_ref[0:1, :] + sums[0:1]
        ddt = rate * dlog + sum_ref[rows, 128:]
        de = ddt * jax.nn.sigmoid(e_ref[rows, :] + head_row(par_ref, STEP_BIAS))
        de_ref[...] = jnp.where(iota((Q, 128), 1) < H, de, 0.0).astype(bf16)
        row_ref[1:2, :] = row_ref[1:2, :] + jnp.sum(de, axis=0, keepdims=True)
        row_ref[2:3, :] = row_ref[2:3, :] + rate * jnp.sum(
            dlog * dt_ref[rows, :], axis=0, keepdims=True
        )
        around = pl.ds(pl.multiple_of(start + 8, 8), Q + 8)
        col = col_ref[around, :]
        row = iota((8, 128), 0)
        for j in range(CONVCH // 128):
            lanes = slice(j * 128, (j + 1) * 128)
            taps = [par_ref[3 - d : 4 - d, lanes] for d in range(CONV)]
            ahead = pre_ref[around, lanes]
            before = jnp.where(c == 0, halo_ref[:, lanes], before_ref[:, lanes])
            window = jnp.concatenate([before, rc_ref[:, lanes]], axis=0).astype(f32)
            here = ahead[0:Q]
            found = [None] * (CONV + 1)
            found[CONV] = jnp.sum(here, axis=0, keepdims=True)
            found[3] = jnp.sum(here * window[16:], axis=0, keepdims=True)
            grad = taps[0] * here
            for d in range(1, CONV):
                same = ahead * col[:, d - 1 : d]
                found[3 - d] = jnp.sum(
                    same[0:Q] * window[16 - d : 16 + Q - d], axis=0, keepdims=True
                )
                grad = grad + taps[d] * same[d : d + Q]
            dr_ref[:, lanes] = grad.astype(bf16)
            tail_ref[:, lanes] = jnp.where(step == count, grad[Q - 8 :], tail_ref[:, lanes])
            stacked = jnp.zeros((8, 128), f32)
            for k in range(CONV + 1):
                stacked = jnp.where(row == k, found[k], stacked)
            dw_ref[:, lanes] = dw_ref[:, lanes] + stacked

    @pl.when(step == 2 * count - 1)
    def _():
        dh_ref[0:3, :] = row_ref[1:4, :]
        for j in range(CONVCH // 128):
            lanes = slice(j * 128, (j + 1) * 128)
            front = pre_ref[0:16, lanes]
            early = jnp.zeros((8, 128), f32)
            for d in range(1, CONV):
                tap = par_ref[3 - d : 4 - d, lanes]
                early = early + tap * (front * col_ref[0:16, d - 1 : d])[d : d + 8]
            back_ref[:, lanes] = early


def params(steps, limit=48):
    return pltpu.CompilerParams(
        dimension_semantics=("arbitrary",) * steps, vmem_limit_bytes=limit * 1024 * 1024
    )


def shape(*dims, dtype=f32):
    return jax.ShapeDtypeStruct(dims, dtype)


def whole(array):
    rank = len(array.shape)
    return pl.BlockSpec(array.shape, lambda *_: (0,) * rank)


def conv_forward(rc, halo, e, col, par, spread):
    rows = rc.shape[0]

    def by_row(width):
        return pl.BlockSpec((Q, width), lambda i: (i, 0))

    outs = (
        shape(rows, CONVCH),
        shape(rows, CONVCH, dtype=bf16),
        shape(rows, 128),
        shape(rows, 128),
        shape(rows, 128),
        shape(rows // Q, 2 * STATE, DI, dtype=bf16),
        shape(PACK_WIDE, HALF),
        shape(PACK_WIDE, HALF),
    )
    section = lax.axis_index("section").astype(jnp.int32)[None]
    return pl.pallas_call(
        conv_kernel,
        grid=(rows // Q,),
        in_specs=[
            pl.BlockSpec(memory_space=pltpu.SMEM),
            by_row(CONVCH),
            pl.BlockSpec((16, CONVCH), lambda i: (jnp.maximum(i * (Q // 16) - 1, 0), 0)),
            whole(halo),
            by_row(128),
            by_row(128),
            whole(par),
            whole(spread),
        ],
        out_specs=(
            by_row(CONVCH),
            by_row(CONVCH),
            by_row(128),
            by_row(128),
            by_row(128),
            pl.BlockSpec((1, 2 * STATE, DI), lambda i: (i, 0, 0)),
            whole(outs[-2]),
            whole(outs[-1]),
        ),
        out_shape=outs,
        scratch_shapes=[pltpu.VMEM((STATE, DI), f32), pltpu.VMEM((8, 128), f32)],
        compiler_params=params(1),
    )(section, rc, rc, halo, e, col, par, spread)


def intra_forward(q, dt, cum, col, lab, lin, par, spread):
    rows = q.shape[0]

    def by_row(width):
        return pl.BlockSpec((Q, width), lambda i: (i, 0))

    return pl.pallas_call(
        intra_kernel,
        grid=(rows // Q,),
        in_specs=[
            by_row(CONVCH),
            by_row(128),
            by_row(128),
            by_row(128),
            pl.BlockSpec((8, Q), lambda i: (0, i)),
            pl.BlockSpec((1, 2 * STATE, DI), lambda i: (i, 0, 0)),
            whole(par),
            whole(spread),
        ],
        out_specs=by_row(DI),
        out_shape=shape(rows, DI),
        compiler_params=params(1),
        cost_estimate=pl.CostEstimate(
            flops=8 * rows * Q * DI, bytes_accessed=rows * 20000, transcendentals=rows * Q * H
        ),
    )(q, dt, cum, col, lab, lin, par, spread)


def gate_forward(y0, z, q, total, col, inc, par, w_out, hidden, spread):
    rows = y0.shape[0]
    size = 256

    def by_row(width):
        return pl.BlockSpec((size, width), lambda i: (i, 0))

    return pl.pallas_call(
        gate_kernel,
        grid=(rows // size,),
        in_specs=[
            by_row(DI),
            by_row(DI),
            pl.BlockSpec((size, STATE), lambda i: (i, (DI + STATE) // STATE)),
            by_row(128),
            by_row(128),
            whole(inc),
            whole(par),
            whole(w_out),
            by_row(D),
            whole(spread),
        ],
        out_specs=(by_row(DI), by_row(DI), by_row(D)),
        out_shape=(shape(rows, DI), shape(rows, DI, dtype=bf16), shape(rows, D, dtype=bf16)),
        compiler_params=params(1, 32),
    )(y0, z, q, total, col, inc, par, w_out, hidden, spread)


def gate_backward(grad, w_out, y, z, par, q, total, col, kept, given, spread):
    rows = y.shape[0]
    size = 256

    def by_row(width):
        return pl.BlockSpec((size, width), lambda i: (i, 0))

    outs = (
        shape(rows, DI, dtype=bf16),
        shape(rows, DI, dtype=bf16),
        shape(1, DI),
        shape(PACK, HALF, dtype=bf16),
        shape(PACK, HALF, dtype=bf16),
    )
    section = lax.axis_index("section").astype(jnp.int32)[None]
    return pl.pallas_call(
        gate_back_kernel,
        grid=(rows // size,),
        in_specs=[
            pl.BlockSpec(memory_space=pltpu.SMEM),
            by_row(D),
            whole(w_out),
            by_row(DI),
            by_row(DI),
            whole(par),
            pl.BlockSpec((size, STATE), lambda i: (i, (DI + STATE) // STATE)),
            by_row(128),
            by_row(128),
            whole(kept),
            whole(given),
            whole(spread),
        ],
        out_specs=(by_row(DI), by_row(DI), whole(outs[2]), whole(outs[3]), whole(outs[4])),
        out_shape=outs,
        scratch_shapes=[pltpu.VMEM((STATE, DI), f32)],
        compiler_params=params(1, 32),
    )(section, grad, w_out, y, z, par, q, total, col, kept, given, spread)


def intra_backward(q, dt, cum, total, col, lab, lin, inc, dy, y, par, spread):
    rows = q.shape[0]
    top = rows // Q - 1

    def by_row(width):
        return pl.BlockSpec((Q, width), lambda i: (top - i, 0))

    return pl.pallas_call(
        intra_back_kernel,
        grid=(rows // Q,),
        in_specs=[
            by_row(CONVCH),
            by_row(128),
            by_row(128),
            by_row(128),
            by_row(128),
            pl.BlockSpec((8, Q), lambda i: (0, top - i)),
            pl.BlockSpec((1, 2 * STATE, DI), lambda i: (top - i, 0, 0)),
            whole(inc),
            by_row(DI),
            by_row(DI),
            whole(par),
            whole(spread),
        ],
        out_specs=(by_row(DI), by_row(256), by_row(256)),
        out_shape=(shape(rows, DI), shape(rows, 256), shape(rows, 256)),
        scratch_shapes=[pltpu.VMEM((STATE, DI), f32)],
        compiler_params=params(1),
        cost_estimate=pl.CostEstimate(
            flops=30 * rows * Q * DI, bytes_accessed=rows * 30000, transcendentals=rows * Q * H
        ),
    )(q, dt, cum, total, col, lab, lin, inc, dy, y, par, spread)


def conv_backward(outg, inc, q, ds, dt, total, col, e, rc, halo, dy, dx, dbc, hs, par, spread):
    rows = q.shape[0]
    count = rows // Q

    def first(width):
        return pl.BlockSpec((Q, width), lambda i: (jnp.minimum(i, count - 1), 0))

    def back(i):
        return jnp.minimum(2 * count - 1 - i, count - 1)

    def second(width):
        return pl.BlockSpec((Q, width), lambda i: (back(i), 0))

    outs = (
        shape(rows, CONVCH, dtype=bf16),
        shape(rows, 128, dtype=bf16),
        shape(8, CONVCH),
        shape(8, CONVCH),
        shape(8, CONVCH),
        shape(8, 128),
    )
    return pl.pallas_call(
        conv_back_kernel,
        grid=(2 * count,),
        in_specs=[
            whole(outg),
            whole(inc),
            first(CONVCH),
            first(CONVCH),
            whole(dt),
            whole(total),
            whole(col),
            whole(e),
            second(CONVCH),
            pl.BlockSpec((16, CONVCH), lambda i: (jnp.maximum(back(i) * (Q // 16) - 1, 0), 0)),
            whole(halo),
            first(DI),
            first(DI),
            whole(dbc),
            whole(hs),
            whole(par),
            whole(spread),
        ],
        out_specs=(second(CONVCH), second(128)) + tuple(whole(out) for out in outs[2:]),
        out_shape=outs,
        scratch_shapes=[
            pltpu.VMEM((rows + 16, CONVCH), f32),
            pltpu.VMEM((rows, 256), f32),
            pltpu.VMEM((8, 128), f32),
            pltpu.VMEM((8, DI), f32),
        ],
        compiler_params=params(1),
    )(outg, inc, q, ds, dt, total, col, e, rc, rc, halo, dy, dx, dbc, hs, par, spread)


def pick(first, a, b):
    return jnp.where(first, a, b)


def unpack(block):
    wide = block.astype(f32)
    if block.dtype == f32:
        return wide[STATE : STATE + 1], wide[:STATE]
    return wide[STATE : STATE + 1] + wide[STATE + 1 : STATE + 2], wide[:STATE]


def pack_up(pair, kind):
    if kind == f32:
        decay = jnp.broadcast_to(pair[0], (8, HALF))
        return jnp.concatenate([pair[1], decay], axis=0)
    return jnp.concatenate([pair[1].astype(bf16), decay_rows(pair[0])], axis=0)


def combine(earlier, later):
    return (earlier[0] * later[0], later[0] * earlier[1] + later[1])


def chain_scan(kept, given, reverse, beside):
    section = lax.axis_index("section")
    size = lax.axis_size("seq")
    got = lax.ppermute(given, "section", SWAP)
    leads = (section == 1) if reverse else (section == 0)
    lead = unpack(pick(leads, kept, got))
    follow = unpack(pick(leads, got, kept))
    reached = combine(lead, follow)
    before = None
    distance = 2
    results = []
    other = None
    while distance < size:
        route = [(i, i + distance) for i in range(size - distance)]
        if reverse:
            route = [(b, a) for a, b in route]
        sent = pack_up(reached, kept.dtype)
        if beside:
            arrays, work = beside.pop(0)
            sent, arrays = tie(sent, arrays)
            arrived = lax.ppermute(sent, "seq", route)
            needed, other = work(other, *arrays)
            arrived, needed = tie(arrived, needed)
            results.append((needed, other))
        else:
            arrived = lax.ppermute(sent, "seq", route)
        arrived = unpack(arrived)
        before = arrived if before is None else combine(arrived, before)
        reached = combine(arrived, reached)
        distance *= 2
    first = before[1]
    second = lead[1] + lead[0] * first
    own = pick(leads, first, second).astype(kept.dtype)
    other = lax.ppermute(pick(leads, second, first).astype(kept.dtype), "section", SWAP)
    low = section == 0
    incoming = jnp.concatenate([pick(low, own, other), pick(low, other, own)], axis=1)
    return incoming, results


def move_rows(shard):
    parts = lax.axis_size("fsdp")
    blocks = [shard]
    for shift in range(1, parts):
        blocks.append(lax.ppermute(shard, "fsdp", [(i, (i + shift) % parts) for i in range(parts)]))
    return blocks


def share(blocks):
    section, row = lax.axis_index("section"), lax.axis_index("fsdp")
    parts = lax.axis_size("fsdp")
    others = [lax.ppermute(block, "section", SWAP) for block in blocks]
    layers = []
    for layer in range(2):
        held = [pick(section == layer, a, b) for a, b in zip(blocks, others)]
        if parts == 2:
            low = row == 0
            layers.append([pick(low, held[0], held[1]), pick(low, held[1], held[0])])
            continue
        ordered = []
        for k in range(parts):
            block = held[0]
            for shift in range(1, parts):
                block = pick((row - shift) % parts == k, held[shift], block)
            ordered.append(block)
        layers.append(ordered)
    return layers


def row_sum(summed):
    row, parts = lax.axis_index("fsdp"), lax.axis_size("fsdp")
    if parts == 2:
        kept = lax.dynamic_index_in_dim(summed, row, 0, keepdims=False)
        given = lax.dynamic_index_in_dim(summed, 1 - row, 0, keepdims=False)
        got = lax.ppermute(given, "fsdp", SWAP)
        return (kept.astype(f32) + got.astype(f32)).astype(bf16)
    return lax.psum_scatter(summed, "fsdp", scatter_dimension=0, tiled=False)


def halve(array, distance):
    size, bit = lax.axis_size("seq"), (lax.axis_index("seq") // distance) % 2
    halves = array.reshape(2, -1, array.shape[1])
    kept = lax.dynamic_index_in_dim(halves, bit, 0, keepdims=False)
    given = lax.dynamic_index_in_dim(halves, 1 - bit, 0, keepdims=False)
    got = lax.ppermute(given, "seq", [(i, i ^ distance) for i in range(size)])
    return (kept.astype(f32) + got.astype(f32)).astype(bf16)


def rejoin(array, distance):
    size, low = lax.axis_size("seq"), (lax.axis_index("seq") // distance) % 2 == 0
    got = lax.ppermute(array, "seq", [(i, i ^ distance) for i in range(size)])
    return jnp.concatenate([pick(low, array, got), pick(low, got, array)], axis=0)


def distances():
    found = [1]
    while 2 * found[-1] < lax.axis_size("seq"):
        found.append(2 * found[-1])
    return found


def exchanges():
    found = []
    for axis in ("fsdp", "seq"):
        distance = 1
        while distance < lax.axis_size(axis):
            found.append((axis, distance))
            distance *= 2
    return found


def exchange_sum(array, step):
    axis, distance = step
    partners = [(i, i ^ distance) for i in range(lax.axis_size(axis))]
    return array + lax.ppermute(array, axis, partners)


def tie(*arrays):
    return lax.optimization_barrier(arrays)


def place_kernel(
    section_ref, early_ref, early_got_ref, late_ref, late_got_ref, e_ref, in_ref, out_ref
):
    low = section_ref[0] == 0
    conv_rows = CONVCH // 2
    for half in range(2):
        own = low if half == 0 else jnp.logical_not(low)

        def block(ref, got_ref, start, count):
            rows = slice(start, start + count)
            return jnp.where(own, ref[rows, :], got_ref[rows, :]).astype(f32)

        in_ref[half * HALF : (half + 1) * HALF, :] = block(early_ref, early_got_ref, 0, HALF)
        lanes = slice(half * (D // 2), (half + 1) * (D // 2))
        out_ref[:, lanes] = block(early_ref, early_got_ref, HALF, HALF)
        at = DI + half * conv_rows
        in_ref[at : at + conv_rows, :] = block(late_ref, late_got_ref, 0, conv_rows)
    in_ref[DI + CONVCH :, :] = e_ref[...]


def place(early, early_got, late, late_got, e, rows_out):
    section = lax.axis_index("section")
    width = early.shape[1]
    if rows_out == HALF:
        vmem = pl.BlockSpec(memory_space=pltpu.VMEM)
        w_in, w_out = pl.pallas_call(
            place_kernel,
            in_specs=[pl.BlockSpec(memory_space=pltpu.SMEM)] + [vmem] * 5,
            out_shape=(shape(DI + CONVCH + H, width), shape(rows_out, D)),
            compiler_params=params(0),
        )(section.astype(jnp.int32)[None], early, early_got, late, late_got, e)
        return w_in.T[None], w_out[None]
    gates, convs, backs = [], [], []
    for half in range(2):
        array = pick(section == half, early, early_got).astype(f32)
        gates.append(array[:HALF])
        backs += [array[at : at + rows_out] for at in range(HALF, 2 * HALF, rows_out)]
        convs.append(pick(section == half, late, late_got).astype(f32))
    w_in = jnp.concatenate(gates + convs + [e], axis=0)
    return w_in.T[None], jnp.concatenate(backs, axis=1)[None]


def labels(lengths, order, base, rows):
    documents = jnp.concatenate([lengths, order, base[None]]).astype(jnp.int32)
    return pl.pallas_call(
        label_kernel,
        in_specs=[pl.BlockSpec(memory_space=pltpu.SMEM)],
        out_shape=(shape(rows + 16, 128), shape(rows, 128), shape(8, rows)),
        compiler_params=params(0),
    )(documents)


def parameter_table(norm_gain, conv_w, conv_b, dt_bias, a_log, skip_scale, gate_gain):
    def row(array):
        return jnp.pad(array, ((0, 0), (0, CONVCH - array.shape[1])))

    pieces = [conv_w, conv_b, row(norm_gain), row(gate_gain), row(dt_bias), row(a_log), row(skip_scale)]
    return jnp.pad(jnp.concatenate(pieces, axis=0), ((0, 6), (0, 0)))


def local(
    tokens, cotangent, lengths, doc_order, norm_gain, w_in, conv_w, conv_b, dt_bias, a_log,
    skip_scale, gate_gain, w_out,
):
    rows = tokens.shape[2]
    section, seq = lax.axis_index("section"), lax.axis_index("seq")
    size = lax.axis_size("seq")
    micro = seq % 2
    aligned = section == micro
    spot = (seq // 2) * 2 + section

    def flat(s, i):
        return s * size + i

    everywhere = ("section", "seq")
    exchange = [
        (flat(s, 2 * k + s), flat(s, 2 * k + 1 - s)) for k in range(size // 2) for s in range(2)
    ]

    def to_chain(array):
        given = lax.dynamic_index_in_dim(array[:, 0], 1 - section, 0, keepdims=False)
        own = lax.dynamic_index_in_dim(array[:, 0], section, 0, keepdims=False)
        return pick(aligned, own, lax.ppermute(given, everywhere, exchange))

    turned = w_in[0].T
    shard_conv = jnp.pad(turned[DI:], ((0, 8), (0, 0)))
    width = turned.shape[1]
    rows_out = w_out.shape[1]
    pieces = [w_out[0, :, k * width : (k + 1) * width] for k in range(D // width)]
    shard_rest = jnp.concatenate([turned[:DI]] + pieces, axis=0)

    def join_conv(blocks):
        whole_rows = jnp.concatenate([block[: CONVCH + 32] for block in blocks], axis=1)
        return whole_rows[:CONVCH], jnp.pad(whole_rows[CONVCH:], ((0, 96), (0, 0)))

    def join_rest(blocks):
        gate = jnp.concatenate([block[:DI] for block in blocks], axis=1)
        back = [
            jnp.concatenate(
                [block[at : at + rows_out] for at in range(DI, block.shape[0], rows_out)], axis=1
            )
            for block in blocks
        ]
        return gate, jnp.concatenate(back, axis=0)

    blocks = move_rows(shard_conv)
    hidden = to_chain(tokens)
    top_grad = to_chain(cotangent)
    blocks, hidden, shard_rest, top_grad = tie(blocks, hidden, shard_rest, top_grad)
    joined = [join_conv(layer) for layer in share(blocks)]
    w_conv, w_step = [[pair[k] for pair in joined] for k in range(2)]
    moved_rest = move_rows(shard_rest)
    w_gate, w_back = [None, None], [None, None]

    table = parameter_table(
        norm_gain, conv_w[0], conv_b, dt_bias, a_log, skip_scale, gate_gain
    )
    other = lax.ppermute(table, "section", SWAP)
    low = section == 0
    tables = [pick(low, table, other), pick(low, other, table)]
    spread = spread_matrix()

    stream_lengths = lax.dynamic_index_in_dim(lengths[:, 0], micro, 0, keepdims=False)
    stream_order = lax.dynamic_index_in_dim(doc_order[:, 0], micro, 0, keepdims=False)
    col_padded, col, lab = labels(stream_lengths, stream_order, spot * rows, rows)
    follow = [(flat(0, i), flat(1, i)) for i in range(size)] + [
        (flat(1, i), flat(0, i + 2)) for i in range(size - 2)
    ]
    precede = [(b, a) for a, b in follow]

    routes = [[], []]
    for k in range(size // 2):
        for s in range(2):
            for m in range(2):
                for way in range(2):
                    routes[way].append((flat(s, 2 * k + m), flat((m + way) % 2, 2 * k + s)))

    def to_holders(first, second):
        even = micro == 0
        return (
            lax.ppermute(pick(even, first, second), everywhere, routes[0]),
            lax.ppermute(pick(even, second, first), everywhere, routes[1]),
        )

    def held(one, two):
        return jnp.stack([pick(low, one, two), pick(low, two, one)])[None, :, None]

    kept = []
    results = []
    for layer in range(2):
        par = tables[layer]
        wide = hidden.astype(f32)
        scale = lax.rsqrt(jnp.mean(wide * wide, axis=1, keepdims=True) + epsilon)
        u = (wide * scale * par[NORM : NORM + 1, :D]).astype(bf16)
        rc = nt(u, w_conv[layer]).astype(bf16)
        e = nt(u, w_step[layer])
        halo = lax.ppermute(rc[rows - 16 :], everywhere, follow)
        q, ds, dt, cum, total, lin, to_keep, to_give = conv_forward(
            rc, halo, e, col, par, spread
        )
        def beside_first(_, *arrays):
            return intra_forward(*arrays, spread), None

        def beside_second(_, u, moved):
            if layer == 0:
                for k, blocks in enumerate(share(moved)):
                    w_gate[k], w_back[k] = join_rest(blocks)
            return nt(u, w_gate[layer]), None

        inc, ((y0, _), (z, _)) = chain_scan(
            to_keep,
            to_give,
            False,
            [
                ((q, dt, cum, col, lab, lin, par), beside_first),
                ((u, moved_rest if layer == 0 else ()), beside_second),
            ],
        )
        y, v, out = gate_forward(
            y0, z, q, total, col, inc, par, w_back[layer], hidden, spread
        )
        kept.append((hidden, scale, u, rc, e, halo, q, ds, dt, cum, total, lin, to_keep, to_give, inc, z, y, v))
        results.append(out)
        hidden = out

    def columns(a, b):
        return lax.dot_general(a, b, (((0,), (0,)), ((), ())), preferred_element_type=f32)

    parts = lax.axis_size("fsdp")

    def half_of(array, half):
        width = array.shape[1] // 2
        return lax.dynamic_slice_in_dim(array, half * width, width, axis=1)

    def by_part(array):
        width = D // parts
        return jnp.stack([array[:, k * width : (k + 1) * width] for k in range(parts)])

    def early_grads(u, dz, v, grad):
        def make(half):
            for_in = by_part(columns(half_of(dz, half), u))
            for_out = columns(v, half_of(grad, half)).reshape(parts, -1, D // 2)
            step = D // parts
            pieces = [for_out[:, :, at : at + step] for at in range(0, D // 2, step)]
            return jnp.concatenate([for_in] + pieces, axis=1)

        return make

    def late_grads(u, dr):
        return lambda half: by_part(columns(half_of(dr, half), u))

    grad = top_grad
    early = [None, None]
    late = [None, None]
    pieces = [None, None]
    acts = [None, None]
    grads = [None, None]
    for layer in (1, 0):
        par = tables[layer]
        hidden, scale, u, rc, e, halo, q, ds, dt, cum, total, lin, to_keep, to_give, inc, z, y, v = kept[layer]
        dy, dz, dgain, back, back_given = gate_backward(
            grad, w_back[layer], y, z, par, q, total, col, to_keep, to_give, spread
        )
        extra = ()
        if layer == 0:
            back, back_given, early[1], late[1], acts = tie(back, back_given, early[1], late[1], acts)
            extra = (early[1], late[1])
        given = early_grads(u, dz, v, grad)(1 - section).astype(bf16)

        def first(_, extra, given, *arrays):
            if layer == 0:
                extra = (halve(extra[0], 1), halve(extra[1], 1))
            got = lax.ppermute(given, "section", SWAP)
            return (intra_backward(*arrays, spread), extra, got), None

        def second(_, u, dz, v, grad):
            return (nn(dz, w_gate[layer]), early_grads(u, dz, v, grad)(section)), None

        outg, ((((dx, dbc, hs), extra, got), _), ((du, kept_half), _)) = chain_scan(
            back,
            back_given,
            True,
            [
                ((extra, given, q, dt, cum, total, col, lab, lin, inc, dy, y, par), first),
                ((u, dz, v, grad), second),
            ],
        )
        summed = (kept_half + got.astype(f32)).astype(bf16)
        early[layer] = row_sum(summed)
        if layer == 0:
            outg, extra = tie(outg, extra)
        else:
            outg, results = tie(outg, results)
            acts = to_holders(*results)
        dr, de, tail, front, dw, dh = conv_backward(
            outg, inc, q, ds, dt, total, col_padded, e, rc, halo, dy, dx, dbc, hs, par, spread
        )
        if layer == 1:
            front, early[1] = tie(front, early[1])
        else:
            front, extra = tie(front, extra)
            upper = halve(jnp.concatenate(extra, axis=0), 2)
        returned = lax.ppermute(front, everywhere, precede)
        dr = lax.dynamic_update_slice(dr, (tail + returned).astype(bf16), (rows - 8, 0))
        given = late_grads(u, dr)(1 - section).astype(bf16)
        given, dr, de = tie(given, dr, de)
        got = lax.ppermute(given, "section", SWAP)
        summed = (late_grads(u, dr)(section) + got.astype(f32)).astype(bf16)
        if layer == 0:
            summed, early[0], upper, pieces[1] = tie(summed, early[0], upper, pieces[1])
            early[0] = halve(early[0], 1)
            upper = halve(upper, 4) if size > 4 else upper
        summed, dr, de = tie(summed, dr, de)
        late[layer] = row_sum(summed)
        du = du + nn(dr, w_conv[layer]) + nn(de, w_step[layer])
        wide = hidden.astype(f32)
        normed = wide * scale
        dn = du * par[NORM : NORM + 1, :D]
        dnorm = jnp.sum(du * normed, axis=0)
        dhidden = scale * (dn - normed * jnp.mean(dn * normed, axis=1, keepdims=True))
        grad_e = columns(de, u)[:H].reshape(H // 2, 2 * D)
        grad = (grad.astype(f32) + dhidden).astype(bf16)
        if layer == 1:
            holding = grad
        else:
            grads = to_holders(grad, holding)
        pieces[layer] = (dw, dnorm, dgain, dh, grad_e)

    def table_of(dw, dnorm, dgain, dh, grad_e):
        return jnp.concatenate(
            [
                dw[: CONV + 1],
                jnp.pad(dnorm, (0, CONVCH - D))[None],
                jnp.pad(dgain, ((0, 0), (0, CONVCH - DI))),
                jnp.pad(dh[0:3], ((0, 0), (0, CONVCH - 128))),
                jnp.pad(grad_e, ((0, 0), (0, CONVCH - 2 * D))),
            ],
            axis=0,
        )

    steps = exchanges()
    small = [table_of(*pieces[layer]) for layer in range(2)]
    mine = pick(low, small[0], small[1]) + lax.ppermute(pick(low, small[1], small[0]), "section", SWAP)
    mine = exchange_sum(mine, steps[0])
    late[0], early[0], mine, upper = tie(late[0], early[0], mine, upper)
    far = distances()
    for distance in far[3:]:
        upper = halve(upper, distance)
    late[0] = halve(late[0], 1)
    mine = exchange_sum(mine, steps[1])
    for distance in far[1:]:
        early[0] = halve(early[0], distance)
    for distance in reversed(far[1:]):
        upper = rejoin(upper, distance)
    for distance in far[1:2]:
        late[0] = halve(late[0], distance)
    late[0], early[0], mine, grads, upper = tie(late[0], early[0], mine, grads, upper)
    early[1], late[1] = rejoin(upper[:HALF], 1), rejoin(upper[HALF:], 1)
    for distance in far[2:]:
        late[0] = halve(late[0], distance)
    for step in steps[2:]:
        mine = exchange_sum(mine, step)
    for distance in reversed(far[1:]):
        early[0] = rejoin(early[0], distance)
    for distance in reversed(far[2:]):
        late[0] = rejoin(late[0], distance)
    late[0], early[0], mine, upper = tie(late[0], early[0], mine, (early[1], late[1]))
    early[1], late[1] = upper
    early[0] = rejoin(early[0], 1)
    for distance in far[1:2]:
        late[0] = rejoin(late[0], distance)
    late[0] = rejoin(late[0], 1)
    early_got = lax.ppermute(pick(low, early[1], early[0]), "section", SWAP)
    late_got = lax.ppermute(pick(low, late[1], late[0]), "section", SWAP)
    early_own, late_own = pick(low, early[0], early[1]), pick(low, late[0], late[1])
    grad_e = mine[SKIP + 1 :, : 2 * D].reshape(H, D)
    grad_e = lax.dynamic_slice_in_dim(grad_e, lax.axis_index("fsdp") * width, width, axis=1)
    shard_in, shard_out = place(early_own, early_got, late_own, late_got, grad_e, rows_out)
    return (
        held(*acts),
        held(*grads),
        mine[NORM : NORM + 1, :D],
        shard_in,
        mine[None, :CONV],
        mine[TAP_BIAS : TAP_BIAS + 1],
        mine[STEP_BIAS : STEP_BIAS + 1, :H],
        mine[BASE_RATE : BASE_RATE + 1, :H],
        mine[SKIP : SKIP + 1, :H],
        mine[GAIN : GAIN + 1, :DI],
        shard_out,
    )


def solution(mesh):
    in_specs = (
        P(None, "fsdp", "seq", None),
        P(None, "fsdp", "seq", None),
        P(None, "fsdp", None),
        P(None, "fsdp", None),
        P("section", None),
        P("section", "fsdp", None),
        P("section", None, None),
        P("section", None),
        P("section", None),
        P("section", None),
        P("section", None),
        P("section", None),
        P("section", "fsdp", None),
    )
    out_specs = (
        P("section", None, "fsdp", "seq", None),
        P("section", None, "fsdp", "seq", None),
        P("section", None),
        P("section", "fsdp", None),
        P("section", None, None),
        P("section", None),
        P("section", None),
        P("section", None),
        P("section", None),
        P("section", None),
        P("section", "fsdp", None),
    )
    return jax.shard_map(local, mesh=mesh, in_specs=in_specs, out_specs=out_specs, check_vma=False)
```
